256 devices in a mesh: dp: 32 (over x, z), tensor: 8 (over y, core).
Axes of the slice: x: 4, y: 4, z: 8, core: 2. Of those that a mesh axis runs over, the one named last changes fastest.
Arguments:
- patches: bfloat16 [32768, 1176], P('dp')
- rank_groups: int32 [32], P('dp'), may hold values from 1 to 256, 4096 in all
- patch_weight: bfloat16 [1176, 1280], P(None, 'tensor')
- merge_weight: bfloat16 [4, 1280, 8192], P(None, 'tensor', 'dp'), may hold values from -0.078125 to 0.078125
- emb_grad: bfloat16 [8192, 8192], P('dp', 'tensor'), may hold values from -6 to 6
Outputs:
- embeds: bfloat16 [8192, 8192], P('dp', 'tensor')
- grad_merge: float32 [4, 1280, 8192], P(None, 'tensor', 'dp')
- grad_patch: float32 [1176, 1280], P(None, 'tensor')
The draws below stay inside these ranges and needn't reach their ends.
Inputs may be any that keep to these rules, and one draw needn't show every extreme that they name: `rank_groups`: the counts of all dp ranks add up to 4096; some rank holds exactly 256.
All inputs are finite; a program needn't handle non-finite values. No bound on the sum of `rank_groups` on one device may be relied on, other than what follows from the above.
Results may differ from the reference program's by a relative error of at most 0.02.
Values may be sent and summed in bfloat16 or wider, within the bound.
A program may use at most 128 MiB of HBM per device.

```python
import math
import jax
import jax.numpy as jnp
import numpy as np
from jax import lax

PD = 1176
E = 1280
D = 8192
GSLOT = 256
GROUPS = 8192
TOTAL_GROUPS = 4096
PATCH_ROWS = 32768
N_DP = 32


def draw_patches(key, part):
    key = jax.random.fold_in(key, 11)
    first_key, second_key = jax.random.split(key)
    values = jax.random.normal(first_key, (PATCH_ROWS, PD), jnp.float32)
    spread = jnp.exp(jax.random.uniform(second_key, (PATCH_ROWS, 1), jnp.float32, 0.0, math.log(10.0)))
    return (0.4 * values * spread).astype(jnp.bfloat16)


def draw_patch_weight(key, part):
    key = jax.random.fold_in(key, 23)
    column = jnp.arange(E, dtype=jnp.float32) / E
    values = jax.random.normal(key, (PD, E), jnp.float32)
    growth = jnp.exp(column * math.log(3.0))
    return (values * growth[None, :] / math.sqrt(PD)).astype(jnp.bfloat16)


def raised(entries, own_key, source, target, parts, factor):
    owner, partner = [(jnp.arange(entries.shape[axis_at]) // (entries.shape[axis_at] // parts)).reshape([-1 if axis == axis_at else 1 for axis in range(entries.ndim)]) for axis_at in (source, target)]
    chosen = jax.random.permutation(own_key, parts)[partner]
    strong = (owner == chosen) | (owner == (partner + parts // 2) % parts)
    return jnp.where(strong, factor * entries, entries)


def level_of(stream_key, dims, shards, least, largest):
    def one(axis_at, shards_of):
        draws = jax.random.uniform(jax.random.fold_in(jax.random.fold_in(stream_key, 6), axis_at), (shards_of,), jnp.float32, least / len(shards), largest / len(shards))
        return jnp.repeat(jnp.exp(draws), dims[axis_at] // shards_of).reshape((-1,) + (1,) * (len(dims) - axis_at - 1))

    gain = one(*shards[0])
    for cut in shards[1:]:
        gain = gain * one(*cut)
    return gain


def length_profile(amount, total, most, skew):
    weights = [(1 << 20) // math.isqrt(standing ** skew) + 1 for standing in range(2, amount + 1)]
    rest, given = total - most - (amount - 1), [1] * (amount - 1)
    while rest > 0:
        candidates = [i for i in range(amount - 1) if given[i] < most]
        mass, budget = sum([weights[i] for i in candidates]), rest
        for i in candidates:
            extra = min(most - given[i], max(1, budget * weights[i] // mass), rest)
            given[i] = given[i] + extra
            rest = rest - extra
    return np.array([most] + given)


def ragged(key, number_of, total, reach, skew):
    if number_of == 2:
        one = jax.random.randint(key, (), max(1, total - reach), min(reach, total - 1) + 1)
        return jnp.stack([one, total - one])
    tallies = jnp.asarray(length_profile(number_of, total, reach, skew), jnp.int32)
    pairs = (number_of - 1) // 2
    giver, receiver = tallies[1:1 + 2 * pairs:2], tallies[2:2 + 2 * pairs:2]
    margin = jnp.minimum(giver - 1, reach - receiver)
    moved = jax.random.randint(jax.random.fold_in(key, 1), (pairs,), 0, 1 << 20) % (margin + 1)
    tallies = tallies.at[1:1 + 2 * pairs:2].set(giver - moved).at[2:2 + 2 * pairs:2].set(receiver + moved)
    return tallies[jax.random.permutation(jax.random.fold_in(key, 2), number_of)]


def bell_draw(key, dims, width, limit, pieces=(), held_as=jnp.bfloat16):
    level = level_of(key, dims, pieces, -0.22, 0.18) if pieces else 1.0
    entries = jax.random.normal(key, dims, jnp.float32) * width * level
    return jnp.minimum(jnp.maximum(entries, -limit), limit).astype(held_as)


def noise_with(own_key, shape, deviation, reach, pieces, heavy, kind=jnp.bfloat16):
    result = deviation * jax.random.normal(own_key, shape, jnp.float32)
    if pieces:
        result = result * level_of(own_key, shape, pieces, -0.22, 0.18)
    return jnp.clip(raised(result, jax.random.fold_in(own_key, 3), *heavy), -reach, reach).astype(kind)


def setup_inputs(seed: int = 0) -> dict:
    key_of = jax.random.split(jax.random.key(seed), 6)
    return {
        "patches": draw_patches(jax.random.fold_in(key_of[5], 71), 0),
        "rank_groups": ragged(key_of[1], N_DP, TOTAL_GROUPS, GSLOT, 2).astype(jnp.int32),
        "patch_weight": draw_patch_weight(jax.random.fold_in(key_of[5], 71), 0),
        "merge_weight": bell_draw(key_of[3], (4, E, D), (4 * E) ** -0.5, 0.078125, ((1, 8), (2, 32))),
        "emb_grad": noise_with(key_of[4], (GROUPS, D), 1.0, 6.0, ((0, 32), (1, 8)), (0, 1, 32, 2.75)),
    }


def reference(patches, rank_groups, patch_weight, merge_weight, emb_grad):
    projected = jnp.dot(patches, patch_weight, preferred_element_type=jnp.float32)
    row_mean = lax.optimization_barrier(jnp.mean(projected, axis=1, keepdims=True))
    square = lax.optimization_barrier(jnp.mean(projected * projected, axis=1, keepdims=True))
    inv_scale = lax.rsqrt(square - row_mean * row_mean + 1e-05)
    normed = (projected - row_mean) * inv_scale
    merged = normed.reshape(GROUPS, 4 * E).astype(jnp.bfloat16)
    position = jnp.arange(GSLOT, dtype=jnp.int32)
    live_mask = (position[None, :] < rank_groups[:, None]).reshape(GROUPS, 1)
    merge_table = merge_weight.reshape(4 * E, D)
    product = jnp.dot(merged, merge_table, preferred_element_type=jnp.float32)
    embeds = jnp.where(live_mask, product, jnp.zeros_like(product)).astype(jnp.bfloat16)
    cotangent = jnp.where(live_mask, emb_grad, jnp.zeros_like(emb_grad))
    merged_blocks = merged.reshape(N_DP, GSLOT, 4 * E)
    cot_blocks = cotangent.reshape(N_DP, GSLOT, D)

    def accumulate(running, operands):
        part_term = lax.dot_general(operands[0], operands[1], (((0,), (0,)), ((), ())), preferred_element_type=jnp.float32)
        rounded = lax.optimization_barrier(part_term.astype(jnp.bfloat16))
        return (running + rounded.astype(jnp.float32), None)
    grad_merge, _ = lax.scan(accumulate, jnp.zeros((4 * E, D), jnp.float32), (merged_blocks, cot_blocks))
    grad_merge = grad_merge.reshape(4, E, D)
    dmerged = lax.dot_general(cotangent, merge_table, (((1,), (1,)), ((), ())), preferred_element_type=jnp.float32)
    dnormed = dmerged.reshape(PATCH_ROWS, E)
    first_mean = lax.optimization_barrier(jnp.mean(dnormed, axis=1, keepdims=True))
    second_mean = lax.optimization_barrier(jnp.mean(dnormed * normed, axis=1, keepdims=True))
    grad_input = ((dnormed - first_mean - normed * second_mean) * inv_scale).astype(jnp.bfloat16)
    grad_patch = lax.dot_general(patches, grad_input, (((0,), (0,)), ((), ())), preferred_element_type=jnp.float32)
    return (embeds, grad_merge, grad_patch)
```

```python
import functools

import jax
import jax.numpy as jnp
from jax import lax
from jax.experimental import pallas as pl
from jax.experimental.pallas import tpu as pltpu
from jax.sharding import PartitionSpec as P

E = 1280
X, Y, Z = 4, 4, 8
T = 2 * Y
F32, BF16 = jnp.float32, jnp.bfloat16
HIGH = lax.Precision.HIGHEST

PD = 1176
FS = E // T
K = 4 * FS
G = 256
NC = 256
HALF = K // 2
QUAD = Z // 2


def dot(a, b, dims=((1,), (0,)), precision=None):
    return lax.dot_general(a, b, (dims, ((), ())), precision=precision, preferred_element_type=F32)


def wrap(value, count):
    return lax.rem(value + count, count)


def group_rows(offset):
    row = lax.broadcasted_iota(jnp.int32, (8, K), 0)
    lane = lax.broadcasted_iota(jnp.int32, (8, K), 1)
    low = (row - offset) * FS
    return jnp.where((lane >= low) & (lane < low + FS), 1.0, 0.0).astype(F32)


def kernel(
    live_ref, patches_ref, pw_ref, w_ref, emb_ref,
    embeds_ref, gm_ref, gp_ref,
    wg, cot_own, cot_y, cot_all, merged_all, merged_t, proj_s, pw_s, normed_s,
    stats, g_send_buf, g_recv_buf, d_send_buf, d_own, d_recv_buf,
    e_sib_send, e_sib_recv, e_send, e_recv, e_sum, e_fin,
    t_s, a_own, a_xr, a_x, a_zr, a_all,
    w_ss, w_rs, tr_ss, tr_rs, cy_ss, cy_rs, cs_ss, cs_rs, st_ss, st_rs, m_ss, m_rs,
    d_ss, d_rs, g_ss, g_rs, es_ss, es_rs, ey_ss, ey_rs, ax_ss, ax_rs, az_ss, az_rs,
    bz_ss, bz_rs, bx_ss, bx_rs,
):
    dp = lax.axis_index("dp")
    t = lax.axis_index("tensor")
    x, z = lax.div(dp, Z), lax.rem(dp, Z)
    y, c = lax.div(t, 2), lax.rem(t, 2)

    def device(x, y, z, c):
        return (x * Z + z, y * 2 + c)

    started = []

    def send(src, dst, ssem, rsem, to):
        copy = pltpu.make_async_remote_copy(
            src_ref=src, dst_ref=dst, send_sem=ssem, recv_sem=rsem,
            device_id=to, device_id_type=pl.DeviceIdType.MESH,
        )
        copy.start()
        started.append(copy)

    def arrived(dst, rsem, to):
        pltpu.make_async_remote_copy(
            src_ref=dst, dst_ref=dst, send_sem=w_ss.at[0, 0, 0], recv_sem=rsem,
            device_id=to, device_id_type=pl.DeviceIdType.MESH,
        ).wait_recv()

    right = device(x, y, wrap(z + 1, Z), c)
    left = device(x, y, wrap(z - 1, Z), c)
    sibling = device(x, y, z, 1 - c)
    partner = device(y, x, z, c)
    x_peers = [device(wrap(x + k, X), y, z, c) for k in range(1, X)]
    y_peers = [device(x, wrap(y + k, Y), z, c) for k in range(1, Y)]
    z_peers = [device(x, y, wrap(z + k, Z), c) for k in range(1, Z)]
    t_peers = [(dp, wrap(t + k, T)) for k in range(1, T)]
    diagonal = x == y

    barrier = pltpu.get_barrier_semaphore()
    greeted = x_peers + z_peers + t_peers
    for peer in greeted:
        pl.semaphore_signal(barrier, inc=1, device_id=peer, device_id_type=pl.DeviceIdType.MESH)

    @pl.when(jnp.logical_not(diagonal))
    def _():
        pl.semaphore_signal(barrier, inc=1, device_id=partner, device_id_type=pl.DeviceIdType.MESH)

    pl.semaphore_wait(barrier, len(greeted) + jnp.where(diagonal, 0, 1))

    wg[z] = w_ref[...]

    def w_part(index, half):
        return wg.at[index, pl.ds(half * HALF, HALF)]

    def w_halves(way, step):
        return (0, 1) if step < 3 else (way,)

    def w_send(step):
        for way, to, block in ((0, right, wrap(z - step, Z)), (1, left, wrap(z + step, Z))):
            for half in w_halves(way, step):
                if step:
                    arrived(w_part(block, half), w_rs.at[way, step - 1, half], to)
                send(w_part(block, half), w_part(block, half), w_ss.at[way, step, half],
                     w_rs.at[way, step, half], to)

    def w_finish():
        for way, block in ((0, wrap(z - 3, Z)), (1, wrap(z + 3, Z))):
            half = 1 - way
            arrived(w_part(block, half), w_rs.at[way, 2, half], right)
        for way in (0, 1):
            arrived(w_part(wrap(z + 4, Z), way), w_rs.at[way, 3, way], right)

    w_send(0)

    live = live_ref[0]

    def live_rows(columns):
        return lax.broadcasted_iota(jnp.int32, (G, columns), 0) < live

    for k in range(QUAD):
        block = emb_ref[:, k * NC:(k + 1) * NC]
        cot_own[k] = jnp.where(live_rows(NC), block, jnp.zeros_like(block))

    def swap_start(src, dst, index):
        @pl.when(diagonal)
        def _():
            pltpu.make_async_copy(src, dst, tr_rs.at[index]).start()

        @pl.when(jnp.logical_not(diagonal))
        def _():
            pltpu.make_async_remote_copy(
                src_ref=src, dst_ref=dst, send_sem=tr_ss.at[index], recv_sem=tr_rs.at[index],
                device_id=partner, device_id_type=pl.DeviceIdType.MESH,
            ).start()

    def swap_wait(src, dst, index):
        @pl.when(diagonal)
        def _():
            pltpu.make_async_copy(src, dst, tr_rs.at[index]).wait()

        @pl.when(jnp.logical_not(diagonal))
        def _():
            pltpu.make_async_remote_copy(
                src_ref=src, dst_ref=dst, send_sem=tr_ss.at[index], recv_sem=tr_rs.at[index],
                device_id=partner, device_id_type=pl.DeviceIdType.MESH,
            ).wait()

    swap_start(cot_own, cot_y, 0)

    pw_s[...] = jnp.zeros_like(pw_s)
    pw_s[:, :FS] = pw_ref[...]

    @pl.loop(0, 4)
    def _(i):
        rows = pl.ds(i * 256, 256)
        product = dot(patches_ref[rows, :], pw_s[...])
        proj_s[0, rows] = product[:, :128]
        proj_s[1, rows] = product[:, 128:]

    parts = []
    for q in range(4):
        rows = pl.ds(q, G, stride=4)
        parts.append(jnp.concatenate([proj_s[0, rows, :], proj_s[1, rows, :]], axis=1)[:, :FS])
    projected = jnp.concatenate(parts, axis=1)

    first, second = group_rows(0), group_rows(4)

    def sums_over_tensor(index, one, two):
        stats[index, t] = (
            dot(first, one, ((1,), (1,)), HIGH) + dot(second, two, ((1,), (1,)), HIGH)
        )
        for k, peer in enumerate(t_peers):
            send(stats.at[index, t], stats.at[index, t], st_ss.at[index, k], st_rs.at[index, k], peer)

    def totals(index):
        for k, peer in enumerate(t_peers):
            owner = wrap(t - 1 - k, T)
            arrived(stats.at[index, owner], st_rs.at[index, k], peer)
        total = stats[index, 0]
        for k in range(1, T):
            total = total + stats[index, k]
        return total / E

    def spread(rows, value):
        return dot(value, rows, ((0,), (0,)), HIGH)

    sums_over_tensor(0, projected, projected * projected)

    def forward_cot():
        for k, peer in enumerate(y_peers):
            send(cot_y, cot_all.at[y, pl.ds(c * QUAD, QUAD)], cy_ss.at[k], cy_rs.at[k], peer)
        mine = cot_all.at[y, pl.ds(c * QUAD, QUAD)]
        send(cot_y, mine, cs_ss.at[0], cs_rs.at[0], sibling)
        mine[...] = cot_y[...]

    swap_wait(cot_own, cot_y, 0)
    forward_cot()

    means = totals(0)
    row = lax.broadcasted_iota(jnp.int32, (8, G), 0)
    row_mean = pltpu.roll(means, 4, 0)
    inv_scale = jnp.where(row >= 4, lax.rsqrt(
        jnp.where(row >= 4, means - row_mean * row_mean, 1.0) + 1e-05), 0.0)
    inv_wide = spread(second, inv_scale)
    normed = (projected - spread(first, means)) * inv_wide
    normed_s[0] = normed
    normed_s[1] = inv_wide
    merged_all[x] = normed.astype(BF16)
    for k, peer in enumerate(x_peers):
        send(merged_all.at[x], merged_all.at[x], m_ss.at[k], m_rs.at[k], peer)

    w_send(1)
    for k, peer in enumerate(y_peers):
        block = cot_all.at[wrap(y - 1 - k, Y), pl.ds(c * QUAD, QUAD)]
        arrived(block, cy_rs.at[k], peer)
        send(block, block, cs_ss.at[k + 1], cs_rs.at[k + 1], sibling)
    w_send(2)
    for k, peer in enumerate(x_peers):
        arrived(merged_all.at[wrap(x - 1 - k, X)], m_rs.at[k], peer)
    for i in range(X):
        merged_t[:, i * G:(i + 1) * G] = jnp.transpose(merged_all[i])
    for k in range(4):
        block = cot_all.at[wrap(y - k, Y), pl.ds((1 - c) * QUAD, QUAD)]
        arrived(block, cs_rs.at[k], sibling)

    def merge_term(block):
        return dot(merged_t[...], cot_all[:, block].reshape(X * G, NC))

    def g_send(step):
        for way, to, block in ((0, right, wrap(z + 4 - step, Z)), (1, left, wrap(z - 4 + step, Z))):
            term = merge_term(block)
            for half in (0, 1) if step else (way,):
                value = term[half * HALF:(half + 1) * HALF]
                if step > 1 or (step == 1 and half == way):
                    arrived(g_recv_buf.at[way, step - 1, half], g_rs.at[way, step - 1, half], to)
                    value = value + g_recv_buf[way, step - 1, half].astype(F32)
                g_send_buf[way, step, half] = value.astype(BF16)
                send(g_send_buf.at[way, step, half], g_recv_buf.at[way, step, half],
                     g_ss.at[way, step, half], g_rs.at[way, step, half], to)

    g_send(0)
    w_send(3)
    w_finish()

    def d_term(owner):
        total = None
        for block in range(Z):
            term = dot(cot_all[owner, block], wg[block], ((1,), (1,)))
            total = term if total is None else total + term
        return total

    @pl.loop(0, X - 1)
    def _(k):
        d_send_buf[k] = d_term(wrap(x + 1 + k, X)).astype(BF16)

    for k, peer in enumerate(x_peers):
        send(d_send_buf.at[k], d_recv_buf.at[k], d_ss.at[k], d_rs.at[k], peer)
    d_own[...] = d_term(x)

    g_send(1)

    @pl.loop(0, QUAD)
    def _(k):
        block = wg[(1 - c) * QUAD + k]
        for i in range(X):
            e_sib_send[k, i] = dot(merged_all[i], block).astype(BF16)

    for k in range(QUAD):
        send(e_sib_send.at[k], e_sib_recv.at[k], es_ss.at[k], es_rs.at[k], sibling)

    for k in range(X - 1):
        arrived(d_recv_buf.at[k], d_rs.at[k], sibling)
    dnormed = d_own[...]
    for k in range(X - 1):
        dnormed = dnormed + d_recv_buf[k].astype(F32)
    normed = normed_s[0]
    sums_over_tensor(1, dnormed, dnormed * normed)
    d_own[...] = dnormed

    for k in range(QUAD):
        arrived(e_sib_recv.at[k], es_rs.at[k], sibling)

    @pl.loop(0, QUAD)
    def _(k):
        block = wg[c * QUAD + k]
        for i in range(X):
            value = dot(merged_all[i], block) + e_sib_recv[k, i].astype(F32)
            e_send[i, k] = value.astype(BF16)

    for k, peer in enumerate(y_peers):
        send(e_send.at[wrap(y + 1 + k, Y)], e_recv.at[k], ey_ss.at[k], ey_rs.at[k], peer)

    means = totals(1)
    d_mean = spread(first, means)
    dn_mean = spread(second, means)
    grad_input = (d_own[...] - d_mean - normed_s[0] * dn_mean) * normed_s[1]
    for q in range(4):
        part = grad_input[:, q * FS:(q + 1) * FS]
        part = jnp.concatenate([part, jnp.zeros((G, 256 - FS), F32)], axis=1)
        rows = pl.ds(q, G, stride=4)
        proj_s[0, rows, :] = part[:, :128]
        proj_s[1, rows, :] = part[:, 128:]
    grad_rows = jnp.concatenate([proj_s[0], proj_s[1]], axis=1)[:, :FS].astype(BF16)
    t_s[:, 1152:] = jnp.zeros((FS, 128), BF16)
    t_s[:, :PD] = dot(grad_rows, patches_ref[...], ((0,), (0,))).astype(BF16)
    for j in range(10):
        a_own[pl.ds(10 * j, 10)] = t_s[:, 128 * j:128 * (j + 1)].reshape(10, 16, 128)
    a_own[pl.ds(100, 28)] = jnp.zeros((28, 16, 128), BF16)
    for k, peer in enumerate(x_peers):
        send(a_own.at[pl.ds(32 * wrap(x + 1 + k, X), 32)], a_xr.at[k], ax_ss.at[k], ax_rs.at[k], peer)

    g_send(2)

    total = a_own[pl.ds(32 * x, 32)].astype(F32)
    for k in range(X - 1):
        arrived(a_xr.at[k], ax_rs.at[k], sibling)
        total = total + a_xr[k].astype(F32)
    a_x[...] = total.astype(BF16)
    for k, peer in enumerate(z_peers):
        send(a_x.at[pl.ds(4 * wrap(z + 1 + k, Z), 4)], a_zr.at[k], az_ss.at[k], az_rs.at[k], peer)

    for k in range(Y - 1):
        arrived(e_recv.at[k], ey_rs.at[k], sibling)
    for k in range(QUAD):
        total = e_send[y, k].astype(F32)
        for j in range(Y - 1):
            total = total + e_recv[j, k].astype(F32)
        e_sum[k] = total.astype(BF16)
    swap_start(e_sum, e_fin, 1)

    total = a_x[pl.ds(4 * z, 4)].astype(F32)
    for k in range(Z - 1):
        arrived(a_zr.at[k], az_rs.at[k], sibling)
        total = total + a_zr[k].astype(F32)
    fin = a_all.at[pl.ds(32 * x + 4 * z, 4)]
    fin[...] = total.astype(BF16)
    for k, peer in enumerate(z_peers):
        send(fin, fin, bz_ss.at[k], bz_rs.at[k], peer)

    g_send(3)

    for k in range(Z - 1):
        arrived(a_all.at[pl.ds(32 * x + 4 * wrap(z - 1 - k, Z), 4)], bz_rs.at[k], sibling)
    fin = a_all.at[pl.ds(32 * x, 32)]
    for k, peer in enumerate(x_peers):
        send(fin, fin, bx_ss.at[k], bx_rs.at[k], peer)

    term = merge_term(z)
    for half in (0, 1):
        value = term[half * HALF:(half + 1) * HALF]
        for way in (0, 1):
            arrived(g_recv_buf.at[way, 3, half], g_rs.at[way, 3, half], sibling)
            value = value + g_recv_buf[way, 3, half].astype(F32)
        gm_ref[pl.ds(half * HALF, HALF)] = value

    swap_wait(e_sum, e_fin, 1)
    for k in range(QUAD):
        block = e_fin[k]
        embeds_ref[:, k * NC:(k + 1) * NC] = jnp.where(live_rows(NC), block, jnp.zeros_like(block))

    for k in range(X - 1):
        arrived(a_all.at[pl.ds(32 * wrap(x - 1 - k, X), 32)], bx_rs.at[k], sibling)
    for j in range(9):
        gp_ref[:, 128 * j:128 * (j + 1)] = a_all[pl.ds(10 * j, 10)].reshape(FS, 128).astype(F32)
    gp_ref[:, 1152:] = a_all[pl.ds(90, 10)].reshape(FS, 128).astype(F32)[:, :PD - 1152]

    for copy in started:
        copy.wait_send()


def body(patches, rank_groups, patch_weight, merge_weight, emb_grad):
    vmem = pl.BlockSpec(memory_space=pltpu.VMEM)
    dma = pltpu.SemaphoreType.DMA
    rows = 4 * G
    scratch = [
        pltpu.VMEM((Z, K, NC), BF16),
        pltpu.VMEM((QUAD, G, NC), BF16),
        pltpu.VMEM((QUAD, G, NC), BF16),
        pltpu.VMEM((X, Z, G, NC), BF16),
        pltpu.VMEM((X, G, K), BF16),
        pltpu.VMEM((K, X * G), BF16),
        pltpu.VMEM((2, rows, 128), F32),
        pltpu.VMEM((PD, 256), BF16),
        pltpu.VMEM((2, G, K), F32),
        pltpu.VMEM((2, T, 8, G), F32),
        pltpu.VMEM((2, 4, 2, HALF, NC), BF16),
        pltpu.VMEM((2, 4, 2, HALF, NC), BF16),
        pltpu.VMEM((X - 1, G, K), BF16),
        pltpu.VMEM((G, K), F32),
        pltpu.VMEM((X - 1, G, K), BF16),
        pltpu.VMEM((QUAD, X, G, NC), BF16),
        pltpu.VMEM((QUAD, X, G, NC), BF16),
        pltpu.VMEM((Y, QUAD, G, NC), BF16),
        pltpu.VMEM((Y - 1, QUAD, G, NC), BF16),
        pltpu.VMEM((QUAD, G, NC), BF16),
        pltpu.VMEM((QUAD, G, NC), BF16),
        pltpu.VMEM((FS, 1280), BF16),
        pltpu.VMEM((128, 16, 128), BF16),
        pltpu.VMEM((X - 1, 32, 16, 128), BF16),
        pltpu.VMEM((32, 16, 128), BF16),
        pltpu.VMEM((Z - 1, 4, 16, 128), BF16),
        pltpu.VMEM((128, 16, 128), BF16),
    ]
    for shape in (
        (2, 4, 2), (2, 4, 2), (2,), (2,), (3,), (3,), (4,), (4,), (2, 7), (2, 7), (3,), (3,),
        (3,), (3,), (2, 4, 2), (2, 4, 2), (4,), (4,), (3,), (3,), (3,), (3,), (7,), (7,),
        (7,), (7,), (3,), (3,),
    ):
        scratch.append(dma(shape))
    embeds, grad_merge, grad_patch = pl.pallas_call(
        kernel,
        out_shape=(
            jax.ShapeDtypeStruct((G, QUAD * NC), BF16),
            jax.ShapeDtypeStruct((K, NC), F32),
            jax.ShapeDtypeStruct((FS, PD), F32),
        ),
        in_specs=[pl.BlockSpec(memory_space=pltpu.SMEM)] + [vmem] * 4,
        out_specs=(vmem, vmem, vmem),
        scratch_shapes=scratch,
        compiler_params=pltpu.CompilerParams(
            collective_id=0, has_side_effects=True, vmem_limit_bytes=56 * 2**20
        ),
        name="tower",
    )(rank_groups, patches, patch_weight, merge_weight.reshape(K, NC), emb_grad)
    return embeds, grad_merge.reshape(4, FS, NC), grad_patch.T


def solution(mesh):
    return jax.shard_map(
        body,
        mesh=mesh,
        in_specs=(
            P("dp", None),
            P("dp"),
            P(None, "tensor"),
            P(None, "tensor", "dp"),
            P("dp", "tensor"),
        ),
        out_specs=(P("dp", "tensor"), P(None, "tensor", "dp"), P(None, "tensor")),
        check_vma=False,
    )
```

```python
import functools

import jax
import jax.numpy as jnp
from jax import lax
from jax.experimental import pallas as pl
from jax.experimental.pallas import tpu as pltpu
from jax.sharding import PartitionSpec as P

E = 1280
X, Y, Z = 4, 4, 8
T = 2 * Y
F32, BF16 = jnp.float32, jnp.bfloat16
HIGH = lax.Precision.HIGHEST

PD = 1176
FS = E // T
K = 4 * FS
G = 256
NC = 256
HALF = K // 2
QUAD = Z // 2


def dot(a, b, dims=((1,), (0,)), precision=None):
    return lax.dot_general(a, b, (dims, ((), ())), precision=precision, preferred_element_type=F32)


def wrap(value, count):
    return lax.rem(value + count, count)


def group_rows(offset):
    row = lax.broadcasted_iota(jnp.int32, (8, K), 0)
    lane = lax.broadcasted_iota(jnp.int32, (8, K), 1)
    low = (row - offset) * FS
    return jnp.where((lane >= low) & (lane < low + FS), 1.0, 0.0).astype(F32)


def kernel(
    live_ref, patches_hbm, pw_hbm, w_hbm, emb_hbm,
    embeds_ref, gm_ref, gp_ref,
    patches_ref, pw_ref, emb_ref,
    wg, cot_own, cot_p1, cot_all, merged_all, merged_t, proj_s, normed_s,
    stats, g_send_buf, g_recv_buf, d_send_buf, d_own, d_recv_buf,
    e_sib_send, e_sib_recv, e_send, e_recv, e_sum, e_p2, e_fin,
    t_s, a_own, a_xr, a_x, a_zr, a_all,
    in_s,
    w_ss, w_rs, p1_ss, p1_rs, p2_ss, p2_rs, p3_ss, p3_rs, cs_ss, cs_rs,
    st_ss, st_rs, m_ss, m_rs,
    d_ss, d_rs, g_ss, g_rs, es_ss, es_rs, ey_ss, ey_rs, e2_ss, e2_rs, e1_ss, e1_rs,
    ax_ss, ax_rs, az_ss, az_rs, bz_ss, bz_rs, bx_ss, bx_rs,
):
    dp = lax.axis_index("dp")
    t = lax.axis_index("tensor")
    x, z = lax.div(dp, Z), lax.rem(dp, Z)
    y, c = lax.div(t, 2), lax.rem(t, 2)

    def device(x, y, z, c):
        return (x * Z + z, y * 2 + c)

    started = []

    def send(src, dst, ssem, rsem, to):
        copy = pltpu.make_async_remote_copy(
            src_ref=src, dst_ref=dst, send_sem=ssem, recv_sem=rsem,
            device_id=to, device_id_type=pl.DeviceIdType.MESH,
        )
        copy.start()
        started.append(copy)

    def arrived(dst, rsem):
        pltpu.make_async_remote_copy(
            src_ref=dst, dst_ref=dst, send_sem=w_ss.at[0, 0, 0], recv_sem=rsem,
            device_id=sibling, device_id_type=pl.DeviceIdType.MESH,
        ).wait_recv()

    right = device(x, y, wrap(z + 1, Z), c)
    left = device(x, y, wrap(z - 1, Z), c)
    sibling = device(x, y, z, 1 - c)
    xs = [wrap(x + k, X) for k in range(X)]
    ys = [wrap(y + k, Y) for k in range(Y)]
    zs = [wrap(z + k, Z) for k in range(Z)]
    x_peers = [device(i, y, z, c) for i in xs]
    y_peers = [device(x, i, z, c) for i in ys]
    z_peers = [device(x, y, i, c) for i in zs]
    t_peers = [(dp, wrap(t + k, T)) for k in range(T)]

    inputs = [
        pltpu.make_async_copy(w_hbm, wg.at[z], in_s.at[0]),
        pltpu.make_async_copy(emb_hbm, emb_ref, in_s.at[1]),
        pltpu.make_async_copy(pw_hbm, pw_ref, in_s.at[2]),
        pltpu.make_async_copy(patches_hbm, patches_ref, in_s.at[3]),
    ]
    for copy in inputs:
        copy.start()

    barrier = pltpu.get_barrier_semaphore()
    greeted = x_peers[1:] + z_peers[1:] + t_peers[1:]
    for peer in greeted:
        pl.semaphore_signal(barrier, inc=1, device_id=peer, device_id_type=pl.DeviceIdType.MESH)

    inputs[0].wait()
    inputs[1].wait()
    live = live_ref[0]
    live_rows = lax.broadcasted_iota(jnp.int32, (G, NC), 0) < live
    for k in range(QUAD):
        block = emb_ref[:, k * NC:(k + 1) * NC]
        cot_own[k] = jnp.where(live_rows, block, jnp.zeros_like(block))

    pl.semaphore_wait(barrier, len(greeted))

    for k in range(1, Y):
        send(cot_own.at[ys[k]], cot_p1.at[y], p1_ss.at[k], p1_rs.at[y], y_peers[k])

    def w_part(index, half):
        return wg.at[index, pl.ds(half * HALF, HALF)]

    def w_send(step):
        for way, to, block in ((0, right, wrap(z - step, Z)), (1, left, wrap(z + step, Z))):
            for half in (0, 1) if step < 3 else (way,):
                part = w_part(block, half)
                if step:
                    arrived(part, w_rs.at[way, step - 1, half])
                send(part, part, w_ss.at[way, step, half], w_rs.at[way, step, half], to)

    def w_finish():
        for way, block in ((0, wrap(z - 3, Z)), (1, wrap(z + 3, Z))):
            arrived(w_part(block, 1 - way), w_rs.at[way, 2, 1 - way])
        for way in (0, 1):
            arrived(w_part(wrap(z + 4, Z), way), w_rs.at[way, 3, way])

    w_send(0)
    cot_p1[y] = cot_own[y]

    inputs[2].wait()
    inputs[3].wait()
    for i in range(4):
        rows = pl.ds(i * 256, 256)
        product = dot(pw_ref[...], patches_ref[:, i * 256:(i + 1) * 256])
        product = jnp.transpose(jnp.concatenate([product, jnp.zeros((256 - FS, 256), F32)], axis=0))
        proj_s[0, rows] = product[:, :128]
        proj_s[1, rows] = product[:, 128:]

    parts = []
    for q in range(4):
        rows = pl.ds(q, G, stride=4)
        parts.append(jnp.concatenate([proj_s[0, rows, :], proj_s[1, rows, :]], axis=1)[:, :FS])
    projected = jnp.concatenate(parts, axis=1)

    first, second = group_rows(0), group_rows(4)

    def sums_over_tensor(index, one, two):
        stats[index, t] = (
            dot(first, one, ((1,), (1,)), HIGH) + dot(second, two, ((1,), (1,)), HIGH)
        )
        mine = stats.at[index, t]
        for k in range(1, T):
            send(mine, mine, st_ss.at[index, k], st_rs.at[index, t], t_peers[k])

    def totals(index):
        for k in range(1, T):
            owner = wrap(t + k, T)
            arrived(stats.at[index, owner], st_rs.at[index, owner])
        total = stats[index, 0]
        for k in range(1, T):
            total = total + stats[index, k]
        return total / E

    def spread(rows, value):
        return dot(value, rows, ((0,), (0,)), HIGH)

    sums_over_tensor(0, projected, projected * projected)

    for k in (1, 2, 3, 0):
        origin = xs[k]
        block = cot_p1.at[origin]

        @pl.when(origin != y)
        def _():
            arrived(block, p1_rs.at[origin])

        slot = cot_all.at[x, c * QUAD + y]
        if k:
            send(block, slot, p2_ss.at[k], p2_rs.at[x], x_peers[k])
        else:
            slot[...] = block[...]

    def cot_out(k):
        block = cot_all.at[xs[k], c * QUAD + y]
        if k:
            arrived(block, p2_rs.at[xs[k]])
        for j in range(1, Y):
            send(block, block, p3_ss.at[k, j], p3_rs.at[xs[k], y], y_peers[j])
        send(block, block, cs_ss.at[k, 0], cs_rs.at[xs[k], y], sibling)

    def cot_on(k):
        for j in range(1, Y):
            block = cot_all.at[xs[k], c * QUAD + ys[j]]
            arrived(block, p3_rs.at[xs[k], ys[j]])
            send(block, block, cs_ss.at[k, j], cs_rs.at[xs[k], ys[j]], sibling)

    def cot_in(k):
        for j in range(Y):
            arrived(cot_all.at[xs[k], (1 - c) * QUAD + ys[j]], cs_rs.at[xs[k], ys[j]])

    cot_out(0)

    means = totals(0)
    row = lax.broadcasted_iota(jnp.int32, (8, G), 0)
    row_mean = pltpu.roll(means, 4, 0)
    inv_scale = jnp.where(row >= 4, lax.rsqrt(
        jnp.where(row >= 4, means - row_mean * row_mean, 1.0) + 1e-05), 0.0)
    inv_wide = spread(second, inv_scale)
    normed = (projected - spread(first, means)) * inv_wide
    normed_s[0] = normed
    normed_s[1] = inv_wide
    merged_all[x] = normed.astype(BF16)
    for k in range(1, X):
        send(merged_all.at[x], merged_all.at[x], m_ss.at[k], m_rs.at[x], x_peers[k])

    w_send(1)
    for k in (1, 2, 3):
        cot_out(k)
    merged_t[:, pl.ds(x * G, G)] = jnp.transpose(merged_all[x])
    cot_on(0)
    w_send(2)
    cot_on(1)
    w_send(3)
    for k in range(1, X):
        arrived(merged_all.at[xs[k]], m_rs.at[xs[k]])
        merged_t[:, pl.ds(xs[k] * G, G)] = jnp.transpose(merged_all[xs[k]])
    cot_on(2)
    w_finish()

    def d_term(owner):
        total = None
        for block in range(Z):
            term = dot(cot_all[owner, block], wg[block], ((1,), (1,)))
            total = term if total is None else total + term
        return total

    def d_send(k):
        d_send_buf[k] = d_term(xs[k]).astype(BF16)
        send(d_send_buf.at[k], d_recv_buf.at[x], d_ss.at[k], d_rs.at[x], x_peers[k])

    cot_in(1)
    d_send(1)
    cot_on(3)
    cot_in(2)
    d_send(2)

    for k in range(QUAD):
        block = wg[(1 - c) * QUAD + ys[(k + 1) % Y]]
        for i in range(X):
            e_sib_send[k, i] = dot(merged_all[i], block).astype(BF16)
        send(e_sib_send.at[k], e_sib_recv.at[k], es_ss.at[k], es_rs.at[k], sibling)

    cot_in(3)
    d_send(3)
    cot_in(0)

    def merge_term(block):
        return dot(merged_t[...], cot_all[:, block].reshape(X * G, NC))

    def g_send(step):
        for way, to, block in ((0, right, wrap(z + 4 - step, Z)), (1, left, wrap(z - 4 + step, Z))):
            term = merge_term(block)
            for half in (0, 1) if step else (way,):
                value = term[half * HALF:(half + 1) * HALF]
                if step > 1 or (step == 1 and half == way):
                    arrived(g_recv_buf.at[way, step - 1, half], g_rs.at[way, step - 1, half])
                    value = value + g_recv_buf[way, step - 1, half].astype(F32)
                g_send_buf[way, step, half] = value.astype(BF16)
                send(g_send_buf.at[way, step, half], g_recv_buf.at[way, step, half],
                     g_ss.at[way, step, half], g_rs.at[way, step, half], to)

    g_send(0)

    d_own[...] = d_term(x)

    for k in range(QUAD):
        target = (k + 1) % Y
        block = wg[c * QUAD + ys[target]]
        arrived(e_sib_recv.at[k], es_rs.at[k])
        for i in range(X):
            value = dot(merged_all[i], block) + e_sib_recv[k, i].astype(F32)
            e_send[k, i] = value.astype(BF16)
        if target:
            send(e_send.at[k], e_recv.at[y], ey_ss.at[k], ey_rs.at[y], y_peers[target])

    g_send(1)

    dnormed = d_own[...]
    for k in range(1, X):
        arrived(d_recv_buf.at[xs[k]], d_rs.at[xs[k]])
        dnormed = dnormed + d_recv_buf[xs[k]].astype(F32)
    normed = normed_s[0]
    sums_over_tensor(1, dnormed, dnormed * normed)
    d_own[...] = dnormed

    g_send(2)

    means = totals(1)
    d_mean = spread(first, means)
    dn_mean = spread(second, means)
    grad_input = (d_own[...] - d_mean - normed_s[0] * dn_mean) * normed_s[1]
    for q in range(4):
        part = grad_input[:, q * FS:(q + 1) * FS]
        part = jnp.concatenate([part, jnp.zeros((G, 256 - FS), F32)], axis=1)
        rows = pl.ds(q, G, stride=4)
        proj_s[0, rows, :] = part[:, :128]
        proj_s[1, rows, :] = part[:, 128:]
    grad_rows = jnp.concatenate([proj_s[0], proj_s[1]], axis=1)
    grad_rows = jnp.transpose(grad_rows)[:FS].astype(BF16)
    t_s[:, 1152:] = jnp.zeros((FS, 128), BF16)
    t_s[:, :PD] = dot(grad_rows, patches_ref[...], ((1,), (1,))).astype(BF16)
    for j in range(10):
        a_own[pl.ds(10 * j, 10)] = t_s[:, 128 * j:128 * (j + 1)].reshape(10, 16, 128)
    a_own[pl.ds(100, 28)] = jnp.zeros((28, 16, 128), BF16)
    for k in range(1, X):
        send(a_own.at[pl.ds(32 * xs[k], 32)], a_xr.at[x], ax_ss.at[k], ax_rs.at[x], x_peers[k])

    for k in range(1, Y):
        arrived(e_recv.at[ys[k]], ey_rs.at[ys[k]])
    for k in (1, 2, 3, 0):
        total = e_send[QUAD - 1, xs[k]].astype(F32)
        for j in range(1, Y):
            total = total + e_recv[ys[j], xs[k]].astype(F32)
        total = total.astype(BF16)
        if k:
            e_sum[k] = total
            send(e_sum.at[k], e_p2.at[x], e2_ss.at[k], e2_rs.at[x], x_peers[k])
        else:
            e_p2[x] = total

    total = a_own[pl.ds(32 * x, 32)].astype(F32)
    for k in range(1, X):
        arrived(a_xr.at[xs[k]], ax_rs.at[xs[k]])
        total = total + a_xr[xs[k]].astype(F32)
    a_x[...] = total.astype(BF16)
    for k in range(1, Z):
        send(a_x.at[pl.ds(4 * zs[k], 4)], a_zr.at[z], az_ss.at[k], az_rs.at[z], z_peers[k])

    for k in (1, 2, 3, 0):
        origin = ys[k]
        block = e_p2.at[origin]

        @pl.when(origin != x)
        def _():
            arrived(block, e2_rs.at[origin])

        if k:
            send(block, e_fin.at[y], e1_ss.at[k], e1_rs.at[y], y_peers[k])
        else:
            e_fin[y] = block[...]

    total = a_x[pl.ds(4 * z, 4)].astype(F32)
    for k in range(1, Z):
        arrived(a_zr.at[zs[k]], az_rs.at[zs[k]])
        total = total + a_zr[zs[k]].astype(F32)
    fin = a_all.at[pl.ds(32 * x + 4 * z, 4)]
    fin[...] = total.astype(BF16)
    for k in range(1, Z):
        send(fin, fin, bz_ss.at[k], bz_rs.at[z], z_peers[k])

    g_send(3)

    for k in range(1, Z):
        arrived(a_all.at[pl.ds(32 * x + 4 * zs[k], 4)], bz_rs.at[zs[k]])
    fin = a_all.at[pl.ds(32 * x, 32)]
    for k in range(1, X):
        send(fin, fin, bx_ss.at[k], bx_rs.at[x], x_peers[k])

    term = merge_term(z)
    for half in (0, 1):
        value = term[half * HALF:(half + 1) * HALF]
        for way in (0, 1):
            arrived(g_recv_buf.at[way, 3, half], g_rs.at[way, 3, half])
            value = value + g_recv_buf[way, 3, half].astype(F32)
        gm_ref[pl.ds(half * HALF, HALF)] = value

    for k in range(1, Y):
        arrived(e_fin.at[ys[k]], e1_rs.at[ys[k]])
    for k in range(QUAD):
        block = e_fin[k]
        embeds_ref[:, k * NC:(k + 1) * NC] = jnp.where(live_rows, block, jnp.zeros_like(block))

    for k in range(1, X):
        arrived(a_all.at[pl.ds(32 * xs[k], 32)], bx_rs.at[xs[k]])
    for j in range(9):
        gp_ref[:, 128 * j:128 * (j + 1)] = a_all[pl.ds(10 * j, 10)].reshape(FS, 128).astype(F32)
    gp_ref[:, 1152:] = a_all[pl.ds(90, 10)].reshape(FS, 128).astype(F32)[:, :PD - 1152]

    for copy in started:
        copy.wait_send()


def body(patches, rank_groups, patch_weight, merge_weight, emb_grad):
    vmem = pl.BlockSpec(memory_space=pltpu.VMEM)
    dma = pltpu.SemaphoreType.DMA
    rows = 4 * G
    scratch = [
        pltpu.VMEM((PD, rows), BF16),
        pltpu.VMEM((FS, PD), BF16),
        pltpu.VMEM((G, QUAD * NC), BF16),
        pltpu.VMEM((Z, K, NC), BF16),
        pltpu.VMEM((QUAD, G, NC), BF16),
        pltpu.VMEM((Y, G, NC), BF16),
        pltpu.VMEM((X, Z, G, NC), BF16),
        pltpu.VMEM((X, G, K), BF16),
        pltpu.VMEM((K, X * G), BF16),
        pltpu.VMEM((2, rows, 128), F32),
        pltpu.VMEM((2, G, K), F32),
        pltpu.VMEM((2, T, 8, G), F32),
        pltpu.VMEM((2, 4, 2, HALF, NC), BF16),
        pltpu.VMEM((2, 4, 2, HALF, NC), BF16),
        pltpu.VMEM((X, G, K), BF16),
        pltpu.VMEM((G, K), F32),
        pltpu.VMEM((X, G, K), BF16),
        pltpu.VMEM((QUAD, X, G, NC), BF16),
        pltpu.VMEM((QUAD, X, G, NC), BF16),
        pltpu.VMEM((QUAD, X, G, NC), BF16),
        pltpu.VMEM((Y, X, G, NC), BF16),
        pltpu.VMEM((X, G, NC), BF16),
        pltpu.VMEM((X, G, NC), BF16),
        pltpu.VMEM((QUAD, G, NC), BF16),
        pltpu.VMEM((FS, 1280), BF16),
        pltpu.VMEM((128, 16, 128), BF16),
        pltpu.VMEM((X, 32, 16, 128), BF16),
        pltpu.VMEM((32, 16, 128), BF16),
        pltpu.VMEM((Z, 4, 16, 128), BF16),
        pltpu.VMEM((128, 16, 128), BF16),
        dma((4,)),
    ]
    for shape in (
        (2, 4, 2), (4,), (4,), (4, 4), (4, 4), (2, 8), (4,),
        (4,), (2, 4, 2), (4,), (4,), (4,), (4,), (4,), (8,), (8,), (4,),
    ):
        scratch += [dma(shape), dma(shape)]
    embeds, grad_merge, grad_patch = pl.pallas_call(
        kernel,
        out_shape=(
            jax.ShapeDtypeStruct((G, QUAD * NC), BF16),
            jax.ShapeDtypeStruct((K, NC), F32),
            jax.ShapeDtypeStruct((FS, PD), F32),
        ),
        in_specs=[pl.BlockSpec(memory_space=pltpu.SMEM)] + [pl.BlockSpec(memory_space=pl.ANY)] * 4,
        out_specs=(vmem, vmem, vmem),
        scratch_shapes=scratch,
        compiler_params=pltpu.CompilerParams(
            collective_id=0, has_side_effects=True, vmem_limit_bytes=56 * 2**20
        ),
        name="tower",
    )(rank_groups, patches.T, patch_weight.T, merge_weight.reshape(K, NC), emb_grad)
    return embeds, grad_merge.reshape(4, FS, NC), grad_patch.T


def solution(mesh):
    return jax.shard_map(
        body,
        mesh=mesh,
        in_specs=(
            P("dp", None),
            P("dp"),
            P(None, "tensor"),
            P(None, "tensor", "dp"),
            P("dp", "tensor"),
        ),
        out_specs=(P("dp", "tensor"), P(None, "tensor", "dp"), P(None, "tensor")),
        check_vma=False,
    )
```

```python
import functools

import jax
import jax.numpy as jnp
from jax import lax
from jax.experimental import pallas as pl
from jax.experimental.pallas import tpu as pltpu
from jax.sharding import PartitionSpec as P

E = 1280
X, Y, Z = 4, 4, 8
T = 2 * Y
F32, BF16 = jnp.float32, jnp.bfloat16
HIGH = lax.Precision.HIGHEST

PD = 1176
FS = E // T
K = 4 * FS
G = 256
NC = 256
HALF = K // 2
QUAD = Z // 2


def dot(a, b, dims=((1,), (0,)), precision=None):
    return lax.dot_general(a, b, (dims, ((), ())), precision=precision, preferred_element_type=F32)


def wrap(value, count):
    return lax.rem(value + count, count)


def group_rows(offset):
    row = lax.broadcasted_iota(jnp.int32, (8, K), 0)
    lane = lax.broadcasted_iota(jnp.int32, (8, K), 1)
    low = (row - offset) * FS
    return jnp.where((lane >= low) & (lane < low + FS), 1.0, 0.0).astype(F32)


def kernel(
    live_ref, patches_hbm, pw_hbm, w_hbm, emb_hbm,
    embeds_hbm, gm_hbm, gp_hbm,
    embeds_ref, gm_ref, gp_ref,
    patches_ref, pw_ref, emb_ref,
    wg, cot_own, cot_p1, cot_all, merged_all, merged_t, proj_s, normed_s,
    stats, sx_send, sx_recv, g_send_buf, g_recv_buf, d_send_buf, d_own, d_recv_buf,
    e_sib_send, e_sib_recv, e_send, e_recv, e_sum, e_p2, e_fin,
    t_s, a_own, a_xr, a_x, a_zr, a_all,
    in_s, out_s,
    w_ss, w_rs, p1_ss, p1_rs, p2_ss, p2_rs, p3_ss, p3_rs, ph_ss, ph_rs, cs_ss, cs_rs,
    st_ss, st_rs, sx_ss, sx_rs, m_ss, m_rs,
    d_ss, d_rs, g_ss, g_rs, es_ss, es_rs, ey_ss, ey_rs, e2_ss, e2_rs, e1_ss, e1_rs,
    ax_ss, ax_rs, az_ss, az_rs, bz_ss, bz_rs, bx_ss, bx_rs,
):
    dp = lax.axis_index("dp")
    t = lax.axis_index("tensor")
    x, z = lax.div(dp, Z), lax.rem(dp, Z)
    y, c = lax.div(t, 2), lax.rem(t, 2)

    def device(x, y, z, c):
        return (x * Z + z, y * 2 + c)

    started = []

    def send(src, dst, ssem, rsem, to):
        copy = pltpu.make_async_remote_copy(
            src_ref=src, dst_ref=dst, send_sem=ssem, recv_sem=rsem,
            device_id=to, device_id_type=pl.DeviceIdType.MESH,
        )
        copy.start()
        started.append(copy)

    def arrived(dst, rsem):
        pltpu.make_async_remote_copy(
            src_ref=dst, dst_ref=dst, send_sem=w_ss.at[0, 0, 0], recv_sem=rsem,
            device_id=sibling, device_id_type=pl.DeviceIdType.MESH,
        ).wait_recv()

    right = device(x, y, wrap(z + 1, Z), c)
    left = device(x, y, wrap(z - 1, Z), c)
    sibling = device(x, y, z, 1 - c)
    xs = [wrap(x + k, X) for k in range(X)]
    ys = [wrap(y + k, Y) for k in range(Y)]
    zs = [wrap(z + k, Z) for k in range(Z)]
    x_peers = [device(i, y, z, c) for i in xs]
    y_peers = [device(x, i, z, c) for i in ys]
    z_peers = [device(x, y, i, c) for i in zs]
    t_peers = [(dp, wrap(t + k, T)) for k in range(T)]

    inputs = [
        pltpu.make_async_copy(w_hbm, wg.at[z], in_s.at[0]),
        pltpu.make_async_copy(emb_hbm, emb_ref, in_s.at[1]),
        pltpu.make_async_copy(pw_hbm, pw_ref, in_s.at[2]),
        pltpu.make_async_copy(patches_hbm, patches_ref, in_s.at[3]),
    ]
    for copy in inputs:
        copy.start()

    barrier = pltpu.get_barrier_semaphore()
    greeted = x_peers[1:] + z_peers[1:] + t_peers[1:]
    for peer in greeted:
        pl.semaphore_signal(barrier, inc=1, device_id=peer, device_id_type=pl.DeviceIdType.MESH)

    inputs[0].wait()
    inputs[1].wait()
    live = live_ref[0]
    live_rows = lax.broadcasted_iota(jnp.int32, (G, NC), 0) < live
    for k in range(QUAD):
        block = emb_ref[:, k * NC:(k + 1) * NC]
        cot_own[k] = jnp.where(live_rows, block, jnp.zeros_like(block))

    pl.semaphore_wait(barrier, len(greeted))

    for k in range(1, Y):
        send(cot_own.at[ys[k]], cot_p1.at[y], p1_ss.at[k], p1_rs.at[y], y_peers[k])

    def w_part(index, half):
        return wg.at[index, pl.ds(half * HALF, HALF)]

    def w_fwd(step, piece):
        for way, to, block in ((0, right, wrap(z - step, Z)), (1, left, wrap(z + step, Z))):
            half = piece if way == 0 else 1 - piece
            part = w_part(block, half)
            if step:
                arrived(part, w_rs.at[way, step - 1, half])
            send(part, part, w_ss.at[way, step, half], w_rs.at[way, step, half], to)

    def w_finish():
        for way, block in ((0, wrap(z - 3, Z)), (1, wrap(z + 3, Z))):
            arrived(w_part(block, 1 - way), w_rs.at[way, 2, 1 - way])
        for way in (0, 1):
            arrived(w_part(wrap(z + 4, Z), way), w_rs.at[way, 3, way])

    w_fwd(0, 0)
    w_fwd(0, 1)
    cot_p1[y] = cot_own[y]

    inputs[2].wait()
    inputs[3].wait()
    for i in range(4):
        rows = pl.ds(i * 256, 256)
        product = dot(pw_ref[...], patches_ref[:, i * 256:(i + 1) * 256])
        product = jnp.transpose(jnp.concatenate([product, jnp.zeros((256 - FS, 256), F32)], axis=0))
        proj_s[0, rows] = product[:, :128]
        proj_s[1, rows] = product[:, 128:]

    parts = []
    for q in range(4):
        rows = pl.ds(q, G, stride=4)
        parts.append(jnp.concatenate([proj_s[0, rows, :], proj_s[1, rows, :]], axis=1)[:, :FS])
    projected = jnp.concatenate(parts, axis=1)

    first, second = group_rows(0), group_rows(4)

    def send_stats(index):
        mine = stats.at[index, t]
        for k in range(1, T):
            send(mine, mine, st_ss.at[index, k], st_rs.at[index, t], t_peers[k])

    def totals(index):
        for k in range(1, T):
            owner = wrap(t + k, T)
            arrived(stats.at[index, owner], st_rs.at[index, owner])
        total = stats[index, 0]
        for k in range(1, T):
            total = total + stats[index, k]
        return total / E

    def spread(rows, value):
        return dot(value, rows, ((0,), (0,)), HIGH)

    stats[0, t] = (
        dot(first, projected, ((1,), (1,)), HIGH)
        + dot(second, projected * projected, ((1,), (1,)), HIGH)
    )
    send_stats(0)
    w_fwd(1, 0)

    for k in (1, 3, 2, 0):
        origin = xs[k]
        block = cot_p1.at[origin]

        @pl.when(origin != y)
        def _():
            arrived(block, p1_rs.at[origin])

        slot = cot_all.at[x, c * QUAD + y]
        if k:
            send(block, slot, p2_ss.at[k], p2_rs.at[x], x_peers[k])
        else:
            slot[...] = block[...]

    def cot_block(k, j):
        return cot_all.at[xs[k], c * QUAD + ys[j]]

    def to_sibling(k, j):
        block = cot_block(k, j)
        send(block, block, cs_ss.at[k, j], cs_rs.at[xs[k], ys[j]], sibling)

    def cot_out(k):
        block = cot_block(k, 0)
        if k:
            arrived(block, p2_rs.at[xs[k]])
        for j in (1, 3):
            send(block, block, p3_ss.at[k, j], p3_rs.at[xs[k], y], y_peers[j])
        to_sibling(k, 0)

    def cot_on(k):
        for half, j in ((0, 1), (1, 3)):
            block = cot_block(k, j)
            arrived(block, p3_rs.at[xs[k], ys[j]])
            part = block.at[pl.ds(half * 128, 128)]
            send(part, part, ph_ss.at[k, half], ph_rs.at[xs[k], half], y_peers[4 - j])
        to_sibling(k, 1)
        to_sibling(k, 3)

    def cot_far(k):
        for half in (0, 1):
            arrived(cot_block(k, 2).at[pl.ds(half * 128, 128)], ph_rs.at[xs[k], half])
        to_sibling(k, 2)

    def cot_in(k):
        for j in range(Y):
            arrived(cot_all.at[xs[k], (1 - c) * QUAD + ys[j]], cs_rs.at[xs[k], ys[j]])

    cot_out(0)
    w_fwd(1, 1)

    means = totals(0)
    row = lax.broadcasted_iota(jnp.int32, (8, G), 0)
    row_mean = pltpu.roll(means, 4, 0)
    inv_scale = jnp.where(row >= 4, lax.rsqrt(
        jnp.where(row >= 4, means - row_mean * row_mean, 1.0) + 1e-05), 0.0)
    inv_wide = spread(second, inv_scale)
    normed = (projected - spread(first, means)) * inv_wide
    normed_s[0] = normed
    normed_s[1] = inv_wide
    merged_all[x] = normed.astype(BF16)
    for k in range(1, X):
        send(merged_all.at[x], merged_all.at[x], m_ss.at[k], m_rs.at[x], x_peers[k])

    w_fwd(2, 0)
    cot_out(1)
    cot_out(3)
    cot_out(2)
    cot_on(0)
    w_fwd(2, 1)
    merged_t[:, pl.ds(x * G, G)] = jnp.transpose(merged_all[x])
    cot_far(0)
    cot_on(1)
    w_fwd(3, 0)
    cot_on(3)
    cot_far(1)
    cot_on(2)
    cot_far(3)
    for k in range(1, X):
        arrived(merged_all.at[xs[k]], m_rs.at[xs[k]])
        merged_t[:, pl.ds(xs[k] * G, G)] = jnp.transpose(merged_all[xs[k]])
    cot_far(2)
    for k in (0, 1, 3, 2):
        cot_in(k)

    def merge_term(block, rows=slice(None)):
        return dot(merged_t[rows], cot_all[:, block].reshape(X * G, NC))

    def g_block(way, step):
        return wrap(z + 4 - step, Z) if way == 0 else wrap(z - 4 + step, Z)

    def g_out(way, step, half, value):
        g_send_buf[way, step, half] = value.astype(BF16)
        send(g_send_buf.at[way, step, half], g_recv_buf.at[way, step, half],
             g_ss.at[way, step, half], g_rs.at[way, step, half], right if way == 0 else left)

    def g_in(way, step, half):
        arrived(g_recv_buf.at[way, step, half], g_rs.at[way, step, half])
        return g_recv_buf[way, step, half].astype(F32)

    def half_rows(half):
        return slice(half * HALF, (half + 1) * HALF)

    for way in (0, 1):
        g_out(way, 0, way, merge_term(g_block(way, 0), half_rows(way)))
    for way in (0, 1):
        g_out(way, 1, 1 - way, merge_term(g_block(way, 1), half_rows(1 - way)))

    def g_step(step):
        terms = [merge_term(g_block(way, step)) for way in (0, 1)]
        for piece in (0, 1):
            for way in (0, 1):
                half = 1 - way if piece == 0 else way
                g_out(way, step, half, terms[way][half_rows(half)] + g_in(way, step - 1, half))

    w_finish()

    def d_term(owner):
        total = None
        for block in range(Z):
            term = dot(cot_all[owner, block], wg[block], ((1,), (1,)))
            total = term if total is None else total + term
        return total

    def d_sums(term, owner):
        rounded = term.astype(BF16)
        product = (term * merged_all[owner].astype(F32)).astype(BF16)
        return (dot(first.astype(BF16), rounded, ((1,), (1,)))
                + dot(second.astype(BF16), product, ((1,), (1,))))

    for k in (1, 3, 2):
        term = d_term(xs[k])
        d_send_buf[k] = term.astype(BF16)
        sx_send[k] = d_sums(term, xs[k])
        send(sx_send.at[k], sx_recv.at[x], sx_ss.at[k], sx_rs.at[x], x_peers[k])
    for k in (1, 3, 2):
        send(d_send_buf.at[k], d_recv_buf.at[x], d_ss.at[k], d_rs.at[x], x_peers[k])

    for n in range(X):
        rows = merged_all[xs[(n + 1) % X]]
        for m in range(QUAD):
            block = wg[(1 - c) * QUAD + ys[(m + 1) % Y]]
            e_sib_send[n, m] = dot(rows, block).astype(BF16)
        send(e_sib_send.at[n], e_sib_recv.at[n], es_ss.at[n], es_rs.at[n], sibling)

    def e_out(n):
        rows = merged_all[xs[(n + 1) % X]]
        arrived(e_sib_recv.at[n], es_rs.at[n])
        for m in range(QUAD):
            value = dot(rows, wg[c * QUAD + ys[(m + 1) % Y]]) + e_sib_recv[n, m].astype(F32)
            e_send[n, m] = value.astype(BF16)
            if m < QUAD - 1:
                send(e_send.at[n, m], e_recv.at[y, n], ey_ss.at[n, m], ey_rs.at[y, n], y_peers[m + 1])

    def e_sum_up(n):
        total = e_send[n, QUAD - 1].astype(F32)
        for j in range(1, Y):
            arrived(e_recv.at[ys[j], n], ey_rs.at[ys[j], n])
            total = total + e_recv[ys[j], n].astype(F32)
        total = total.astype(BF16)
        if n < X - 1:
            e_sum[n] = total
            send(e_sum.at[n], e_p2.at[x], e2_ss.at[n], e2_rs.at[x], x_peers[n + 1])
        else:
            e_p2[x] = total

    def e_home(k):
        origin = xs[k]
        block = e_p2.at[origin]
        if k:
            arrived(block, e2_rs.at[origin])

        @pl.when(origin == y)
        def _():
            e_fin[y] = block[...]

        @pl.when(origin != y)
        def _():
            pltpu.make_async_remote_copy(
                src_ref=block, dst_ref=e_fin.at[y], send_sem=e1_ss.at[k], recv_sem=e1_rs.at[y],
                device_id=device(x, origin, z, c), device_id_type=pl.DeviceIdType.MESH,
            ).start()

    e_out(0)
    term = d_term(x)
    d_own[...] = term
    total = d_sums(term, x)
    for k in range(1, X):
        arrived(sx_recv.at[xs[k]], sx_rs.at[xs[k]])
        total = total + sx_recv[xs[k]]
    stats[1, t] = total
    send_stats(1)
    for way in (0, 1):
        value = merge_term(g_block(way, 1), half_rows(way))
        g_out(way, 1, way, value + g_in(way, 0, way))
    e_out(1)
    e_out(2)
    e_out(3)
    e_sum_up(0)
    g_step(2)

    means = totals(1)
    d_mean = spread(first, means)
    dn_mean = spread(second, means)
    dnormed = d_own[...]
    for k in (3, 1, 2):
        arrived(d_recv_buf.at[xs[k]], d_rs.at[xs[k]])
        dnormed = dnormed + d_recv_buf[xs[k]].astype(F32)
    grad_input = (dnormed - d_mean - normed_s[0] * dn_mean) * normed_s[1]
    for q in range(4):
        part = grad_input[:, q * FS:(q + 1) * FS]
        part = jnp.concatenate([part, jnp.zeros((G, 256 - FS), F32)], axis=1)
        rows = pl.ds(q, G, stride=4)
        proj_s[0, rows, :] = part[:, :128]
        proj_s[1, rows, :] = part[:, 128:]
    grad_rows = jnp.concatenate([proj_s[0], proj_s[1]], axis=1)
    grad_rows = jnp.transpose(grad_rows)[:FS].astype(BF16)

    for chunk in (0, 1):
        low, high = 640 * chunk, min(640 * (chunk + 1), PD)
        if chunk:
            t_s[chunk, :, 512:] = jnp.zeros((FS, 128), BF16)
        t_s[chunk, :, :high - low] = dot(
            grad_rows, patches_ref[low:high], ((1,), (1,))).astype(BF16)
        for p in range(50):
            i, j = p % 10, p // 10
            a_own[chunk, p // 13, p % 13] = t_s[chunk, 16 * i:16 * (i + 1), 128 * j:128 * (j + 1)]
        for p in range(50, 52):
            a_own[chunk, p // 13, p % 13] = jnp.zeros((16, 128), BF16)
        for k in (1, 3, 2):
            send(a_own.at[chunk, xs[k]], a_xr.at[chunk, x], ax_ss.at[chunk, k],
                 ax_rs.at[chunk, x], x_peers[k])

    def over_z(chunk):
        total = a_own[chunk, x].astype(F32)
        for k in (3, 1, 2):
            arrived(a_xr.at[chunk, xs[k]], ax_rs.at[chunk, xs[k]])
            total = total + a_xr[chunk, xs[k]].astype(F32)
        a_x[chunk, pl.ds(0, 13)] = total.astype(BF16)
        a_x[chunk, pl.ds(13, 3)] = jnp.zeros((3, 16, 128), BF16)
        for k in (1, 7, 2, 6, 3, 5, 4):
            send(a_x.at[chunk, pl.ds(2 * zs[k], 2)], a_zr.at[chunk, z], az_ss.at[chunk, k],
                 az_rs.at[chunk, z], z_peers[k])

    def back_over_z(chunk):
        total = a_x[chunk, pl.ds(2 * z, 2)].astype(F32)
        for k in range(1, Z):
            arrived(a_zr.at[chunk, zs[k]], az_rs.at[chunk, zs[k]])
            total = total + a_zr[chunk, zs[k]].astype(F32)
        mine = a_all.at[chunk, x, pl.ds(2 * z, 2)]
        mine[...] = total.astype(BF16)
        for k in (1, 7, 2, 6, 3, 5, 4):
            send(mine, mine, bz_ss.at[chunk, k], bz_rs.at[chunk, z], z_peers[k])

    def back_over_x(chunk):
        for k in range(1, Z):
            arrived(a_all.at[chunk, x, pl.ds(2 * zs[k], 2)], bz_rs.at[chunk, zs[k]])
        mine = a_all.at[chunk, x, pl.ds(0, 13)]
        for k in (1, 3, 2):
            send(mine, mine, bx_ss.at[chunk, k], bx_rs.at[chunk, x], x_peers[k])

    e_sum_up(1)
    g_step(3)
    over_z(0)
    over_z(1)
    e_sum_up(2)
    back_over_z(0)
    back_over_z(1)
    e_sum_up(3)
    back_over_x(0)
    back_over_x(1)
    e_home(3)
    e_home(2)
    e_home(1)
    e_home(0)

    term = merge_term(z)
    for half in (0, 1):
        gm_ref[pl.ds(half * HALF, HALF)] = (
            term[half_rows(half)] + g_in(0, 3, half) + g_in(1, 3, half))
    outputs = [pltpu.make_async_copy(gm_ref, gm_hbm, out_s.at[0])]
    outputs[0].start()

    for k in range(1, Y):
        arrived(e_fin.at[ys[k]], e1_rs.at[ys[k]])
    for k in range(QUAD):
        block = e_fin[k]
        embeds_ref[:, k * NC:(k + 1) * NC] = jnp.where(live_rows, block, jnp.zeros_like(block))
    outputs.append(pltpu.make_async_copy(embeds_ref, embeds_hbm, out_s.at[1]))
    outputs[1].start()

    for chunk in (0, 1):
        for k in range(1, X):
            arrived(a_all.at[chunk, xs[k], pl.ds(0, 13)], bx_rs.at[chunk, xs[k]])
        for p in range(50):
            i, j = p % 10, 5 * chunk + p // 10
            rows = slice(16 * i, 16 * (i + 1))
            tile = a_all[chunk, p // 13, p % 13].astype(F32)
            if j < 9:
                gp_ref[rows, 128 * j:128 * (j + 1)] = tile
            else:
                gp_ref[rows, 1152:] = tile[:, :PD - 1152]
    outputs.append(pltpu.make_async_copy(gp_ref, gp_hbm, out_s.at[2]))
    outputs[2].start()

    for k in range(X):
        @pl.when(xs[k] != y)
        def _():
            pltpu.make_async_remote_copy(
                src_ref=e_p2.at[xs[k]], dst_ref=e_fin.at[y], send_sem=e1_ss.at[k],
                recv_sem=e1_rs.at[y], device_id=device(x, xs[k], z, c),
                device_id_type=pl.DeviceIdType.MESH,
            ).wait_send()
    for copy in outputs:
        copy.wait()
    for copy in started:
        copy.wait_send()


def finish(embeds_in, gm_in, gp_in, embeds_out, gm_out, gp_out, sems):
    copies = []
    for i, (src, dst, rows) in enumerate(
        ((embeds_in, embeds_out, G), (gm_in, gm_out, K), (gp_in, gp_out, FS))
    ):
        for half in (0, 1):
            part = pl.ds(half * rows // 2, rows // 2)
            copies.append(pltpu.make_async_copy(src.at[part], dst.at[part], sems.at[i, half]))
    for copy in copies:
        copy.start()
    for copy in copies:
        copy.wait()


def body(patches, rank_groups, patch_weight, merge_weight, emb_grad):
    dma = pltpu.SemaphoreType.DMA
    rows = 4 * G
    scratch = [
        pltpu.VMEM((G, QUAD * NC), BF16),
        pltpu.VMEM((K, NC), F32),
        pltpu.VMEM((FS, PD), F32),
        pltpu.VMEM((PD, rows), BF16),
        pltpu.VMEM((FS, PD), BF16),
        pltpu.VMEM((G, QUAD * NC), BF16),
        pltpu.VMEM((Z, K, NC), BF16),
        pltpu.VMEM((QUAD, G, NC), BF16),
        pltpu.VMEM((Y, G, NC), BF16),
        pltpu.VMEM((X, Z, G, NC), BF16),
        pltpu.VMEM((X, G, K), BF16),
        pltpu.VMEM((K, X * G), BF16),
        pltpu.VMEM((2, rows, 128), F32),
        pltpu.VMEM((2, G, K), F32),
        pltpu.VMEM((2, T, 8, G), F32),
        pltpu.VMEM((X, 8, G), F32),
        pltpu.VMEM((X, 8, G), F32),
        pltpu.VMEM((2, 4, 2, HALF, NC), BF16),
        pltpu.VMEM((2, 4, 2, HALF, NC), BF16),
        pltpu.VMEM((X, G, K), BF16),
        pltpu.VMEM((G, K), F32),
        pltpu.VMEM((X, G, K), BF16),
        pltpu.VMEM((X, QUAD, G, NC), BF16),
        pltpu.VMEM((X, QUAD, G, NC), BF16),
        pltpu.VMEM((X, QUAD, G, NC), BF16),
        pltpu.VMEM((Y, X, G, NC), BF16),
        pltpu.VMEM((X, G, NC), BF16),
        pltpu.VMEM((X, G, NC), BF16),
        pltpu.VMEM((QUAD, G, NC), BF16),
        pltpu.VMEM((2, FS, 640), BF16),
        pltpu.VMEM((2, X, 13, 16, 128), BF16),
        pltpu.VMEM((2, X, 13, 16, 128), BF16),
        pltpu.VMEM((2, 16, 16, 128), BF16),
        pltpu.VMEM((2, Z, 2, 16, 128), BF16),
        pltpu.VMEM((2, X, 16, 16, 128), BF16),
        dma((4,)),
        dma((3,)),
    ]
    for shape in (
        (2, 4, 2), (4,), (4,), (4, 4), (4, 2), (4, 4), (2, 8), (4,), (4,),
        (4,), (2, 4, 2), (4,), (4, 4), (4,), (4,), (2, 4), (2, 8), (2, 8), (2, 4),
    ):
        scratch += [dma(shape), dma(shape)]
    results = (
        jax.ShapeDtypeStruct((G, QUAD * NC), BF16),
        jax.ShapeDtypeStruct((K, NC), F32),
        jax.ShapeDtypeStruct((FS, PD), F32),
    )
    hbm = pl.BlockSpec(memory_space=pl.ANY)
    partial = pl.pallas_call(
        kernel,
        out_shape=results,
        in_specs=[pl.BlockSpec(memory_space=pltpu.SMEM)] + [hbm] * 4,
        out_specs=(hbm, hbm, hbm),
        scratch_shapes=scratch,
        compiler_params=pltpu.CompilerParams(
            collective_id=0, has_side_effects=True, vmem_limit_bytes=56 * 2**20
        ),
        name="tower",
    )(rank_groups, patches.T, patch_weight.T, merge_weight.reshape(K, NC), emb_grad)
    embeds, grad_merge, grad_patch = pl.pallas_call(
        finish,
        out_shape=results,
        in_specs=[hbm, hbm, hbm],
        out_specs=(hbm, hbm, hbm),
        scratch_shapes=[dma((3, 2))],
        name="finish",
    )(*partial)
    return embeds, grad_merge.reshape(4, FS, NC), grad_patch.T


def solution(mesh):
    return jax.shard_map(
        body,
        mesh=mesh,
        in_specs=(
            P("dp", None),
            P("dp"),
            P(None, "tensor"),
            P(None, "tensor", "dp"),
            P("dp", "tensor"),
        ),
        out_specs=(P("dp", "tensor"), P(None, "tensor", "dp"), P(None, "tensor")),
        check_vma=False,
    )
```

```python
import functools

import jax
import jax.numpy as jnp
from jax import lax
from jax.experimental import pallas as pl
from jax.experimental.pallas import tpu as pltpu
from jax.sharding import PartitionSpec as P

E = 1280
X, Y, Z = 4, 4, 8
T = 2 * Y
F32, BF16 = jnp.float32, jnp.bfloat16
HIGH = lax.Precision.HIGHEST

PD = 1176
FS = E // T
K = 4 * FS
G = 256
NC = 256
HALF = K // 2
QUAD = Z // 2


def dot(a, b, dims=((1,), (0,)), precision=None):
    return lax.dot_general(a, b, (dims, ((), ())), precision=precision, preferred_element_type=F32)


def wrap(value, count):
    return lax.rem(value + count, count)


def group_rows(offset):
    row = lax.broadcasted_iota(jnp.int32, (8, K), 0)
    lane = lax.broadcasted_iota(jnp.int32, (8, K), 1)
    low = (row - offset) * FS
    return jnp.where((lane >= low) & (lane < low + FS), 1.0, 0.0).astype(F32)


def kernel(
    live_ref, patches_hbm, pw_hbm, w_hbm, emb_hbm,
    embeds_hbm, gm_hbm, gp_hbm,
    embeds_ref, gm_ref, gp_ref,
    patches_ref, pw_ref, emb_ref,
    wg, cot_own, cot_p1, cot_all, merged_all, merged_t, proj_s, normed_s,
    stats, sx_send, sx_recv, g_send_buf, g_recv_buf, d_send_buf, d_own, d_recv_buf,
    e_sib_send, e_sib_recv, e_send, e_recv, e_sum, e_p2, e_fin,
    t_s, a_own, a_xr, a_x, a_zr, a_all,
    in_s, out_s,
    w_ss, w_rs, p1_ss, p1_rs, p2_ss, p2_rs, p3_ss, p3_rs, ph_ss, ph_rs, cs_ss, cs_rs,
    st_ss, st_rs, sx_ss, sx_rs, m_ss, m_rs,
    d_ss, d_rs, g_ss, g_rs, es_ss, es_rs, ey_ss, ey_rs, e2_ss, e2_rs, e1_ss, e1_rs,
    ax_ss, ax_rs, az_ss, az_rs, bz_ss, bz_rs, bx_ss, bx_rs,
):
    dp = lax.axis_index("dp")
    t = lax.axis_index("tensor")
    x, z = lax.div(dp, Z), lax.rem(dp, Z)
    y, c = lax.div(t, 2), lax.rem(t, 2)

    def device(x, y, z, c):
        return (x * Z + z, y * 2 + c)

    started = []

    def send(src, dst, ssem, rsem, to):
        copy = pltpu.make_async_remote_copy(
            src_ref=src, dst_ref=dst, send_sem=ssem, recv_sem=rsem,
            device_id=to, device_id_type=pl.DeviceIdType.MESH,
        )
        copy.start()
        started.append(copy)

    def arrived(dst, rsem):
        pltpu.make_async_remote_copy(
            src_ref=dst, dst_ref=dst, send_sem=w_ss.at[0, 0, 0], recv_sem=rsem,
            device_id=sibling, device_id_type=pl.DeviceIdType.MESH,
        ).wait_recv()

    right = device(x, y, wrap(z + 1, Z), c)
    left = device(x, y, wrap(z - 1, Z), c)
    sibling = device(x, y, z, 1 - c)
    xs = [wrap(x + k, X) for k in range(X)]
    ys = [wrap(y + k, Y) for k in range(Y)]
    zs = [wrap(z + k, Z) for k in range(Z)]
    x_peers = [device(i, y, z, c) for i in xs]
    y_peers = [device(x, i, z, c) for i in ys]
    z_peers = [device(x, y, i, c) for i in zs]
    t_peers = [(dp, wrap(t + k, T)) for k in range(T)]

    inputs = [
        pltpu.make_async_copy(w_hbm, wg.at[z], in_s.at[0]),
        pltpu.make_async_copy(emb_hbm, emb_ref, in_s.at[1]),
        pltpu.make_async_copy(pw_hbm, pw_ref, in_s.at[2]),
        pltpu.make_async_copy(patches_hbm, patches_ref, in_s.at[3]),
    ]
    for copy in inputs:
        copy.start()

    barrier = pltpu.get_barrier_semaphore()
    greeted = x_peers[1:] + z_peers[1:] + t_peers[1:]
    for peer in greeted:
        pl.semaphore_signal(barrier, inc=1, device_id=peer, device_id_type=pl.DeviceIdType.MESH)

    inputs[0].wait()
    inputs[1].wait()
    live = live_ref[0]
    live_rows = lax.broadcasted_iota(jnp.int32, (G, NC), 0) < live
    for k in range(QUAD):
        block = emb_ref[:, k * NC:(k + 1) * NC]
        cot_own[k] = jnp.where(live_rows, block, jnp.zeros_like(block))

    pl.semaphore_wait(barrier, len(greeted))

    for k in range(1, Y):
        send(cot_own.at[ys[k]], cot_p1.at[y], p1_ss.at[k], p1_rs.at[y], y_peers[k])

    def w_part(index, half):
        return wg.at[index, pl.ds(half * HALF, HALF)]

    def w_fwd(step, piece):
        for way, to, block in ((0, right, wrap(z - step, Z)), (1, left, wrap(z + step, Z))):
            half = piece if way == 0 else 1 - piece
            part = w_part(block, half)
            if step:
                arrived(part, w_rs.at[way, step - 1, half])
            send(part, part, w_ss.at[way, step, half], w_rs.at[way, step, half], to)

    def w_finish():
        for way, block in ((0, wrap(z - 3, Z)), (1, wrap(z + 3, Z))):
            arrived(w_part(block, 1 - way), w_rs.at[way, 2, 1 - way])
        for way in (0, 1):
            arrived(w_part(wrap(z + 4, Z), way), w_rs.at[way, 3, way])

    w_fwd(0, 0)
    w_fwd(0, 1)
    cot_p1[y] = cot_own[y]

    inputs[2].wait()
    inputs[3].wait()
    for i in range(4):
        rows = pl.ds(i * 256, 256)
        product = dot(pw_ref[...], patches_ref[:, i * 256:(i + 1) * 256])
        product = jnp.transpose(jnp.concatenate([product, jnp.zeros((256 - FS, 256), F32)], axis=0))
        proj_s[0, rows] = product[:, :128]
        proj_s[1, rows] = product[:, 128:]

    parts = []
    for q in range(4):
        rows = pl.ds(q, G, stride=4)
        parts.append(jnp.concatenate([proj_s[0, rows, :], proj_s[1, rows, :]], axis=1)[:, :FS])
    projected = jnp.concatenate(parts, axis=1)

    first, second = group_rows(0), group_rows(4)

    def send_stats(index):
        mine = stats.at[index, t]
        for k in range(1, T):
            send(mine, mine, st_ss.at[index, k], st_rs.at[index, t], t_peers[k])

    def totals(index):
        for k in range(1, T):
            owner = wrap(t + k, T)
            arrived(stats.at[index, owner], st_rs.at[index, owner])
        total = stats[index, 0]
        for k in range(1, T):
            total = total + stats[index, k]
        return total / E

    def spread(rows, value):
        return dot(value, rows, ((0,), (0,)), HIGH)

    stats[0, t] = (
        dot(first, projected, ((1,), (1,)), HIGH)
        + dot(second, projected * projected, ((1,), (1,)), HIGH)
    )
    send_stats(0)
    w_fwd(1, 0)

    for k in (1, 3, 2, 0):
        origin = xs[k]
        block = cot_p1.at[origin]

        @pl.when(origin != y)
        def _():
            arrived(block, p1_rs.at[origin])

        slot = cot_all.at[x, c * QUAD + y]
        if k:
            send(block, slot, p2_ss.at[k], p2_rs.at[x], x_peers[k])
        else:
            slot[...] = block[...]

    def cot_block(k, j):
        return cot_all.at[xs[k], c * QUAD + ys[j]]

    def to_sibling(k, j):
        block = cot_block(k, j)
        send(block, block, cs_ss.at[k, j], cs_rs.at[xs[k], ys[j]], sibling)

    def cot_out(k):
        block = cot_block(k, 0)
        if k:
            arrived(block, p2_rs.at[xs[k]])
        for j in (1, 3):
            send(block, block, p3_ss.at[k, j], p3_rs.at[xs[k], y], y_peers[j])
        to_sibling(k, 0)

    def cot_on(k):
        for half, j in ((0, 1), (1, 3)):
            block = cot_block(k, j)
            arrived(block, p3_rs.at[xs[k], ys[j]])
            part = block.at[pl.ds(half * 128, 128)]
            send(part, part, ph_ss.at[k, half], ph_rs.at[xs[k], half], y_peers[4 - j])
        to_sibling(k, 1)
        to_sibling(k, 3)

    def cot_far(k):
        for half in (0, 1):
            arrived(cot_block(k, 2).at[pl.ds(half * 128, 128)], ph_rs.at[xs[k], half])
        to_sibling(k, 2)

    def cot_in(k):
        for j in range(Y):
            arrived(cot_all.at[xs[k], (1 - c) * QUAD + ys[j]], cs_rs.at[xs[k], ys[j]])

    cot_out(0)
    w_fwd(1, 1)

    means = totals(0)
    row = lax.broadcasted_iota(jnp.int32, (8, G), 0)
    row_mean = pltpu.roll(means, 4, 0)
    inv_scale = jnp.where(row >= 4, lax.rsqrt(
        jnp.where(row >= 4, means - row_mean * row_mean, 1.0) + 1e-05), 0.0)
    inv_wide = spread(second, inv_scale)
    normed = (projected - spread(first, means)) * inv_wide
    normed_s[0] = normed
    normed_s[1] = inv_wide
    merged_all[x] = normed.astype(BF16)
    for k in range(1, X):
        send(merged_all.at[x], merged_all.at[x], m_ss.at[k], m_rs.at[x], x_peers[k])

    w_fwd(2, 0)
    cot_on(0)
    cot_out(1)
    cot_out(3)
    w_fwd(2, 1)
    cot_out(2)
    merged_t[:, pl.ds(x * G, G)] = jnp.transpose(merged_all[x])
    cot_far(0)
    w_fwd(3, 0)
    cot_on(1)
    cot_on(3)
    cot_far(1)
    cot_on(2)
    cot_far(3)
    cot_far(2)
    w_finish()
    for k in (0, 1, 3, 2):
        cot_in(k)
    for k in (3, 1, 2):
        arrived(merged_all.at[xs[k]], m_rs.at[xs[k]])

    def d_term(owner):
        total = None
        for block in range(Z):
            term = dot(cot_all[owner, block], wg[block], ((1,), (1,)))
            total = term if total is None else total + term
        return total

    def d_sums(term, owner):
        rounded = term.astype(BF16)
        product = (term * merged_all[owner].astype(F32)).astype(BF16)
        return (dot(first.astype(BF16), rounded, ((1,), (1,)))
                + dot(second.astype(BF16), product, ((1,), (1,))))

    for k in (1, 3, 2):
        term = d_term(xs[k])
        d_send_buf[k] = term.astype(BF16)
        sx_send[k] = d_sums(term, xs[k])
        send(sx_send.at[k], sx_recv.at[x], sx_ss.at[k], sx_rs.at[x], x_peers[k])
        send(d_send_buf.at[k], d_recv_buf.at[x], d_ss.at[k], d_rs.at[x], x_peers[k])

    for k in range(1, X):
        merged_t[:, pl.ds(xs[k] * G, G)] = jnp.transpose(merged_all[xs[k]])

    def merge_term(block, rows=slice(None)):
        return dot(merged_t[rows], cot_all[:, block].reshape(X * G, NC))

    def g_block(way, step):
        return wrap(z + 4 - step, Z) if way == 0 else wrap(z - 4 + step, Z)

    def g_out(way, step, half, value):
        g_send_buf[way, step, half] = value.astype(BF16)
        send(g_send_buf.at[way, step, half], g_recv_buf.at[way, step, half],
             g_ss.at[way, step, half], g_rs.at[way, step, half], right if way == 0 else left)

    def g_in(way, step, half):
        arrived(g_recv_buf.at[way, step, half], g_rs.at[way, step, half])
        return g_recv_buf[way, step, half].astype(F32)

    def half_rows(half):
        return slice(half * HALF, (half + 1) * HALF)

    for way in (0, 1):
        g_out(way, 0, way, merge_term(g_block(way, 0), half_rows(way)))
    for way in (0, 1):
        g_out(way, 1, 1 - way, merge_term(g_block(way, 1), half_rows(1 - way)))

    def g_piece(step, piece):
        for way in (0, 1):
            half = 1 - way if piece == 0 else way
            term = merge_term(g_block(way, step), half_rows(half))
            g_out(way, step, half, term + g_in(way, step - 1, half))

    for n in range(X):
        rows = merged_all[xs[(n + 1) % X]]
        for m in range(QUAD):
            block = wg[(1 - c) * QUAD + ys[(m + 1) % Y]]
            e_sib_send[n, m] = dot(rows, block).astype(BF16)
        send(e_sib_send.at[n], e_sib_recv.at[n], es_ss.at[n], es_rs.at[n], sibling)

    def e_out(n):
        rows = merged_all[xs[(n + 1) % X]]
        arrived(e_sib_recv.at[n], es_rs.at[n])
        for m in range(QUAD):
            value = dot(rows, wg[c * QUAD + ys[(m + 1) % Y]]) + e_sib_recv[n, m].astype(F32)
            e_send[n, m] = value.astype(BF16)
            if m < QUAD - 1:
                send(e_send.at[n, m], e_recv.at[y, n], ey_ss.at[n, m], ey_rs.at[y, n], y_peers[m + 1])

    def e_sum_up(n):
        total = e_send[n, QUAD - 1].astype(F32)
        for j in range(1, Y):
            arrived(e_recv.at[ys[j], n], ey_rs.at[ys[j], n])
            total = total + e_recv[ys[j], n].astype(F32)
        total = total.astype(BF16)
        if n < X - 1:
            e_sum[n] = total
            send(e_sum.at[n], e_p2.at[x], e2_ss.at[n], e2_rs.at[x], x_peers[n + 1])
        else:
            e_p2[x] = total

    def e_home(k):
        origin = xs[k]
        block = e_p2.at[origin]
        if k:
            arrived(block, e2_rs.at[origin])

        @pl.when(origin == y)
        def _():
            e_fin[y] = block[...]

        @pl.when(origin != y)
        def _():
            pltpu.make_async_remote_copy(
                src_ref=block, dst_ref=e_fin.at[y], send_sem=e1_ss.at[k], recv_sem=e1_rs.at[y],
                device_id=device(x, origin, z, c), device_id_type=pl.DeviceIdType.MESH,
            ).start()

    e_out(0)
    term = d_term(x)
    d_own[...] = term
    total = d_sums(term, x)
    g_piece(1, 1)
    for k in range(1, X):
        arrived(sx_recv.at[xs[k]], sx_rs.at[xs[k]])
        total = total + sx_recv[xs[k]]
    stats[1, t] = total
    send_stats(1)
    g_piece(2, 0)
    e_out(1)
    e_out(2)
    e_out(3)
    g_piece(2, 1)
    e_sum_up(0)

    means = totals(1)
    d_mean = spread(first, means)
    dn_mean = spread(second, means)
    dnormed = d_own[...]
    for k in (3, 1, 2):
        arrived(d_recv_buf.at[xs[k]], d_rs.at[xs[k]])
        dnormed = dnormed + d_recv_buf[xs[k]].astype(F32)
    grad_input = (dnormed - d_mean - normed_s[0] * dn_mean) * normed_s[1]
    for q in range(4):
        part = grad_input[:, q * FS:(q + 1) * FS]
        part = jnp.concatenate([part, jnp.zeros((G, 256 - FS), F32)], axis=1)
        rows = pl.ds(q, G, stride=4)
        proj_s[0, rows, :] = part[:, :128]
        proj_s[1, rows, :] = part[:, 128:]
    grad_rows = jnp.concatenate([proj_s[0], proj_s[1]], axis=1)
    grad_rows = jnp.transpose(grad_rows)[:FS].astype(BF16)

    g_piece(3, 0)

    for chunk in (0, 1):
        low, high = 640 * chunk, min(640 * (chunk + 1), PD)
        if chunk:
            t_s[chunk, :, 512:] = jnp.zeros((FS, 128), BF16)
        t_s[chunk, :, :high - low] = dot(
            grad_rows, patches_ref[low:high], ((1,), (1,))).astype(BF16)
        for p in range(50):
            i, j = p % 10, p // 10
            a_own[chunk, p // 13, p % 13] = t_s[chunk, 16 * i:16 * (i + 1), 128 * j:128 * (j + 1)]
        for p in range(50, 52):
            a_own[chunk, p // 13, p % 13] = jnp.zeros((16, 128), BF16)
        for k in (1, 3, 2):
            send(a_own.at[chunk, xs[k]], a_xr.at[chunk, x], ax_ss.at[chunk, k],
                 ax_rs.at[chunk, x], x_peers[k])

    def over_z(chunk):
        total = a_own[chunk, x].astype(F32)
        for k in (3, 1, 2):
            arrived(a_xr.at[chunk, xs[k]], ax_rs.at[chunk, xs[k]])
            total = total + a_xr[chunk, xs[k]].astype(F32)
        a_x[chunk, pl.ds(0, 13)] = total.astype(BF16)
        a_x[chunk, pl.ds(13, 3)] = jnp.zeros((3, 16, 128), BF16)
        for k in (1, 7, 2, 6, 3, 5, 4):
            send(a_x.at[chunk, pl.ds(2 * zs[k], 2)], a_zr.at[chunk, z], az_ss.at[chunk, k],
                 az_rs.at[chunk, z], z_peers[k])

    def back_over_z(chunk):
        total = a_x[chunk, pl.ds(2 * z, 2)].astype(F32)
        for k in range(1, Z):
            arrived(a_zr.at[chunk, zs[k]], az_rs.at[chunk, zs[k]])
            total = total + a_zr[chunk, zs[k]].astype(F32)
        mine = a_all.at[chunk, x, pl.ds(2 * z, 2)]
        mine[...] = total.astype(BF16)
        for k in (1, 7, 2, 6, 3, 5, 4):
            send(mine, mine, bz_ss.at[chunk, k], bz_rs.at[chunk, z], z_peers[k])

    def back_over_x(chunk):
        for k in range(1, Z):
            arrived(a_all.at[chunk, x, pl.ds(2 * zs[k], 2)], bz_rs.at[chunk, zs[k]])
        mine = a_all.at[chunk, x, pl.ds(0, 13)]
        for k in (1, 3, 2):
            send(mine, mine, bx_ss.at[chunk, k], bx_rs.at[chunk, x], x_peers[k])

    g_piece(3, 1)
    e_sum_up(1)
    over_z(0)
    over_z(1)
    e_sum_up(2)
    back_over_z(0)
    back_over_z(1)
    e_sum_up(3)
    back_over_x(0)
    e_home(3)
    e_home(2)
    back_over_x(1)
    e_home(1)
    e_home(0)

    term = merge_term(z)
    for half in (0, 1):
        gm_ref[pl.ds(half * HALF, HALF)] = (
            term[half_rows(half)] + g_in(0, 3, half) + g_in(1, 3, half))
    outputs = [pltpu.make_async_copy(gm_ref, gm_hbm, out_s.at[0])]
    outputs[0].start()

    for k in range(1, Y):
        arrived(e_fin.at[ys[k]], e1_rs.at[ys[k]])
    for k in range(QUAD):
        block = e_fin[k]
        embeds_ref[:, k * NC:(k + 1) * NC] = jnp.where(live_rows, block, jnp.zeros_like(block))
    outputs.append(pltpu.make_async_copy(embeds_ref, embeds_hbm, out_s.at[1]))
    outputs[1].start()

    for chunk in (0, 1):
        for k in range(1, X):
            arrived(a_all.at[chunk, xs[k], pl.ds(0, 13)], bx_rs.at[chunk, xs[k]])
        for p in range(50):
            i, j = p % 10, 5 * chunk + p // 10
            rows = slice(16 * i, 16 * (i + 1))
            tile = a_all[chunk, p // 13, p % 13].astype(F32)
            if j < 9:
                gp_ref[rows, 128 * j:128 * (j + 1)] = tile
            else:
                gp_ref[rows, 1152:] = tile[:, :PD - 1152]
    outputs.append(pltpu.make_async_copy(gp_ref, gp_hbm, out_s.at[2]))
    outputs[2].start()

    for k in range(X):
        @pl.when(xs[k] != y)
        def _():
            pltpu.make_async_remote_copy(
                src_ref=e_p2.at[xs[k]], dst_ref=e_fin.at[y], send_sem=e1_ss.at[k],
                recv_sem=e1_rs.at[y], device_id=device(x, xs[k], z, c),
                device_id_type=pl.DeviceIdType.MESH,
            ).wait_send()
    for copy in outputs:
        copy.wait()
    for copy in started:
        copy.wait_send()


def finish(embeds_in, gm_in, gp_in, embeds_out, gm_out, gp_out, embeds_s, gm_s, gp_s, sems):
    parts = []
    for i, (src, held, dst, rows) in enumerate((
        (embeds_in, embeds_s, embeds_out, G), (gm_in, gm_s, gm_out, K), (gp_in, gp_s, gp_out, FS)
    )):
        for half in (0, 1):
            part = pl.ds(half * rows // 2, rows // 2)
            parts.append((
                pltpu.make_async_copy(src.at[part], held.at[part], sems.at[0, i, half]),
                pltpu.make_async_copy(held.at[part], dst.at[part], sems.at[1, i, half]),
            ))
    for load, _ in parts:
        load.start()
    for load, store in parts:
        load.wait()
        store.start()
    for _, store in parts:
        store.wait()


def body(patches, rank_groups, patch_weight, merge_weight, emb_grad):
    dma = pltpu.SemaphoreType.DMA
    rows = 4 * G
    scratch = [
        pltpu.VMEM((G, QUAD * NC), BF16),
        pltpu.VMEM((K, NC), F32),
        pltpu.VMEM((FS, PD), F32),
        pltpu.VMEM((PD, rows), BF16),
        pltpu.VMEM((FS, PD), BF16),
        pltpu.VMEM((G, QUAD * NC), BF16),
        pltpu.VMEM((Z, K, NC), BF16),
        pltpu.VMEM((QUAD, G, NC), BF16),
        pltpu.VMEM((Y, G, NC), BF16),
        pltpu.VMEM((X, Z, G, NC), BF16),
        pltpu.VMEM((X, G, K), BF16),
        pltpu.VMEM((K, X * G), BF16),
        pltpu.VMEM((2, rows, 128), F32),
        pltpu.VMEM((2, G, K), F32),
        pltpu.VMEM((2, T, 8, G), F32),
        pltpu.VMEM((X, 8, G), F32),
        pltpu.VMEM((X, 8, G), F32),
        pltpu.VMEM((2, 4, 2, HALF, NC), BF16),
        pltpu.VMEM((2, 4, 2, HALF, NC), BF16),
        pltpu.VMEM((X, G, K), BF16),
        pltpu.VMEM((G, K), F32),
        pltpu.VMEM((X, G, K), BF16),
        pltpu.VMEM((X, QUAD, G, NC), BF16),
        pltpu.VMEM((X, QUAD, G, NC), BF16),
        pltpu.VMEM((X, QUAD, G, NC), BF16),
        pltpu.VMEM((Y, X, G, NC), BF16),
        pltpu.VMEM((X, G, NC), BF16),
        pltpu.VMEM((X, G, NC), BF16),
        pltpu.VMEM((QUAD, G, NC), BF16),
        pltpu.VMEM((2, FS, 640), BF16),
        pltpu.VMEM((2, X, 13, 16, 128), BF16),
        pltpu.VMEM((2, X, 13, 16, 128), BF16),
        pltpu.VMEM((2, 16, 16, 128), BF16),
        pltpu.VMEM((2, Z, 2, 16, 128), BF16),
        pltpu.VMEM((2, X, 16, 16, 128), BF16),
        dma((4,)),
        dma((3,)),
    ]
    for shape in (
        (2, 4, 2), (4,), (4,), (4, 4), (4, 2), (4, 4), (2, 8), (4,), (4,),
        (4,), (2, 4, 2), (4,), (4, 4), (4,), (4,), (2, 4), (2, 8), (2, 8), (2, 4),
    ):
        scratch += [dma(shape), dma(shape)]
    results = (
        jax.ShapeDtypeStruct((G, QUAD * NC), BF16),
        jax.ShapeDtypeStruct((K, NC), F32),
        jax.ShapeDtypeStruct((FS, PD), F32),
    )
    hbm = pl.BlockSpec(memory_space=pl.ANY)
    partial = pl.pallas_call(
        kernel,
        out_shape=results,
        in_specs=[pl.BlockSpec(memory_space=pltpu.SMEM)] + [hbm] * 4,
        out_specs=(hbm, hbm, hbm),
        scratch_shapes=scratch,
        compiler_params=pltpu.CompilerParams(
            collective_id=0, has_side_effects=True, vmem_limit_bytes=56 * 2**20
        ),
        name="tower",
    )(rank_groups, patches.T, patch_weight.T, merge_weight.reshape(K, NC), emb_grad)
    embeds, grad_merge, grad_patch = pl.pallas_call(
        finish,
        out_shape=results,
        in_specs=[hbm, hbm, hbm],
        out_specs=(hbm, hbm, hbm),
        scratch_shapes=[
            pltpu.VMEM((G, QUAD * NC), BF16),
            pltpu.VMEM((K, NC), F32),
            pltpu.VMEM((FS, PD), F32),
            dma((2, 3, 2)),
        ],
        name="finish",
    )(*partial)
    return embeds, grad_merge.reshape(4, FS, NC), grad_patch.T


def solution(mesh):
    return jax.shard_map(
        body,
        mesh=mesh,
        in_specs=(
            P("dp", None),
            P("dp"),
            P(None, "tensor"),
            P(None, "tensor", "dp"),
            P("dp", "tensor"),
        ),
        out_specs=(P("dp", "tensor"), P(None, "tensor", "dp"), P(None, "tensor")),
        check_vma=False,
    )
```

```python
import functools

import jax
import jax.numpy as jnp
from jax import lax
from jax.experimental import pallas as pl
from jax.experimental.pallas import tpu as pltpu
from jax.sharding import PartitionSpec as P

E = 1280
X, Y, Z = 4, 4, 8
T = 2 * Y
F32, BF16 = jnp.float32, jnp.bfloat16
HIGH = lax.Precision.HIGHEST

PD = 1176
FS = E // T
K = 4 * FS
G = 256
NC = 256
HALF = K // 2
QUAD = Z // 2


def dot(a, b, dims=((1,), (0,)), precision=None):
    return lax.dot_general(a, b, (dims, ((), ())), precision=precision, preferred_element_type=F32)


def wrap(value, count):
    return lax.rem(value + count, count)


def group_rows(offset):
    row = lax.broadcasted_iota(jnp.int32, (8, K), 0)
    lane = lax.broadcasted_iota(jnp.int32, (8, K), 1)
    low = (row - offset) * FS
    return jnp.where((lane >= low) & (lane < low + FS), 1.0, 0.0).astype(F32)


def kernel(
    live_ref, patches_hbm, pw_hbm, w_hbm, emb_hbm,
    embeds_hbm, gm_hbm, gp_hbm,
    embeds_ref, gm_ref, gp_ref,
    patches_ref, pw_ref, emb_ref,
    wg, cot_own, cot_p1, cot_all, merged_all, merged_t, proj_s, normed_s,
    stats, sx_send, sx_recv, g_send_buf, g_recv_buf,
    d_send_buf, d_keep, d_far, d_own, d_recv_buf,
    e_sib_send, e_sib_recv, e_send, e_recv, e_sum, e_p2, e_fin,
    t_s, a_own, a_xr, a_x, a_zr, a_all,
    in_s, out_s,
    w_ss, w_rs, p1_ss, p1_rs, p2_ss, p2_rs, p3_ss, p3_rs, ph_ss, ph_rs, cs_ss, cs_rs,
    st_ss, st_rs, sx_ss, sx_rs, m_ss, m_rs,
    d_ss, d_rs, df_ss, df_rs, g_ss, g_rs, es_ss, es_rs, ey_ss, ey_rs, e2_ss, e2_rs, e1_ss, e1_rs,
    ax_ss, ax_rs, az_ss, az_rs, bz_ss, bz_rs, bx_ss, bx_rs,
):
    dp = lax.axis_index("dp")
    t = lax.axis_index("tensor")
    x, z = lax.div(dp, Z), lax.rem(dp, Z)
    y, c = lax.div(t, 2), lax.rem(t, 2)

    def device(x, y, z, c):
        return (x * Z + z, y * 2 + c)

    started = []

    def send(src, dst, ssem, rsem, to):
        copy = pltpu.make_async_remote_copy(
            src_ref=src, dst_ref=dst, send_sem=ssem, recv_sem=rsem,
            device_id=to, device_id_type=pl.DeviceIdType.MESH,
        )
        copy.start()
        started.append(copy)

    def arrived(dst, rsem):
        pltpu.make_async_remote_copy(
            src_ref=dst, dst_ref=dst, send_sem=w_ss.at[0, 0, 0], recv_sem=rsem,
            device_id=sibling, device_id_type=pl.DeviceIdType.MESH,
        ).wait_recv()

    right = device(x, y, wrap(z + 1, Z), c)
    left = device(x, y, wrap(z - 1, Z), c)
    sibling = device(x, y, z, 1 - c)
    xs = [wrap(x + k, X) for k in range(X)]
    ys = [wrap(y + k, Y) for k in range(Y)]
    zs = [wrap(z + k, Z) for k in range(Z)]
    x_peers = [device(i, y, z, c) for i in xs]
    y_peers = [device(x, i, z, c) for i in ys]
    z_peers = [device(x, y, i, c) for i in zs]
    t_peers = [(dp, wrap(t + k, T)) for k in range(T)]

    inputs = [
        pltpu.make_async_copy(w_hbm, wg.at[z], in_s.at[0]),
        pltpu.make_async_copy(emb_hbm, emb_ref, in_s.at[1]),
        pltpu.make_async_copy(pw_hbm, pw_ref, in_s.at[2]),
        pltpu.make_async_copy(patches_hbm, patches_ref, in_s.at[3]),
    ]
    for copy in inputs:
        copy.start()

    barrier = pltpu.get_barrier_semaphore()
    greeted = x_peers[1:] + z_peers[1:] + t_peers[1:]
    for peer in greeted:
        pl.semaphore_signal(barrier, inc=1, device_id=peer, device_id_type=pl.DeviceIdType.MESH)

    inputs[0].wait()
    inputs[1].wait()
    live = live_ref[0]
    live_rows = lax.broadcasted_iota(jnp.int32, (G, NC), 0) < live
    for k in range(QUAD):
        block = emb_ref[:, k * NC:(k + 1) * NC]
        cot_own[k] = jnp.where(live_rows, block, jnp.zeros_like(block))

    pl.semaphore_wait(barrier, len(greeted))

    def rows_of(half):
        return pl.ds(half * 128, 128)

    for half in (0, 1):
        for k in (1, 3, 2):
            send(cot_own.at[ys[k], rows_of(half)], cot_p1.at[y, rows_of(half)],
                 p1_ss.at[k, half], p1_rs.at[y, half], y_peers[k])

    def w_part(index, half):
        return wg.at[index, pl.ds(half * HALF, HALF)]

    def w_fwd(step, piece):
        for way, to, block in ((0, right, wrap(z - step, Z)), (1, left, wrap(z + step, Z))):
            half = piece if way == 0 else 1 - piece
            part = w_part(block, half)
            if step:
                arrived(part, w_rs.at[way, step - 1, half])
            send(part, part, w_ss.at[way, step, half], w_rs.at[way, step, half], to)

    def w_finish():
        for way, block in ((0, wrap(z - 3, Z)), (1, wrap(z + 3, Z))):
            arrived(w_part(block, 1 - way), w_rs.at[way, 2, 1 - way])
        for way in (0, 1):
            arrived(w_part(wrap(z + 4, Z), way), w_rs.at[way, 3, way])

    w_fwd(0, 0)
    w_fwd(0, 1)
    cot_p1[y] = cot_own[y]

    inputs[2].wait()
    inputs[3].wait()
    for i in range(4):
        rows = pl.ds(i * 256, 256)
        product = dot(pw_ref[...], patches_ref[:, i * 256:(i + 1) * 256])
        product = jnp.transpose(jnp.concatenate([product, jnp.zeros((256 - FS, 256), F32)], axis=0))
        proj_s[0, rows] = product[:, :128]
        proj_s[1, rows] = product[:, 128:]

    parts = []
    for q in range(4):
        rows = pl.ds(q, G, stride=4)
        parts.append(jnp.concatenate([proj_s[0, rows, :], proj_s[1, rows, :]], axis=1)[:, :FS])
    projected = jnp.concatenate(parts, axis=1)

    first, second = group_rows(0), group_rows(4)

    def send_stats(index):
        mine = stats.at[index, t]
        for k in range(1, T):
            send(mine, mine, st_ss.at[index, k], st_rs.at[index, t], t_peers[k])

    def totals(index):
        for k in range(1, T):
            owner = wrap(t + k, T)
            arrived(stats.at[index, owner], st_rs.at[index, owner])
        total = stats[index, 0]
        for k in range(1, T):
            total = total + stats[index, k]
        return total / E

    def spread(rows, value):
        return dot(value, rows, ((0,), (0,)), HIGH)

    stats[0, t] = (
        dot(first, projected, ((1,), (1,)), HIGH)
        + dot(second, projected * projected, ((1,), (1,)), HIGH)
    )
    send_stats(0)
    def cot_over_x(half):
        for k in (1, 3, 2, 0):
            origin = xs[k]
            block = cot_p1.at[origin, rows_of(half)]

            @pl.when(origin != y)
            def _():
                arrived(block, p1_rs.at[origin, half])

            slot = cot_all.at[x, c * QUAD + y, rows_of(half)]
            if k:
                send(block, slot, p2_ss.at[k, half], p2_rs.at[x, half], x_peers[k])
            else:
                slot[...] = block[...]

    def cot_block(k, j):
        return cot_all.at[xs[k], c * QUAD + ys[j]]

    def to_sibling(k, j):
        block = cot_block(k, j)
        send(block, block, cs_ss.at[k, j], cs_rs.at[xs[k], ys[j]], sibling)

    def cot_out(k, half):
        part = cot_block(k, 0).at[rows_of(half)]
        if k:
            arrived(part, p2_rs.at[xs[k], half])
        for j in (1, 3):
            send(part, part, p3_ss.at[k, j, half], p3_rs.at[xs[k], y, half], y_peers[j])
        if half:
            to_sibling(k, 0)

    def cot_on(k):
        for half, j in ((0, 1), (1, 3)):
            part = cot_block(k, j).at[rows_of(half)]
            arrived(part, p3_rs.at[xs[k], ys[j], half])
            send(part, part, ph_ss.at[k, half], ph_rs.at[xs[k], half], y_peers[4 - j])
        for half, j in ((1, 1), (0, 3)):
            arrived(cot_block(k, j).at[rows_of(half)], p3_rs.at[xs[k], ys[j], half])
            to_sibling(k, j)

    def cot_far(k):
        for half in (0, 1):
            arrived(cot_block(k, 2).at[rows_of(half)], ph_rs.at[xs[k], half])
        to_sibling(k, 2)

    def cot_in(k):
        for j in range(Y):
            arrived(cot_all.at[xs[k], (1 - c) * QUAD + ys[j]], cs_rs.at[xs[k], ys[j]])

    cot_over_x(0)
    w_fwd(1, 0)
    cot_out(0, 0)
    cot_over_x(1)
    cot_out(0, 1)
    cot_out(1, 0)
    cot_out(3, 0)
    w_fwd(1, 1)

    means = totals(0)
    row = lax.broadcasted_iota(jnp.int32, (8, G), 0)
    row_mean = pltpu.roll(means, 4, 0)
    inv_scale = jnp.where(row >= 4, lax.rsqrt(
        jnp.where(row >= 4, means - row_mean * row_mean, 1.0) + 1e-05), 0.0)
    inv_wide = spread(second, inv_scale)
    normed = (projected - spread(first, means)) * inv_wide
    normed_s[0] = normed
    normed_s[1] = inv_wide
    merged_all[x] = normed.astype(BF16)
    for k in range(1, X):
        send(merged_all.at[x], merged_all.at[x], m_ss.at[k], m_rs.at[x], x_peers[k])

    cot_out(2, 0)
    cot_out(1, 1)
    cot_out(3, 1)
    w_fwd(2, 0)
    cot_on(0)
    cot_out(2, 1)
    w_fwd(2, 1)
    merged_t[:, pl.ds(x * G, G)] = jnp.transpose(merged_all[x])
    cot_far(0)
    w_fwd(3, 0)
    cot_on(1)
    cot_on(3)
    cot_far(1)
    cot_on(2)
    cot_far(3)
    cot_far(2)
    w_finish()
    for k in (0, 1, 3, 2):
        cot_in(k)
    for k in (3, 1, 2):
        arrived(merged_all.at[xs[k]], m_rs.at[xs[k]])

    def d_term(owner):
        total = None
        for block in range(Z):
            term = dot(cot_all[owner, block], wg[block], ((1,), (1,)))
            total = term if total is None else total + term
        return total

    def d_sums(term, owner):
        rounded = term.astype(BF16)
        product = (term * merged_all[owner].astype(F32)).astype(BF16)
        return (dot(first.astype(BF16), rounded, ((1,), (1,)))
                + dot(second.astype(BF16), product, ((1,), (1,))))

    def d_near(way, half, to):
        slot = 1 if way == 0 else 3
        part = pl.ds(half * 128, 128)
        send(d_send_buf.at[slot, part], d_recv_buf.at[way, part], d_ss.at[way, half],
             d_rs.at[way, half], to)

    for k, to in ((2, None), (1, x_peers[1]), (3, x_peers[3])):
        term = d_term(xs[k])
        d_send_buf[k] = term.astype(BF16)
        sx_send[k] = d_sums(term, xs[k])
        send(sx_send.at[k], sx_recv.at[x], sx_ss.at[k], sx_rs.at[x], x_peers[k])
        if k == 2:
            for way, peer in ((0, x_peers[1]), (1, x_peers[3])):
                send(d_send_buf.at[2, rows_of(way)], d_far.at[way], df_ss.at[way],
                     df_rs.at[way], peer)
        else:
            way = 0 if k == 1 else 1
            d_keep[way] = term[way * 128:(way + 1) * 128]
            d_near(way, 1 - way, to)

    def d_combine():
        for way, slot, to in ((0, 1, x_peers[1]), (1, 3, x_peers[3])):
            arrived(d_far.at[way], df_rs.at[way])
            d_send_buf[slot, rows_of(way)] = (d_keep[way] + d_far[way].astype(F32)).astype(BF16)
            d_near(way, way, to)

    for k in range(1, X):
        merged_t[:, pl.ds(xs[k] * G, G)] = jnp.transpose(merged_all[xs[k]])

    def merge_term(block, rows=slice(None)):
        return dot(merged_t[rows], cot_all[:, block].reshape(X * G, NC))

    def g_block(way, step):
        return wrap(z + 4 - step, Z) if way == 0 else wrap(z - 4 + step, Z)

    def g_out(way, step, half, value):
        g_send_buf[way, step, half] = value.astype(BF16)
        send(g_send_buf.at[way, step, half], g_recv_buf.at[way, step, half],
             g_ss.at[way, step, half], g_rs.at[way, step, half], right if way == 0 else left)

    def g_in(way, step, half):
        arrived(g_recv_buf.at[way, step, half], g_rs.at[way, step, half])
        return g_recv_buf[way, step, half].astype(F32)

    def half_rows(half):
        return slice(half * HALF, (half + 1) * HALF)

    for way in (0, 1):
        g_out(way, 0, way, merge_term(g_block(way, 0), half_rows(way)))
    for way in (0, 1):
        g_out(way, 1, 1 - way, merge_term(g_block(way, 1), half_rows(1 - way)))

    def g_piece(step, piece):
        for way in (0, 1):
            half = 1 - way if piece == 0 else way
            term = merge_term(g_block(way, step), half_rows(half))
            g_out(way, step, half, term + g_in(way, step - 1, half))

    for n in range(X):
        rows = merged_all[xs[(n + 1) % X]]
        for m in range(QUAD):
            block = wg[(1 - c) * QUAD + ys[(m + 1) % Y]]
            e_sib_send[n, m] = dot(rows, block).astype(BF16)
        send(e_sib_send.at[n], e_sib_recv.at[n], es_ss.at[n], es_rs.at[n], sibling)

    def e_out(n):
        rows = merged_all[xs[(n + 1) % X]]
        arrived(e_sib_recv.at[n], es_rs.at[n])
        for m in range(QUAD):
            value = dot(rows, wg[c * QUAD + ys[(m + 1) % Y]]) + e_sib_recv[n, m].astype(F32)
            e_send[n, m] = value.astype(BF16)
            if m < QUAD - 1:
                send(e_send.at[n, m], e_recv.at[y, n], ey_ss.at[n, m], ey_rs.at[y, n], y_peers[m + 1])

    def e_sum_up(n):
        total = e_send[n, QUAD - 1].astype(F32)
        for j in range(1, Y):
            arrived(e_recv.at[ys[j], n], ey_rs.at[ys[j], n])
            total = total + e_recv[ys[j], n].astype(F32)
        total = total.astype(BF16)
        if n < X - 1:
            e_sum[n] = total
            send(e_sum.at[n], e_p2.at[x], e2_ss.at[n], e2_rs.at[x], x_peers[n + 1])
        else:
            e_p2[x] = total

    def e_home(k):
        origin = xs[k]
        block = e_p2.at[origin]
        if k:
            arrived(block, e2_rs.at[origin])

        @pl.when(origin == y)
        def _():
            e_fin[y] = block[...]

        @pl.when(origin != y)
        def _():
            pltpu.make_async_remote_copy(
                src_ref=block, dst_ref=e_fin.at[y], send_sem=e1_ss.at[k], recv_sem=e1_rs.at[y],
                device_id=device(x, origin, z, c), device_id_type=pl.DeviceIdType.MESH,
            ).start()

    d_combine()
    term = d_term(x)
    d_own[...] = term
    total = d_sums(term, x)
    for k in range(1, X):
        arrived(sx_recv.at[xs[k]], sx_rs.at[xs[k]])
        total = total + sx_recv[xs[k]]
    stats[1, t] = total
    send_stats(1)
    e_out(0)
    g_piece(1, 1)
    e_out(1)
    e_out(2)
    e_out(3)
    g_piece(2, 0)

    means = totals(1)
    d_mean = spread(first, means)
    dn_mean = spread(second, means)
    dnormed = d_own[...]
    for way in (0, 1):
        for half in (1 - way, way):
            arrived(d_recv_buf.at[way, rows_of(half)], d_rs.at[way, half])
        dnormed = dnormed + d_recv_buf[way].astype(F32)
    grad_input = (dnormed - d_mean - normed_s[0] * dn_mean) * normed_s[1]
    for q in range(4):
        part = grad_input[:, q * FS:(q + 1) * FS]
        part = jnp.concatenate([part, jnp.zeros((G, 256 - FS), F32)], axis=1)
        rows = pl.ds(q, G, stride=4)
        proj_s[0, rows, :] = part[:, :128]
        proj_s[1, rows, :] = part[:, 128:]
    grad_rows = jnp.concatenate([proj_s[0], proj_s[1]], axis=1)
    grad_rows = jnp.transpose(grad_rows)[:FS].astype(BF16)

    for chunk in (0, 1):
        low, high = 640 * chunk, min(640 * (chunk + 1), PD)
        if chunk:
            t_s[chunk, :, 512:] = jnp.zeros((FS, 128), BF16)
        t_s[chunk, :, :high - low] = dot(
            grad_rows, patches_ref[low:high], ((1,), (1,))).astype(BF16)
        for p in range(50):
            i, j = p % 10, p // 10
            a_own[chunk, p // 13, p % 13] = t_s[chunk, 16 * i:16 * (i + 1), 128 * j:128 * (j + 1)]
        for p in range(50, 52):
            a_own[chunk, p // 13, p % 13] = jnp.zeros((16, 128), BF16)
        for k in (1, 3, 2):
            send(a_own.at[chunk, xs[k]], a_xr.at[chunk, x], ax_ss.at[chunk, k],
                 ax_rs.at[chunk, x], x_peers[k])

    def over_z(chunk):
        total = a_own[chunk, x].astype(F32)
        for k in (3, 1, 2):
            arrived(a_xr.at[chunk, xs[k]], ax_rs.at[chunk, xs[k]])
            total = total + a_xr[chunk, xs[k]].astype(F32)
        a_x[chunk, pl.ds(0, 13)] = total.astype(BF16)
        a_x[chunk, pl.ds(13, 3)] = jnp.zeros((3, 16, 128), BF16)
        for k in (1, 7, 2, 6, 3, 5, 4):
            send(a_x.at[chunk, pl.ds(2 * zs[k], 2)], a_zr.at[chunk, z], az_ss.at[chunk, k],
                 az_rs.at[chunk, z], z_peers[k])

    def back_over_z(chunk):
        total = a_x[chunk, pl.ds(2 * z, 2)].astype(F32)
        for k in range(1, Z):
            arrived(a_zr.at[chunk, zs[k]], az_rs.at[chunk, zs[k]])
            total = total + a_zr[chunk, zs[k]].astype(F32)
        mine = a_all.at[chunk, x, pl.ds(2 * z, 2)]
        mine[...] = total.astype(BF16)
        for k in (1, 7, 2, 6, 3, 5, 4):
            send(mine, mine, bz_ss.at[chunk, k], bz_rs.at[chunk, z], z_peers[k])

    def back_over_x(chunk):
        for k in range(1, Z):
            arrived(a_all.at[chunk, x, pl.ds(2 * zs[k], 2)], bz_rs.at[chunk, zs[k]])
        mine = a_all.at[chunk, x, pl.ds(0, 13)]
        for k in (1, 3, 2):
            send(mine, mine, bx_ss.at[chunk, k], bx_rs.at[chunk, x], x_peers[k])

    outputs = []

    def g_finish():
        term = merge_term(z)
        for half in (0, 1):
            gm_ref[pl.ds(half * HALF, HALF)] = (
                term[half_rows(half)] + g_in(0, 3, half) + g_in(1, 3, half))
        outputs.append(pltpu.make_async_copy(gm_ref, gm_hbm, out_s.at[0]))
        outputs[0].start()

    g_piece(2, 1)
    e_sum_up(0)
    g_piece(3, 0)
    over_z(0)
    g_piece(3, 1)
    over_z(1)
    e_sum_up(1)
    e_home(3)
    back_over_z(0)
    back_over_z(1)
    e_sum_up(2)
    e_home(2)
    g_finish()
    back_over_x(0)
    back_over_x(1)
    e_sum_up(3)
    e_home(0)
    e_home(1)

    for k in range(1, Y):
        arrived(e_fin.at[ys[k]], e1_rs.at[ys[k]])
    for k in range(QUAD):
        block = e_fin[k]
        embeds_ref[:, k * NC:(k + 1) * NC] = jnp.where(live_rows, block, jnp.zeros_like(block))
    outputs.append(pltpu.make_async_copy(embeds_ref, embeds_hbm, out_s.at[1]))
    outputs[1].start()

    for chunk in (0, 1):
        for k in range(1, X):
            arrived(a_all.at[chunk, xs[k], pl.ds(0, 13)], bx_rs.at[chunk, xs[k]])
        for p in range(50):
            i, j = p % 10, 5 * chunk + p // 10
            rows = slice(16 * i, 16 * (i + 1))
            tile = a_all[chunk, p // 13, p % 13].astype(F32)
            if j < 9:
                gp_ref[rows, 128 * j:128 * (j + 1)] = tile
            else:
                gp_ref[rows, 1152:] = tile[:, :PD - 1152]
    outputs.append(pltpu.make_async_copy(gp_ref, gp_hbm, out_s.at[2]))
    outputs[2].start()

    for k in range(X):
        @pl.when(xs[k] != y)
        def _():
            pltpu.make_async_remote_copy(
                src_ref=e_p2.at[xs[k]], dst_ref=e_fin.at[y], send_sem=e1_ss.at[k],
                recv_sem=e1_rs.at[y], device_id=device(x, xs[k], z, c),
                device_id_type=pl.DeviceIdType.MESH,
            ).wait_send()
    for copy in outputs:
        copy.wait()
    for copy in started:
        copy.wait_send()


def finish(embeds_in, gm_in, gp_in, embeds_out, gm_out, gp_out, embeds_s, gm_s, gp_s, sems):
    parts = []
    for i, (src, held, dst, rows) in enumerate((
        (embeds_in, embeds_s, embeds_out, G), (gm_in, gm_s, gm_out, K), (gp_in, gp_s, gp_out, FS)
    )):
        for half in (0, 1):
            part = pl.ds(half * rows // 2, rows // 2)
            parts.append((
                pltpu.make_async_copy(src.at[part], held.at[part], sems.at[0, i, half]),
                pltpu.make_async_copy(held.at[part], dst.at[part], sems.at[1, i, half]),
            ))
    for load, _ in parts:
        load.start()
    for load, store in parts:
        load.wait()
        store.start()
    for _, store in parts:
        store.wait()


def body(patches, rank_groups, patch_weight, merge_weight, emb_grad):
    dma = pltpu.SemaphoreType.DMA
    rows = 4 * G
    scratch = [
        pltpu.VMEM((G, QUAD * NC), BF16),
        pltpu.VMEM((K, NC), F32),
        pltpu.VMEM((FS, PD), F32),
        pltpu.VMEM((PD, rows), BF16),
        pltpu.VMEM((FS, PD), BF16),
        pltpu.VMEM((G, QUAD * NC), BF16),
        pltpu.VMEM((Z, K, NC), BF16),
        pltpu.VMEM((QUAD, G, NC), BF16),
        pltpu.VMEM((Y, G, NC), BF16),
        pltpu.VMEM((X, Z, G, NC), BF16),
        pltpu.VMEM((X, G, K), BF16),
        pltpu.VMEM((K, X * G), BF16),
        pltpu.VMEM((2, rows, 128), F32),
        pltpu.VMEM((2, G, K), F32),
        pltpu.VMEM((2, T, 8, G), F32),
        pltpu.VMEM((X, 8, G), F32),
        pltpu.VMEM((X, 8, G), F32),
        pltpu.VMEM((2, 4, 2, HALF, NC), BF16),
        pltpu.VMEM((2, 4, 2, HALF, NC), BF16),
        pltpu.VMEM((X, G, K), BF16),
        pltpu.VMEM((2, 128, K), F32),
        pltpu.VMEM((2, 128, K), BF16),
        pltpu.VMEM((G, K), F32),
        pltpu.VMEM((2, G, K), BF16),
        pltpu.VMEM((X, QUAD, G, NC), BF16),
        pltpu.VMEM((X, QUAD, G, NC), BF16),
        pltpu.VMEM((X, QUAD, G, NC), BF16),
        pltpu.VMEM((Y, X, G, NC), BF16),
        pltpu.VMEM((X, G, NC), BF16),
        pltpu.VMEM((X, G, NC), BF16),
        pltpu.VMEM((QUAD, G, NC), BF16),
        pltpu.VMEM((2, FS, 640), BF16),
        pltpu.VMEM((2, X, 13, 16, 128), BF16),
        pltpu.VMEM((2, X, 13, 16, 128), BF16),
        pltpu.VMEM((2, 16, 16, 128), BF16),
        pltpu.VMEM((2, Z, 2, 16, 128), BF16),
        pltpu.VMEM((2, X, 16, 16, 128), BF16),
        dma((4,)),
        dma((3,)),
    ]
    for shape in (
        (2, 4, 2), (4, 2), (4, 2), (4, 4, 2), (4, 2), (4, 4), (2, 8), (4,), (4,),
        (2, 2), (2,), (2, 4, 2), (4,), (4, 4), (4,), (4,), (2, 4), (2, 8), (2, 8), (2, 4),
    ):
        scratch += [dma(shape), dma(shape)]
    results = (
        jax.ShapeDtypeStruct((G, QUAD * NC), BF16),
        jax.ShapeDtypeStruct((K, NC), F32),
        jax.ShapeDtypeStruct((FS, PD), F32),
    )
    hbm = pl.BlockSpec(memory_space=pl.ANY)
    partial = pl.pallas_call(
        kernel,
        out_shape=results,
        in_specs=[pl.BlockSpec(memory_space=pltpu.SMEM)] + [hbm] * 4,
        out_specs=(hbm, hbm, hbm),
        scratch_shapes=scratch,
        compiler_params=pltpu.CompilerParams(
            collective_id=0, has_side_effects=True, vmem_limit_bytes=56 * 2**20
        ),
        name="tower",
    )(rank_groups, patches.T, patch_weight.T, merge_weight.reshape(K, NC), emb_grad)
    embeds, grad_merge, grad_patch = pl.pallas_call(
        finish,
        out_shape=results,
        in_specs=[hbm, hbm, hbm],
        out_specs=(hbm, hbm, hbm),
        scratch_shapes=[
            pltpu.VMEM((G, QUAD * NC), BF16),
            pltpu.VMEM((K, NC), F32),
            pltpu.VMEM((FS, PD), F32),
            dma((2, 3, 2)),
        ],
        name="finish",
    )(*partial)
    return embeds, grad_merge.reshape(4, FS, NC), grad_patch.T


def solution(mesh):
    return jax.shard_map(
        body,
        mesh=mesh,
        in_specs=(
            P("dp", None),
            P("dp"),
            P(None, "tensor"),
            P(None, "tensor", "dp"),
            P("dp", "tensor"),
        ),
        out_specs=(P("dp", "tensor"), P(None, "tensor", "dp"), P(None, "tensor")),
        check_vma=False,
    )
```

```python
import functools

import jax
import jax.numpy as jnp
from jax import lax
from jax.experimental import pallas as pl
from jax.experimental.pallas import tpu as pltpu
from jax.sharding import PartitionSpec as P

E = 1280
X, Y, Z = 4, 4, 8
T = 2 * Y
F32, BF16 = jnp.float32, jnp.bfloat16
HIGH = lax.Precision.HIGHEST

PD = 1176
FS = E // T
K = 4 * FS
G = 256
NC = 256
HALF = K // 2
QUAD = Z // 2


def dot(a, b, dims=((1,), (0,)), precision=None):
    return lax.dot_general(a, b, (dims, ((), ())), precision=precision, preferred_element_type=F32)


def wrap(value, count):
    return lax.rem(value + count, count)


def group_rows(offset):
    row = lax.broadcasted_iota(jnp.int32, (8, K), 0)
    lane = lax.broadcasted_iota(jnp.int32, (8, K), 1)
    low = (row - offset) * FS
    return jnp.where((lane >= low) & (lane < low + FS), 1.0, 0.0).astype(F32)


def kernel(
    live_ref, patches_hbm, pw_hbm, w_hbm, emb_hbm,
    embeds_hbm, gm_hbm, gp_hbm,
    embeds_ref, gm_ref, gp_ref,
    patches_ref, pw_ref, emb_ref,
    wg, cot_own, cot_p1, cot_all, merged_all, merged_t, proj_s, normed_s,
    stats, sx_send, sx_recv, g_send_buf, g_recv_buf,
    d_send_buf, d_keep, d_far, d_own, d_recv_buf,
    e_sib_send, e_sib_recv, e_send, e_far, e_recv, e_sum, e_p2, e_fin,
    t_s, a_own, a_xr, a_x, a_zr, a_all,
    in_s, out_s,
    w_ss, w_rs, p1_ss, p1_rs, p2_ss, p2_rs, p3_ss, p3_rs, ph_ss, ph_rs, cs_ss, cs_rs,
    st_ss, st_rs, sx_ss, sx_rs, m_ss, m_rs,
    d_ss, d_rs, df_ss, df_rs, g_ss, g_rs, es_ss, es_rs, ef_ss, ef_rs, ey_ss, ey_rs, e2_ss, e2_rs, e1_ss, e1_rs,
    ax_ss, ax_rs, az_ss, az_rs, bz_ss, bz_rs, bx_ss, bx_rs,
):
    dp = lax.axis_index("dp")
    t = lax.axis_index("tensor")
    x, z = lax.div(dp, Z), lax.rem(dp, Z)
    y, c = lax.div(t, 2), lax.rem(t, 2)

    def device(x, y, z, c):
        return (x * Z + z, y * 2 + c)

    started = []

    def send(src, dst, ssem, rsem, to):
        copy = pltpu.make_async_remote_copy(
            src_ref=src, dst_ref=dst, send_sem=ssem, recv_sem=rsem,
            device_id=to, device_id_type=pl.DeviceIdType.MESH,
        )
        copy.start()
        started.append(copy)

    def arrived(dst, rsem):
        pltpu.make_async_remote_copy(
            src_ref=dst, dst_ref=dst, send_sem=w_ss.at[0, 0, 0], recv_sem=rsem,
            device_id=sibling, device_id_type=pl.DeviceIdType.MESH,
        ).wait_recv()

    right = device(x, y, wrap(z + 1, Z), c)
    left = device(x, y, wrap(z - 1, Z), c)
    sibling = device(x, y, z, 1 - c)
    xs = [wrap(x + k, X) for k in range(X)]
    ys = [wrap(y + k, Y) for k in range(Y)]
    zs = [wrap(z + k, Z) for k in range(Z)]
    x_peers = [device(i, y, z, c) for i in xs]
    y_peers = [device(x, i, z, c) for i in ys]
    z_peers = [device(x, y, i, c) for i in zs]
    t_peers = [(dp, wrap(t + k, T)) for k in range(T)]

    inputs = [
        pltpu.make_async_copy(w_hbm, wg.at[z], in_s.at[0]),
        pltpu.make_async_copy(emb_hbm, emb_ref, in_s.at[1]),
        pltpu.make_async_copy(pw_hbm, pw_ref, in_s.at[2]),
        pltpu.make_async_copy(patches_hbm, patches_ref, in_s.at[3]),
    ]
    for copy in inputs:
        copy.start()

    barrier = pltpu.get_barrier_semaphore()
    greeted = x_peers[1:] + z_peers[1:] + t_peers[1:]
    for peer in greeted:
        pl.semaphore_signal(barrier, inc=1, device_id=peer, device_id_type=pl.DeviceIdType.MESH)

    inputs[0].wait()
    inputs[1].wait()
    live = live_ref[0]
    live_rows = lax.broadcasted_iota(jnp.int32, (G, NC), 0) < live
    for k in range(QUAD):
        block = emb_ref[:, k * NC:(k + 1) * NC]
        cot_own[k] = jnp.where(live_rows, block, jnp.zeros_like(block))

    pl.semaphore_wait(barrier, len(greeted))

    def rows_of(half):
        return pl.ds(half * 128, 128)

    for half in (0, 1):
        for k in (1, 3, 2):
            send(cot_own.at[ys[k], rows_of(half)], cot_p1.at[y, rows_of(half)],
                 p1_ss.at[k, half], p1_rs.at[y, half], y_peers[k])

    def w_part(index, half):
        return wg.at[index, pl.ds(half * HALF, HALF)]

    def w_fwd(step, piece):
        for way, to, block in ((0, right, wrap(z - step, Z)), (1, left, wrap(z + step, Z))):
            half = piece if way == 0 else 1 - piece
            part = w_part(block, half)
            if step:
                arrived(part, w_rs.at[way, step - 1, half])
            send(part, part, w_ss.at[way, step, half], w_rs.at[way, step, half], to)

    def w_finish():
        for way, block in ((0, wrap(z - 3, Z)), (1, wrap(z + 3, Z))):
            arrived(w_part(block, 1 - way), w_rs.at[way, 2, 1 - way])
        for way in (0, 1):
            arrived(w_part(wrap(z + 4, Z), way), w_rs.at[way, 3, way])

    w_fwd(0, 0)
    w_fwd(0, 1)
    cot_p1[y] = cot_own[y]

    inputs[2].wait()
    inputs[3].wait()
    for i in range(4):
        rows = pl.ds(i * 256, 256)
        product = dot(pw_ref[...], patches_ref[:, i * 256:(i + 1) * 256])
        product = jnp.transpose(jnp.concatenate([product, jnp.zeros((256 - FS, 256), F32)], axis=0))
        proj_s[0, rows] = product[:, :128]
        proj_s[1, rows] = product[:, 128:]

    parts = []
    for q in range(4):
        rows = pl.ds(q, G, stride=4)
        parts.append(jnp.concatenate([proj_s[0, rows, :], proj_s[1, rows, :]], axis=1)[:, :FS])
    projected = jnp.concatenate(parts, axis=1)

    first, second = group_rows(0), group_rows(4)

    def send_stats(index):
        mine = stats.at[index, t]
        for k in range(1, T):
            send(mine, mine, st_ss.at[index, k], st_rs.at[index, t], t_peers[k])

    def totals(index):
        for k in range(1, T):
            owner = wrap(t + k, T)
            arrived(stats.at[index, owner], st_rs.at[index, owner])
        total = stats[index, 0]
        for k in range(1, T):
            total = total + stats[index, k]
        return total / E

    def spread(rows, value):
        return dot(value, rows, ((0,), (0,)), HIGH)

    stats[0, t] = (
        dot(first, projected, ((1,), (1,)), HIGH)
        + dot(second, projected * projected, ((1,), (1,)), HIGH)
    )
    send_stats(0)
    def cot_over_x(half):
        for k in (1, 3, 2, 0):
            origin = xs[k]
            block = cot_p1.at[origin, rows_of(half)]

            @pl.when(origin != y)
            def _():
                arrived(block, p1_rs.at[origin, half])

            slot = cot_all.at[x, c * QUAD + y, rows_of(half)]
            if k:
                send(block, slot, p2_ss.at[k, half], p2_rs.at[x, half], x_peers[k])
            else:
                slot[...] = block[...]

    def cot_block(k, j):
        return cot_all.at[xs[k], c * QUAD + ys[j]]

    def to_sibling(k, j):
        block = cot_block(k, j)
        send(block, block, cs_ss.at[k, j], cs_rs.at[xs[k], ys[j]], sibling)

    def cot_out(k, half):
        part = cot_block(k, 0).at[rows_of(half)]
        if k:
            arrived(part, p2_rs.at[xs[k], half])
        for j in (1, 3):
            send(part, part, p3_ss.at[k, j, half], p3_rs.at[xs[k], y, half], y_peers[j])
        if half:
            to_sibling(k, 0)

    def cot_on(k):
        for half, j in ((0, 1), (1, 3)):
            part = cot_block(k, j).at[rows_of(half)]
            arrived(part, p3_rs.at[xs[k], ys[j], half])
            send(part, part, ph_ss.at[k, half], ph_rs.at[xs[k], half], y_peers[4 - j])
        for half, j in ((1, 1), (0, 3)):
            arrived(cot_block(k, j).at[rows_of(half)], p3_rs.at[xs[k], ys[j], half])
            to_sibling(k, j)

    def cot_far(k):
        for half in (0, 1):
            arrived(cot_block(k, 2).at[rows_of(half)], ph_rs.at[xs[k], half])
        to_sibling(k, 2)

    def cot_in(k):
        for j in range(Y):
            arrived(cot_all.at[xs[k], (1 - c) * QUAD + ys[j]], cs_rs.at[xs[k], ys[j]])

    cot_over_x(0)
    w_fwd(1, 0)
    cot_out(0, 0)
    cot_over_x(1)
    cot_out(0, 1)
    cot_out(1, 0)
    cot_out(3, 0)
    w_fwd(1, 1)

    means = totals(0)
    row = lax.broadcasted_iota(jnp.int32, (8, G), 0)
    row_mean = pltpu.roll(means, 4, 0)
    inv_scale = jnp.where(row >= 4, lax.rsqrt(
        jnp.where(row >= 4, means - row_mean * row_mean, 1.0) + 1e-05), 0.0)
    inv_wide = spread(second, inv_scale)
    normed = (projected - spread(first, means)) * inv_wide
    normed_s[0] = normed
    normed_s[1] = inv_wide
    merged_all[x] = normed.astype(BF16)
    for k in range(1, X):
        send(merged_all.at[x], merged_all.at[x], m_ss.at[k], m_rs.at[x], x_peers[k])

    cot_out(2, 0)
    cot_out(1, 1)
    cot_out(3, 1)
    w_fwd(2, 0)
    cot_on(0)
    cot_out(2, 1)
    w_fwd(2, 1)
    merged_t[:, pl.ds(x * G, G)] = jnp.transpose(merged_all[x])
    cot_far(0)
    w_fwd(3, 0)
    cot_on(1)
    cot_on(3)
    cot_far(1)
    cot_on(2)
    cot_far(3)
    w_finish()
    for k in (3, 1, 2):
        arrived(merged_all.at[xs[k]], m_rs.at[xs[k]])

    for n in range(X):
        rows = merged_all[xs[(n + 1) % X]]
        for m in range(QUAD):
            block = wg[(1 - c) * QUAD + ys[(m + 1) % Y]]
            e_sib_send[n, m] = dot(rows, block).astype(BF16)
        send(e_sib_send.at[n], e_sib_recv.at[n], es_ss.at[n], es_rs.at[n], sibling)

    cot_far(2)
    for k in (0, 1, 3, 2):
        cot_in(k)

    def d_term(owner):
        total = None
        for block in range(Z):
            term = dot(cot_all[owner, block], wg[block], ((1,), (1,)))
            total = term if total is None else total + term
        return total

    def d_sums(term, owner):
        rounded = term.astype(BF16)
        product = (term * merged_all[owner].astype(F32)).astype(BF16)
        return (dot(first.astype(BF16), rounded, ((1,), (1,)))
                + dot(second.astype(BF16), product, ((1,), (1,))))

    def d_near(way, half, to):
        slot = 1 if way == 0 else 3
        part = pl.ds(half * 128, 128)
        send(d_send_buf.at[slot, part], d_recv_buf.at[way, part], d_ss.at[way, half],
             d_rs.at[way, half], to)

    for k, to in ((2, None), (1, x_peers[1]), (3, x_peers[3])):
        term = d_term(xs[k])
        d_send_buf[k] = term.astype(BF16)
        sx_send[k] = d_sums(term, xs[k])
        send(sx_send.at[k], sx_recv.at[x], sx_ss.at[k], sx_rs.at[x], x_peers[k])
        if k == 2:
            for way, peer in ((0, x_peers[1]), (1, x_peers[3])):
                send(d_send_buf.at[2, rows_of(way)], d_far.at[way], df_ss.at[way],
                     df_rs.at[way], peer)
        else:
            way = 0 if k == 1 else 1
            d_keep[way] = term[way * 128:(way + 1) * 128]
            d_near(way, 1 - way, to)

    def d_combine():
        for way, slot, to in ((0, 1, x_peers[1]), (1, 3, x_peers[3])):
            arrived(d_far.at[way], df_rs.at[way])
            d_send_buf[slot, rows_of(way)] = (d_keep[way] + d_far[way].astype(F32)).astype(BF16)
            d_near(way, way, to)

    def e_out(n):
        rows = merged_all[xs[(n + 1) % X]]
        arrived(e_sib_recv.at[n], es_rs.at[n])
        for m in (1, 0, 2, 3):
            value = dot(rows, wg[c * QUAD + ys[(m + 1) % Y]]) + e_sib_recv[n, m].astype(F32)
            e_send[n, m] = value.astype(BF16)
            if m == 1:
                for way, peer in ((0, y_peers[1]), (1, y_peers[3])):
                    send(e_send.at[n, 1, rows_of(way)], e_far.at[n, way], ef_ss.at[n, way],
                         ef_rs.at[n, way], peer)
            elif m < QUAD - 1:
                e_near(n, 0 if m == 0 else 1, 1 if m == 0 else 0)

    def e_near(n, way, half):
        slot, peer = (0, y_peers[1]) if way == 0 else (2, y_peers[3])
        send(e_send.at[n, slot, rows_of(half)], e_recv.at[n, way, rows_of(half)],
             ey_ss.at[n, way, half], ey_rs.at[n, way, half], peer)

    def e_combine(n):
        for way, slot in ((0, 0), (1, 2)):
            arrived(e_far.at[n, way], ef_rs.at[n, way])
            part = e_send.at[n, slot, rows_of(way)]
            part[...] = (part[...].astype(F32) + e_far[n, way].astype(F32)).astype(BF16)
            e_near(n, way, way)

    def e_sum_up(n):
        total = e_send[n, QUAD - 1].astype(F32)
        for way in (0, 1):
            for half in (1 - way, way):
                arrived(e_recv.at[n, way, rows_of(half)], ey_rs.at[n, way, half])
            total = total + e_recv[n, way].astype(F32)
        total = total.astype(BF16)
        if n < X - 1:
            e_sum[n] = total
            send(e_sum.at[n], e_p2.at[x], e2_ss.at[n], e2_rs.at[x], x_peers[n + 1])
        else:
            e_p2[x] = total

    def e_home(k):
        origin = xs[k]
        block = e_p2.at[origin]
        if k:
            arrived(block, e2_rs.at[origin])

        @pl.when(origin == y)
        def _():
            e_fin[y] = block[...]

        @pl.when(origin != y)
        def _():
            pltpu.make_async_remote_copy(
                src_ref=block, dst_ref=e_fin.at[y], send_sem=e1_ss.at[k], recv_sem=e1_rs.at[y],
                device_id=device(x, origin, z, c), device_id_type=pl.DeviceIdType.MESH,
            ).start()

    e_out(0)
    for k in range(1, X):
        merged_t[:, pl.ds(xs[k] * G, G)] = jnp.transpose(merged_all[xs[k]])

    def merge_term(block, rows=slice(None)):
        return dot(merged_t[rows], cot_all[:, block].reshape(X * G, NC))

    def g_block(way, step):
        return wrap(z + 4 - step, Z) if way == 0 else wrap(z - 4 + step, Z)

    def g_out(way, step, half, value):
        g_send_buf[way, step, half] = value.astype(BF16)
        send(g_send_buf.at[way, step, half], g_recv_buf.at[way, step, half],
             g_ss.at[way, step, half], g_rs.at[way, step, half], right if way == 0 else left)

    def g_in(way, step, half):
        arrived(g_recv_buf.at[way, step, half], g_rs.at[way, step, half])
        return g_recv_buf[way, step, half].astype(F32)

    def half_rows(half):
        return slice(half * HALF, (half + 1) * HALF)

    for way in (0, 1):
        g_out(way, 0, way, merge_term(g_block(way, 0), half_rows(way)))
    for way in (0, 1):
        g_out(way, 1, 1 - way, merge_term(g_block(way, 1), half_rows(1 - way)))

    def g_piece(step, piece):
        for way in (0, 1):
            half = 1 - way if piece == 0 else way
            term = merge_term(g_block(way, step), half_rows(half))
            g_out(way, step, half, term + g_in(way, step - 1, half))

    d_combine()
    term = d_term(x)
    d_own[...] = term
    total = d_sums(term, x)
    for k in range(1, X):
        arrived(sx_recv.at[xs[k]], sx_rs.at[xs[k]])
        total = total + sx_recv[xs[k]]
    stats[1, t] = total
    send_stats(1)
    e_combine(0)
    e_out(1)
    g_piece(1, 1)
    e_out(2)
    e_out(3)
    e_combine(1)
    g_piece(2, 0)
    e_combine(2)

    means = totals(1)
    d_mean = spread(first, means)
    dn_mean = spread(second, means)
    dnormed = d_own[...]
    for way in (0, 1):
        for half in (1 - way, way):
            arrived(d_recv_buf.at[way, rows_of(half)], d_rs.at[way, half])
        dnormed = dnormed + d_recv_buf[way].astype(F32)
    e_combine(3)
    grad_input = (dnormed - d_mean - normed_s[0] * dn_mean) * normed_s[1]
    for q in range(4):
        part = grad_input[:, q * FS:(q + 1) * FS]
        part = jnp.concatenate([part, jnp.zeros((G, 256 - FS), F32)], axis=1)
        rows = pl.ds(q, G, stride=4)
        proj_s[0, rows, :] = part[:, :128]
        proj_s[1, rows, :] = part[:, 128:]
    grad_rows = jnp.concatenate([proj_s[0], proj_s[1]], axis=1)
    grad_rows = jnp.transpose(grad_rows)[:FS].astype(BF16)

    for chunk in (0, 1):
        low, high = 640 * chunk, min(640 * (chunk + 1), PD)
        if chunk:
            t_s[chunk, :, 512:] = jnp.zeros((FS, 128), BF16)
        t_s[chunk, :, :high - low] = dot(
            grad_rows, patches_ref[low:high], ((1,), (1,))).astype(BF16)
        for p in range(50):
            i, j = p % 10, p // 10
            a_own[chunk, p // 13, p % 13] = t_s[chunk, 16 * i:16 * (i + 1), 128 * j:128 * (j + 1)]
        for p in range(50, 52):
            a_own[chunk, p // 13, p % 13] = jnp.zeros((16, 128), BF16)
        for k in (1, 3, 2):
            send(a_own.at[chunk, xs[k]], a_xr.at[chunk, x], ax_ss.at[chunk, k],
                 ax_rs.at[chunk, x], x_peers[k])

    def over_z(chunk):
        total = a_own[chunk, x].astype(F32)
        for k in (3, 1, 2):
            arrived(a_xr.at[chunk, xs[k]], ax_rs.at[chunk, xs[k]])
            total = total + a_xr[chunk, xs[k]].astype(F32)
        a_x[chunk, pl.ds(0, 13)] = total.astype(BF16)
        a_x[chunk, pl.ds(13, 3)] = jnp.zeros((3, 16, 128), BF16)
        for k in (1, 7, 2, 6, 3, 5, 4):
            send(a_x.at[chunk, pl.ds(2 * zs[k], 2)], a_zr.at[chunk, z], az_ss.at[chunk, k],
                 az_rs.at[chunk, z], z_peers[k])

    def back_over_z(chunk):
        total = a_x[chunk, pl.ds(2 * z, 2)].astype(F32)
        for k in range(1, Z):
            arrived(a_zr.at[chunk, zs[k]], az_rs.at[chunk, zs[k]])
            total = total + a_zr[chunk, zs[k]].astype(F32)
        mine = a_all.at[chunk, x, pl.ds(2 * z, 2)]
        mine[...] = total.astype(BF16)
        for k in (1, 7, 2, 6, 3, 5, 4):
            send(mine, mine, bz_ss.at[chunk, k], bz_rs.at[chunk, z], z_peers[k])

    def back_over_x(chunk):
        for k in range(1, Z):
            arrived(a_all.at[chunk, x, pl.ds(2 * zs[k], 2)], bz_rs.at[chunk, zs[k]])
        mine = a_all.at[chunk, x, pl.ds(0, 13)]
        for k in (1, 3, 2):
            send(mine, mine, bx_ss.at[chunk, k], bx_rs.at[chunk, x], x_peers[k])

    outputs = []

    def g_finish():
        term = merge_term(z)
        for half in (0, 1):
            gm_ref[pl.ds(half * HALF, HALF)] = (
                term[half_rows(half)] + g_in(0, 3, half) + g_in(1, 3, half))
        outputs.append(pltpu.make_async_copy(gm_ref, gm_hbm, out_s.at[0]))
        outputs[0].start()

    g_piece(2, 1)
    e_sum_up(0)
    g_piece(3, 0)
    e_sum_up(1)
    over_z(0)
    e_sum_up(2)
    e_sum_up(3)
    e_home(0)
    over_z(1)
    g_piece(3, 1)
    e_home(3)
    e_home(2)
    back_over_z(0)
    e_home(1)
    back_over_z(1)
    g_finish()
    back_over_x(0)
    back_over_x(1)

    for k in range(1, Y):
        arrived(e_fin.at[ys[k]], e1_rs.at[ys[k]])
    for k in range(QUAD):
        block = e_fin[k]
        embeds_ref[:, k * NC:(k + 1) * NC] = jnp.where(live_rows, block, jnp.zeros_like(block))
    outputs.append(pltpu.make_async_copy(embeds_ref, embeds_hbm, out_s.at[1]))
    outputs[1].start()

    for chunk in (0, 1):
        for k in range(1, X):
            arrived(a_all.at[chunk, xs[k], pl.ds(0, 13)], bx_rs.at[chunk, xs[k]])
        for p in range(50):
            i, j = p % 10, 5 * chunk + p // 10
            rows = slice(16 * i, 16 * (i + 1))
            tile = a_all[chunk, p // 13, p % 13].astype(F32)
            if j < 9:
                gp_ref[rows, 128 * j:128 * (j + 1)] = tile
            else:
                gp_ref[rows, 1152:] = tile[:, :PD - 1152]
    outputs.append(pltpu.make_async_copy(gp_ref, gp_hbm, out_s.at[2]))
    outputs[2].start()

    for k in range(X):
        @pl.when(xs[k] != y)
        def _():
            pltpu.make_async_remote_copy(
                src_ref=e_p2.at[xs[k]], dst_ref=e_fin.at[y], send_sem=e1_ss.at[k],
                recv_sem=e1_rs.at[y], device_id=device(x, xs[k], z, c),
                device_id_type=pl.DeviceIdType.MESH,
            ).wait_send()
    for copy in outputs:
        copy.wait()
    for copy in started:
        copy.wait_send()


def finish(embeds_in, gm_in, gp_in, embeds_out, gm_out, gp_out, embeds_s, gm_s, gp_s, sems):
    parts = []
    for i, (src, held, dst, rows) in enumerate((
        (embeds_in, embeds_s, embeds_out, G), (gm_in, gm_s, gm_out, K), (gp_in, gp_s, gp_out, FS)
    )):
        for half in (0, 1):
            part = pl.ds(half * rows // 2, rows // 2)
            parts.append((
                pltpu.make_async_copy(src.at[part], held.at[part], sems.at[0, i, half]),
                pltpu.make_async_copy(held.at[part], dst.at[part], sems.at[1, i, half]),
            ))
    for load, _ in parts:
        load.start()
    for load, store in parts:
        load.wait()
        store.start()
    for _, store in parts:
        store.wait()


def body(patches, rank_groups, patch_weight, merge_weight, emb_grad):
    dma = pltpu.SemaphoreType.DMA
    rows = 4 * G
    scratch = [
        pltpu.VMEM((G, QUAD * NC), BF16),
        pltpu.VMEM((K, NC), F32),
        pltpu.VMEM((FS, PD), F32),
        pltpu.VMEM((PD, rows), BF16),
        pltpu.VMEM((FS, PD), BF16),
        pltpu.VMEM((G, QUAD * NC), BF16),
        pltpu.VMEM((Z, K, NC), BF16),
        pltpu.VMEM((QUAD, G, NC), BF16),
        pltpu.VMEM((Y, G, NC), BF16),
        pltpu.VMEM((X, Z, G, NC), BF16),
        pltpu.VMEM((X, G, K), BF16),
        pltpu.VMEM((K, X * G), BF16),
        pltpu.VMEM((2, rows, 128), F32),
        pltpu.VMEM((2, G, K), F32),
        pltpu.VMEM((2, T, 8, G), F32),
        pltpu.VMEM((X, 8, G), F32),
        pltpu.VMEM((X, 8, G), F32),
        pltpu.VMEM((2, 4, 2, HALF, NC), BF16),
        pltpu.VMEM((2, 4, 2, HALF, NC), BF16),
        pltpu.VMEM((X, G, K), BF16),
        pltpu.VMEM((2, 128, K), F32),
        pltpu.VMEM((2, 128, K), BF16),
        pltpu.VMEM((G, K), F32),
        pltpu.VMEM((2, G, K), BF16),
        pltpu.VMEM((X, QUAD, G, NC), BF16),
        pltpu.VMEM((X, QUAD, G, NC), BF16),
        pltpu.VMEM((X, QUAD, G, NC), BF16),
        pltpu.VMEM((X, 2, 128, NC), BF16),
        pltpu.VMEM((X, 2, G, NC), BF16),
        pltpu.VMEM((X, G, NC), BF16),
        pltpu.VMEM((X, G, NC), BF16),
        pltpu.VMEM((QUAD, G, NC), BF16),
        pltpu.VMEM((2, FS, 640), BF16),
        pltpu.VMEM((2, X, 13, 16, 128), BF16),
        pltpu.VMEM((2, X, 13, 16, 128), BF16),
        pltpu.VMEM((2, 16, 16, 128), BF16),
        pltpu.VMEM((2, Z, 2, 16, 128), BF16),
        pltpu.VMEM((2, X, 16, 16, 128), BF16),
        dma((4,)),
        dma((3,)),
    ]
    for shape in (
        (2, 4, 2), (4, 2), (4, 2), (4, 4, 2), (4, 2), (4, 4), (2, 8), (4,), (4,),
        (2, 2), (2,), (2, 4, 2), (4,), (4, 2), (4, 2, 2), (4,), (4,), (2, 4), (2, 8), (2, 8), (2, 4),
    ):
        scratch += [dma(shape), dma(shape)]
    results = (
        jax.ShapeDtypeStruct((G, QUAD * NC), BF16),
        jax.ShapeDtypeStruct((K, NC), F32),
        jax.ShapeDtypeStruct((FS, PD), F32),
    )
    hbm = pl.BlockSpec(memory_space=pl.ANY)
    partial = pl.pallas_call(
        kernel,
        out_shape=results,
        in_specs=[pl.BlockSpec(memory_space=pltpu.SMEM)] + [hbm] * 4,
        out_specs=(hbm, hbm, hbm),
        scratch_shapes=scratch,
        compiler_params=pltpu.CompilerParams(
            collective_id=0, has_side_effects=True, vmem_limit_bytes=56 * 2**20
        ),
        name="tower",
    )(rank_groups, patches.T, patch_weight.T, merge_weight.reshape(K, NC), emb_grad)
    embeds, grad_merge, grad_patch = pl.pallas_call(
        finish,
        out_shape=results,
        in_specs=[hbm, hbm, hbm],
        out_specs=(hbm, hbm, hbm),
        scratch_shapes=[
            pltpu.VMEM((G, QUAD * NC), BF16),
            pltpu.VMEM((K, NC), F32),
            pltpu.VMEM((FS, PD), F32),
            dma((2, 3, 2)),
        ],
        name="finish",
    )(*partial)
    return embeds, grad_merge.reshape(4, FS, NC), grad_patch.T


def solution(mesh):
    return jax.shard_map(
        body,
        mesh=mesh,
        in_specs=(
            P("dp", None),
            P("dp"),
            P(None, "tensor"),
            P(None, "tensor", "dp"),
            P("dp", "tensor"),
        ),
        out_specs=(P("dp", "tensor"), P(None, "tensor", "dp"), P(None, "tensor")),
        check_vma=False,
    )
```

```python
import functools

import jax
import jax.numpy as jnp
from jax import lax
from jax.experimental import pallas as pl
from jax.experimental.pallas import tpu as pltpu
from jax.sharding import PartitionSpec as P

E = 1280
X, Y, Z = 4, 4, 8
T = 2 * Y
F32, BF16 = jnp.float32, jnp.bfloat16
HIGH = lax.Precision.HIGHEST

PD = 1176
FS = E // T
K = 4 * FS
G = 256
NC = 256
HALF = K // 2
QUAD = Z // 2


def dot(a, b, dims=((1,), (0,)), precision=None):
    return lax.dot_general(a, b, (dims, ((), ())), precision=precision, preferred_element_type=F32)


def wrap(value, count):
    return lax.rem(value + count, count)


def group_rows(offset):
    row = lax.broadcasted_iota(jnp.int32, (8, K), 0)
    lane = lax.broadcasted_iota(jnp.int32, (8, K), 1)
    low = (row - offset) * FS
    return jnp.where((lane >= low) & (lane < low + FS), 1.0, 0.0).astype(F32)


def kernel(
    live_ref, patches_hbm, pw_hbm, w_hbm, emb_hbm,
    embeds_hbm, gm_hbm, gp_hbm,
    embeds_ref, gm_ref, gp_ref,
    patches_ref, pw_ref, emb_ref,
    wg, cot_own, cot_p1, cot_all, merged_all, merged_t, proj_s, normed_s,
    stats, sx_send, sx_recv, g_send_buf, g_recv_buf,
    d_send_buf, d_keep, d_far, d_own, d_recv_buf,
    e_sib_send, e_sib_recv, e_send, e_far, e_recv, e_sum, e_p2, e_fin,
    t_s, a_own, a_xr, a_x, a_zr, a_all,
    in_s, out_s,
    w_ss, w_rs, p1_ss, p1_rs, p2_ss, p2_rs, p3_ss, p3_rs, ph_ss, ph_rs, cs_ss, cs_rs,
    st_ss, st_rs, sx_ss, sx_rs, m_ss, m_rs,
    d_ss, d_rs, df_ss, df_rs, g_ss, g_rs, es_ss, es_rs, ef_ss, ef_rs, ey_ss, ey_rs, e2_ss, e2_rs, e1_ss, e1_rs,
    ax_ss, ax_rs, az_ss, az_rs, bz_ss, bz_rs, bx_ss, bx_rs,
):
    dp = lax.axis_index("dp")
    t = lax.axis_index("tensor")
    x, z = lax.div(dp, Z), lax.rem(dp, Z)
    y, c = lax.div(t, 2), lax.rem(t, 2)

    def device(x, y, z, c):
        return (x * Z + z, y * 2 + c)

    started = []

    def send(src, dst, ssem, rsem, to):
        copy = pltpu.make_async_remote_copy(
            src_ref=src, dst_ref=dst, send_sem=ssem, recv_sem=rsem,
            device_id=to, device_id_type=pl.DeviceIdType.MESH,
        )
        copy.start()
        started.append(copy)

    def arrived(dst, rsem):
        pltpu.make_async_remote_copy(
            src_ref=dst, dst_ref=dst, send_sem=w_ss.at[0, 0, 0], recv_sem=rsem,
            device_id=sibling, device_id_type=pl.DeviceIdType.MESH,
        ).wait_recv()

    right = device(x, y, wrap(z + 1, Z), c)
    left = device(x, y, wrap(z - 1, Z), c)
    sibling = device(x, y, z, 1 - c)
    xs = [wrap(x + k, X) for k in range(X)]
    ys = [wrap(y + k, Y) for k in range(Y)]
    zs = [wrap(z + k, Z) for k in range(Z)]
    x_peers = [device(i, y, z, c) for i in xs]
    y_peers = [device(x, i, z, c) for i in ys]
    z_peers = [device(x, y, i, c) for i in zs]
    t_peers = [(dp, wrap(t + k, T)) for k in range(T)]

    inputs = [
        pltpu.make_async_copy(w_hbm, wg.at[z], in_s.at[0]),
        pltpu.make_async_copy(emb_hbm, emb_ref, in_s.at[1]),
        pltpu.make_async_copy(pw_hbm, pw_ref, in_s.at[2]),
        pltpu.make_async_copy(patches_hbm, patches_ref, in_s.at[3]),
    ]
    for copy in inputs:
        copy.start()

    barrier = pltpu.get_barrier_semaphore()
    greeted = x_peers[1:] + z_peers[1:] + t_peers[1:]
    for peer in greeted:
        pl.semaphore_signal(barrier, inc=1, device_id=peer, device_id_type=pl.DeviceIdType.MESH)

    inputs[0].wait()
    inputs[1].wait()
    live = live_ref[0]
    live_rows = lax.broadcasted_iota(jnp.int32, (G, NC), 0) < live
    for k in range(QUAD):
        block = emb_ref[:, k * NC:(k + 1) * NC]
        cot_own[k] = jnp.where(live_rows, block, jnp.zeros_like(block))

    pl.semaphore_wait(barrier, len(greeted))

    def rows_of(half):
        return pl.ds(half * 128, 128)

    for half in (0, 1):
        for k in (1, 3, 2):
            send(cot_own.at[ys[k], rows_of(half)], cot_p1.at[y, rows_of(half)],
                 p1_ss.at[k, half], p1_rs.at[y, half], y_peers[k])

    def w_part(index, half):
        return wg.at[index, pl.ds(half * HALF, HALF)]

    def w_fwd(step, piece):
        for way, to, block in ((0, right, wrap(z - step, Z)), (1, left, wrap(z + step, Z))):
            half = piece if way == 0 else 1 - piece
            part = w_part(block, half)
            if step:
                arrived(part, w_rs.at[way, step - 1, half])
            send(part, part, w_ss.at[way, step, half], w_rs.at[way, step, half], to)

    def w_finish():
        for way, block in ((0, wrap(z - 3, Z)), (1, wrap(z + 3, Z))):
            arrived(w_part(block, 1 - way), w_rs.at[way, 2, 1 - way])
        for way in (0, 1):
            arrived(w_part(wrap(z + 4, Z), way), w_rs.at[way, 3, way])

    w_fwd(0, 0)
    w_fwd(0, 1)
    cot_p1[y] = cot_own[y]

    inputs[2].wait()
    inputs[3].wait()
    for i in range(4):
        rows = pl.ds(i * 256, 256)
        product = dot(pw_ref[...], patches_ref[:, i * 256:(i + 1) * 256])
        product = jnp.transpose(jnp.concatenate([product, jnp.zeros((256 - FS, 256), F32)], axis=0))
        proj_s[0, rows] = product[:, :128]
        proj_s[1, rows] = product[:, 128:]

    parts = []
    for q in range(4):
        rows = pl.ds(q, G, stride=4)
        parts.append(jnp.concatenate([proj_s[0, rows, :], proj_s[1, rows, :]], axis=1)[:, :FS])
    projected = jnp.concatenate(parts, axis=1)

    first, second = group_rows(0), group_rows(4)

    def send_stats(index):
        mine = stats.at[index, t]
        for k in range(1, T):
            send(mine, mine, st_ss.at[index, k], st_rs.at[index, t], t_peers[k])

    def totals(index):
        for k in range(1, T):
            owner = wrap(t + k, T)
            arrived(stats.at[index, owner], st_rs.at[index, owner])
        total = stats[index, 0]
        for k in range(1, T):
            total = total + stats[index, k]
        return total / E

    def spread(rows, value):
        return dot(value, rows, ((0,), (0,)), HIGH)

    stats[0, t] = (
        dot(first, projected, ((1,), (1,)), HIGH)
        + dot(second, projected * projected, ((1,), (1,)), HIGH)
    )
    send_stats(0)
    def cot_over_x(half):
        for k in (1, 3, 2, 0):
            origin = xs[k]
            block = cot_p1.at[origin, rows_of(half)]

            @pl.when(origin != y)
            def _():
                arrived(block, p1_rs.at[origin, half])

            slot = cot_all.at[x, c * QUAD + y, rows_of(half)]
            if k:
                send(block, slot, p2_ss.at[k, half], p2_rs.at[x, half], x_peers[k])
            else:
                slot[...] = block[...]

    def cot_block(k, j):
        return cot_all.at[xs[k], c * QUAD + ys[j]]

    def to_sibling(k, j):
        block = cot_block(k, j)
        send(block, block, cs_ss.at[k, j], cs_rs.at[xs[k], ys[j]], sibling)

    def cot_out(k, half):
        part = cot_block(k, 0).at[rows_of(half)]
        if k:
            arrived(part, p2_rs.at[xs[k], half])
        for j in (1, 3):
            send(part, part, p3_ss.at[k, j, half], p3_rs.at[xs[k], y, half], y_peers[j])
        if half:
            to_sibling(k, 0)

    def cot_on(k):
        for half, j in ((0, 1), (1, 3)):
            part = cot_block(k, j).at[rows_of(half)]
            arrived(part, p3_rs.at[xs[k], ys[j], half])
            send(part, part, ph_ss.at[k, half], ph_rs.at[xs[k], half], y_peers[4 - j])
        for half, j in ((1, 1), (0, 3)):
            arrived(cot_block(k, j).at[rows_of(half)], p3_rs.at[xs[k], ys[j], half])
            to_sibling(k, j)

    def cot_far(k):
        for half in (0, 1):
            arrived(cot_block(k, 2).at[rows_of(half)], ph_rs.at[xs[k], half])
        to_sibling(k, 2)

    def cot_in(k):
        for j in range(Y):
            arrived(cot_all.at[xs[k], (1 - c) * QUAD + ys[j]], cs_rs.at[xs[k], ys[j]])

    cot_over_x(0)
    w_fwd(1, 0)
    cot_out(0, 0)
    cot_over_x(1)
    cot_out(0, 1)
    cot_out(1, 0)
    cot_out(3, 0)
    w_fwd(1, 1)

    means = totals(0)
    row = lax.broadcasted_iota(jnp.int32, (8, G), 0)
    row_mean = pltpu.roll(means, 4, 0)
    inv_scale = jnp.where(row >= 4, lax.rsqrt(
        jnp.where(row >= 4, means - row_mean * row_mean, 1.0) + 1e-05), 0.0)
    inv_wide = spread(second, inv_scale)
    normed = (projected - spread(first, means)) * inv_wide
    normed_s[0] = normed
    normed_s[1] = inv_wide
    merged_all[x] = normed.astype(BF16)
    for k in range(1, X):
        send(merged_all.at[x], merged_all.at[x], m_ss.at[k], m_rs.at[x], x_peers[k])

    cot_out(2, 0)
    cot_out(1, 1)
    cot_out(3, 1)
    w_fwd(2, 0)
    cot_on(0)
    cot_out(2, 1)
    w_fwd(2, 1)
    merged_t[:, pl.ds(x * G, G)] = jnp.transpose(merged_all[x])
    cot_far(0)
    w_fwd(3, 0)
    cot_on(1)
    cot_on(3)
    cot_far(1)
    cot_on(2)
    cot_far(3)
    w_finish()
    for k in (3, 1, 2):
        arrived(merged_all.at[xs[k]], m_rs.at[xs[k]])

    for n in range(X):
        rows = merged_all[xs[(n + 1) % X]]
        for m in range(QUAD):
            block = wg[(1 - c) * QUAD + ys[(m + 1) % Y]]
            e_sib_send[n, m] = dot(rows, block).astype(BF16)
        send(e_sib_send.at[n], e_sib_recv.at[n], es_ss.at[n], es_rs.at[n], sibling)

    cot_far(2)
    for k in (0, 1, 3, 2):
        cot_in(k)

    def d_term(owner):
        total = None
        for block in range(Z):
            term = dot(cot_all[owner, block], wg[block], ((1,), (1,)))
            total = term if total is None else total + term
        return total

    def d_sums(term, owner):
        rounded = term.astype(BF16)
        product = (term * merged_all[owner].astype(F32)).astype(BF16)
        return (dot(first.astype(BF16), rounded, ((1,), (1,)))
                + dot(second.astype(BF16), product, ((1,), (1,))))

    def d_near(way, half, to):
        slot = 1 if way == 0 else 3
        part = pl.ds(half * 128, 128)
        send(d_send_buf.at[slot, part], d_recv_buf.at[way, part], d_ss.at[way, half],
             d_rs.at[way, half], to)

    def d_out(k):
        term = d_term(xs[k])
        d_send_buf[k] = term.astype(BF16)
        sx_send[k] = d_sums(term, xs[k])
        send(sx_send.at[k], sx_recv.at[x], sx_ss.at[k], sx_rs.at[x], x_peers[k])
        if k == 2:
            for way, peer in ((0, x_peers[1]), (1, x_peers[3])):
                send(d_send_buf.at[2, rows_of(way)], d_far.at[way], df_ss.at[way],
                     df_rs.at[way], peer)
        else:
            way = 0 if k == 1 else 1
            d_keep[way] = term[way * 128:(way + 1) * 128]
            d_near(way, 1 - way, x_peers[k])

    def d_combine():
        for way, slot, to in ((0, 1, x_peers[1]), (1, 3, x_peers[3])):
            arrived(d_far.at[way], df_rs.at[way])
            d_send_buf[slot, rows_of(way)] = (d_keep[way] + d_far[way].astype(F32)).astype(BF16)
            d_near(way, way, to)

    def e_term(n, m):
        value = dot(merged_all[xs[(n + 1) % X]], wg[c * QUAD + ys[(m + 1) % Y]])
        e_send[n, m] = (value + e_sib_recv[n, m].astype(F32)).astype(BF16)

    def e_far_out(n):
        arrived(e_sib_recv.at[n], es_rs.at[n])
        e_term(n, 1)
        for way, peer in ((0, y_peers[1]), (1, y_peers[3])):
            send(e_send.at[n, 1, rows_of(way)], e_far.at[n, way], ef_ss.at[n, way],
                 ef_rs.at[n, way], peer)

    def e_near_out(n):
        e_term(n, 0)
        e_near(n, 0, 1)
        e_term(n, 2)
        e_near(n, 1, 0)
        e_term(n, 3)

    def e_near(n, way, half):
        slot, peer = (0, y_peers[1]) if way == 0 else (2, y_peers[3])
        send(e_send.at[n, slot, rows_of(half)], e_recv.at[n, way, rows_of(half)],
             ey_ss.at[n, way, half], ey_rs.at[n, way, half], peer)

    def e_combine(n):
        for way, slot in ((0, 0), (1, 2)):
            arrived(e_far.at[n, way], ef_rs.at[n, way])
            part = e_send.at[n, slot, rows_of(way)]
            part[...] = (part[...].astype(F32) + e_far[n, way].astype(F32)).astype(BF16)
            e_near(n, way, way)

    def e_sum_up(n):
        total = e_send[n, QUAD - 1].astype(F32)
        for way in (0, 1):
            for half in (1 - way, way):
                arrived(e_recv.at[n, way, rows_of(half)], ey_rs.at[n, way, half])
            total = total + e_recv[n, way].astype(F32)
        total = total.astype(BF16)
        if n < X - 1:
            e_sum[n] = total
            send(e_sum.at[n], e_p2.at[x], e2_ss.at[n], e2_rs.at[x], x_peers[n + 1])
        else:
            e_p2[x] = total

    def e_home(k):
        origin = ys[k]
        block = e_p2.at[origin]

        @pl.when(origin != x)
        def _():
            arrived(block, e2_rs.at[origin])

        if k:
            send(block, e_fin.at[y], e1_ss.at[k], e1_rs.at[y], y_peers[k])
        else:
            e_fin[y] = block[...]

    d_out(2)
    for k in range(1, X):
        merged_t[:, pl.ds(xs[k] * G, G)] = jnp.transpose(merged_all[xs[k]])

    def merge_term(block, rows=slice(None)):
        return dot(merged_t[rows], cot_all[:, block].reshape(X * G, NC))

    def g_block(way, step):
        return wrap(z + 4 - step, Z) if way == 0 else wrap(z - 4 + step, Z)

    def g_out(way, step, half, value):
        g_send_buf[way, step, half] = value.astype(BF16)
        send(g_send_buf.at[way, step, half], g_recv_buf.at[way, step, half],
             g_ss.at[way, step, half], g_rs.at[way, step, half], right if way == 0 else left)

    def g_in(way, step, half):
        arrived(g_recv_buf.at[way, step, half], g_rs.at[way, step, half])
        return g_recv_buf[way, step, half].astype(F32)

    def half_rows(half):
        return slice(half * HALF, (half + 1) * HALF)

    for way in (0, 1):
        g_out(way, 0, way, merge_term(g_block(way, 0), half_rows(way)))
    for way in (0, 1):
        g_out(way, 1, 1 - way, merge_term(g_block(way, 1), half_rows(1 - way)))

    def g_piece(step, piece):
        for way in (0, 1):
            half = 1 - way if piece == 0 else way
            term = merge_term(g_block(way, step), half_rows(half))
            g_out(way, step, half, term + g_in(way, step - 1, half))

    e_far_out(0)
    e_near_out(0)
    d_out(1)
    d_out(3)
    term = d_term(x)
    d_own[...] = term
    total = d_sums(term, x)
    d_combine()
    for k in range(1, X):
        arrived(sx_recv.at[xs[k]], sx_rs.at[xs[k]])
        total = total + sx_recv[xs[k]]
    stats[1, t] = total
    send_stats(1)
    g_piece(1, 1)
    for n in (1, 2, 3):
        e_far_out(n)
    e_combine(0)
    for n in (1, 2, 3):
        e_near_out(n)
    g_piece(2, 0)
    for n in (1, 2, 3):
        e_combine(n)

    means = totals(1)
    d_mean = spread(first, means)
    dn_mean = spread(second, means)
    dnormed = d_own[...]
    for way in (0, 1):
        for half in (1 - way, way):
            arrived(d_recv_buf.at[way, rows_of(half)], d_rs.at[way, half])
        dnormed = dnormed + d_recv_buf[way].astype(F32)
    grad_input = (dnormed - d_mean - normed_s[0] * dn_mean) * normed_s[1]
    for q in range(4):
        part = grad_input[:, q * FS:(q + 1) * FS]
        part = jnp.concatenate([part, jnp.zeros((G, 256 - FS), F32)], axis=1)
        rows = pl.ds(q, G, stride=4)
        proj_s[0, rows, :] = part[:, :128]
        proj_s[1, rows, :] = part[:, 128:]
    grad_rows = jnp.concatenate([proj_s[0], proj_s[1]], axis=1)
    grad_rows = jnp.transpose(grad_rows)[:FS].astype(BF16)

    for chunk in (0, 1):
        low, high = 640 * chunk, min(640 * (chunk + 1), PD)
        if chunk:
            t_s[chunk, :, 512:] = jnp.zeros((FS, 128), BF16)
        t_s[chunk, :, :high - low] = dot(
            grad_rows, patches_ref[low:high], ((1,), (1,))).astype(BF16)
        for p in range(50):
            i, j = p % 10, p // 10
            a_own[chunk, p // 13, p % 13] = t_s[chunk, 16 * i:16 * (i + 1), 128 * j:128 * (j + 1)]
        for p in range(50, 52):
            a_own[chunk, p // 13, p % 13] = jnp.zeros((16, 128), BF16)
        for k in (1, 3, 2):
            send(a_own.at[chunk, xs[k]], a_xr.at[chunk, x], ax_ss.at[chunk, k],
                 ax_rs.at[chunk, x], x_peers[k])

    def over_z(chunk):
        total = a_own[chunk, x].astype(F32)
        for k in (3, 1, 2):
            arrived(a_xr.at[chunk, xs[k]], ax_rs.at[chunk, xs[k]])
            total = total + a_xr[chunk, xs[k]].astype(F32)
        a_x[chunk, pl.ds(0, 13)] = total.astype(BF16)
        a_x[chunk, pl.ds(13, 3)] = jnp.zeros((3, 16, 128), BF16)
        for k in (1, 7, 2, 6, 3, 5, 4):
            send(a_x.at[chunk, pl.ds(2 * zs[k], 2)], a_zr.at[chunk, z], az_ss.at[chunk, k],
                 az_rs.at[chunk, z], z_peers[k])

    def back_over_z(chunk):
        total = a_x[chunk, pl.ds(2 * z, 2)].astype(F32)
        for k in range(1, Z):
            arrived(a_zr.at[chunk, zs[k]], az_rs.at[chunk, zs[k]])
            total = total + a_zr[chunk, zs[k]].astype(F32)
        mine = a_all.at[chunk, x, pl.ds(2 * z, 2)]
        mine[...] = total.astype(BF16)
        for k in (1, 7, 2, 6, 3, 5, 4):
            send(mine, mine, bz_ss.at[chunk, k], bz_rs.at[chunk, z], z_peers[k])

    def back_over_x(chunk):
        for k in range(1, Z):
            arrived(a_all.at[chunk, x, pl.ds(2 * zs[k], 2)], bz_rs.at[chunk, zs[k]])
        mine = a_all.at[chunk, x, pl.ds(0, 13)]
        for k in (1, 3, 2):
            send(mine, mine, bx_ss.at[chunk, k], bx_rs.at[chunk, x], x_peers[k])

    outputs = []

    def g_finish():
        term = merge_term(z)
        for half in (0, 1):
            gm_ref[pl.ds(half * HALF, HALF)] = (
                term[half_rows(half)] + g_in(0, 3, half) + g_in(1, 3, half))
        outputs.append(pltpu.make_async_copy(gm_ref, gm_hbm, out_s.at[0]))
        outputs[0].start()

    g_piece(2, 1)
    e_sum_up(0)
    g_piece(3, 0)
    e_sum_up(1)
    over_z(0)
    e_sum_up(2)
    over_z(1)
    e_sum_up(3)
    g_piece(3, 1)
    back_over_z(0)
    for k in (1, 3, 2, 0):
        e_home(k)
    back_over_z(1)
    back_over_x(0)
    back_over_x(1)
    g_finish()

    for k in range(1, Y):
        arrived(e_fin.at[ys[k]], e1_rs.at[ys[k]])
    for k in range(QUAD):
        block = e_fin[k]
        embeds_ref[:, k * NC:(k + 1) * NC] = jnp.where(live_rows, block, jnp.zeros_like(block))
    outputs.append(pltpu.make_async_copy(embeds_ref, embeds_hbm, out_s.at[1]))
    outputs[1].start()

    for chunk in (0, 1):
        for k in range(1, X):
            arrived(a_all.at[chunk, xs[k], pl.ds(0, 13)], bx_rs.at[chunk, xs[k]])
        for p in range(50):
            i, j = p % 10, 5 * chunk + p // 10
            rows = slice(16 * i, 16 * (i + 1))
            tile = a_all[chunk, p // 13, p % 13].astype(F32)
            if j < 9:
                gp_ref[rows, 128 * j:128 * (j + 1)] = tile
            else:
                gp_ref[rows, 1152:] = tile[:, :PD - 1152]
    outputs.append(pltpu.make_async_copy(gp_ref, gp_hbm, out_s.at[2]))
    outputs[2].start()

    for copy in outputs:
        copy.wait()
    for copy in started:
        copy.wait_send()


def finish(embeds_in, gm_in, gp_in, embeds_out, gm_out, gp_out, embeds_s, gm_s, gp_s, sems):
    parts = []
    for i, (src, held, dst, rows) in enumerate((
        (embeds_in, embeds_s, embeds_out, G), (gm_in, gm_s, gm_out, K), (gp_in, gp_s, gp_out, FS)
    )):
        for half in (0, 1):
            part = pl.ds(half * rows // 2, rows // 2)
            parts.append((
                pltpu.make_async_copy(src.at[part], held.at[part], sems.at[0, i, half]),
                pltpu.make_async_copy(held.at[part], dst.at[part], sems.at[1, i, half]),
            ))
    for load, _ in parts:
        load.start()
    for load, store in parts:
        load.wait()
        store.start()
    for _, store in parts:
        store.wait()


def body(patches, rank_groups, patch_weight, merge_weight, emb_grad):
    dma = pltpu.SemaphoreType.DMA
    rows = 4 * G
    scratch = [
        pltpu.VMEM((G, QUAD * NC), BF16),
        pltpu.VMEM((K, NC), F32),
        pltpu.VMEM((FS, PD), F32),
        pltpu.VMEM((PD, rows), BF16),
        pltpu.VMEM((FS, PD), BF16),
        pltpu.VMEM((G, QUAD * NC), BF16),
        pltpu.VMEM((Z, K, NC), BF16),
        pltpu.VMEM((QUAD, G, NC), BF16),
        pltpu.VMEM((Y, G, NC), BF16),
        pltpu.VMEM((X, Z, G, NC), BF16),
        pltpu.VMEM((X, G, K), BF16),
        pltpu.VMEM((K, X * G), BF16),
        pltpu.VMEM((2, rows, 128), F32),
        pltpu.VMEM((2, G, K), F32),
        pltpu.VMEM((2, T, 8, G), F32),
        pltpu.VMEM((X, 8, G), F32),
        pltpu.VMEM((X, 8, G), F32),
        pltpu.VMEM((2, 4, 2, HALF, NC), BF16),
        pltpu.VMEM((2, 4, 2, HALF, NC), BF16),
        pltpu.VMEM((X, G, K), BF16),
        pltpu.VMEM((2, 128, K), F32),
        pltpu.VMEM((2, 128, K), BF16),
        pltpu.VMEM((G, K), F32),
        pltpu.VMEM((2, G, K), BF16),
        pltpu.VMEM((X, QUAD, G, NC), BF16),
        pltpu.VMEM((X, QUAD, G, NC), BF16),
        pltpu.VMEM((X, QUAD, G, NC), BF16),
        pltpu.VMEM((X, 2, 128, NC), BF16),
        pltpu.VMEM((X, 2, G, NC), BF16),
        pltpu.VMEM((X, G, NC), BF16),
        pltpu.VMEM((X, G, NC), BF16),
        pltpu.VMEM((QUAD, G, NC), BF16),
        pltpu.VMEM((2, FS, 640), BF16),
        pltpu.VMEM((2, X, 13, 16, 128), BF16),
        pltpu.VMEM((2, X, 13, 16, 128), BF16),
        pltpu.VMEM((2, 16, 16, 128), BF16),
        pltpu.VMEM((2, Z, 2, 16, 128), BF16),
        pltpu.VMEM((2, X, 16, 16, 128), BF16),
        dma((4,)),
        dma((3,)),
    ]
    for shape in (
        (2, 4, 2), (4, 2), (4, 2), (4, 4, 2), (4, 2), (4, 4), (2, 8), (4,), (4,),
        (2, 2), (2,), (2, 4, 2), (4,), (4, 2), (4, 2, 2), (4,), (4,), (2, 4), (2, 8), (2, 8), (2, 4),
    ):
        scratch += [dma(shape), dma(shape)]
    results = (
        jax.ShapeDtypeStruct((G, QUAD * NC), BF16),
        jax.ShapeDtypeStruct((K, NC), F32),
        jax.ShapeDtypeStruct((FS, PD), F32),
    )
    hbm = pl.BlockSpec(memory_space=pl.ANY)
    partial = pl.pallas_call(
        kernel,
        out_shape=results,
        in_specs=[pl.BlockSpec(memory_space=pltpu.SMEM)] + [hbm] * 4,
        out_specs=(hbm, hbm, hbm),
        scratch_shapes=scratch,
        compiler_params=pltpu.CompilerParams(
            collective_id=0, has_side_effects=True, vmem_limit_bytes=56 * 2**20
        ),
        name="tower",
    )(rank_groups, patches.T, patch_weight.T, merge_weight.reshape(K, NC), emb_grad)
    embeds, grad_merge, grad_patch = pl.pallas_call(
        finish,
        out_shape=results,
        in_specs=[hbm, hbm, hbm],
        out_specs=(hbm, hbm, hbm),
        scratch_shapes=[
            pltpu.VMEM((G, QUAD * NC), BF16),
            pltpu.VMEM((K, NC), F32),
            pltpu.VMEM((FS, PD), F32),
            dma((2, 3, 2)),
        ],
        name="finish",
    )(*partial)
    return embeds, grad_merge.reshape(4, FS, NC), grad_patch.T


def solution(mesh):
    return jax.shard_map(
        body,
        mesh=mesh,
        in_specs=(
            P("dp", None),
            P("dp"),
            P(None, "tensor"),
            P(None, "tensor", "dp"),
            P("dp", "tensor"),
        ),
        out_specs=(P("dp", "tensor"), P(None, "tensor", "dp"), P(None, "tensor")),
        check_vma=False,
    )
```

```python
import functools

import jax
import jax.numpy as jnp
from jax import lax
from jax.experimental import pallas as pl
from jax.experimental.pallas import tpu as pltpu
from jax.sharding import PartitionSpec as P

E = 1280
X, Y, Z = 4, 4, 8
T = 2 * Y
F32, BF16 = jnp.float32, jnp.bfloat16
HIGH = lax.Precision.HIGHEST

PD = 1176
FS = E // T
K = 4 * FS
G = 256
NC = 256
HALF = K // 2
QUAD = Z // 2


def dot(a, b, dims=((1,), (0,)), precision=None):
    return lax.dot_general(a, b, (dims, ((), ())), precision=precision, preferred_element_type=F32)


def wrap(value, count):
    return lax.rem(value + count, count)


def group_rows(offset):
    row = lax.broadcasted_iota(jnp.int32, (8, K), 0)
    lane = lax.broadcasted_iota(jnp.int32, (8, K), 1)
    low = (row - offset) * FS
    return jnp.where((lane >= low) & (lane < low + FS), 1.0, 0.0).astype(F32)


def kernel(
    live_ref, patches_hbm, pw_hbm, w_hbm, emb_hbm,
    embeds_hbm, gm_hbm, gp_hbm,
    embeds_ref, gm_ref, gp_ref,
    patches_ref, pw_ref, emb_ref,
    wg, cot_own, cot_p1, cot_all, merged_all, merged_t, proj_s, normed_s,
    stats, sx_send, sx_recv, g_send_buf, g_recv_buf,
    d_send_buf, d_keep, d_far, d_own, d_recv_buf,
    e_sib_send, e_sib_recv, e_send, e_far, e_recv, e_sum, e_p2, e_fin,
    t_s, a_own, a_xr, a_x, a_zr, a_all,
    in_s, out_s,
    w_ss, w_rs, p1_ss, p1_rs, p2_ss, p2_rs, p3_ss, p3_rs, ph_ss, ph_rs, cs_ss, cs_rs,
    st_ss, st_rs, sx_ss, sx_rs, m_ss, m_rs,
    d_ss, d_rs, df_ss, df_rs, g_ss, g_rs, es_ss, es_rs, ef_ss, ef_rs, ey_ss, ey_rs, e2_ss, e2_rs, e1_ss, e1_rs,
    ax_ss, ax_rs, az_ss, az_rs, bz_ss, bz_rs, bx_ss, bx_rs,
):
    dp = lax.axis_index("dp")
    t = lax.axis_index("tensor")
    x, z = lax.div(dp, Z), lax.rem(dp, Z)
    y, c = lax.div(t, 2), lax.rem(t, 2)

    def device(x, y, z, c):
        return (x * Z + z, y * 2 + c)

    started = []

    def send(src, dst, ssem, rsem, to):
        copy = pltpu.make_async_remote_copy(
            src_ref=src, dst_ref=dst, send_sem=ssem, recv_sem=rsem,
            device_id=to, device_id_type=pl.DeviceIdType.MESH,
        )
        copy.start()
        started.append(copy)

    def arrived(dst, rsem):
        pltpu.make_async_remote_copy(
            src_ref=dst, dst_ref=dst, send_sem=w_ss.at[0, 0, 0], recv_sem=rsem,
            device_id=sibling, device_id_type=pl.DeviceIdType.MESH,
        ).wait_recv()

    right = device(x, y, wrap(z + 1, Z), c)
    left = device(x, y, wrap(z - 1, Z), c)
    sibling = device(x, y, z, 1 - c)
    xs = [wrap(x + k, X) for k in range(X)]
    ys = [wrap(y + k, Y) for k in range(Y)]
    zs = [wrap(z + k, Z) for k in range(Z)]
    x_peers = [device(i, y, z, c) for i in xs]
    y_peers = [device(x, i, z, c) for i in ys]
    z_peers = [device(x, y, i, c) for i in zs]
    t_peers = [(dp, wrap(t + k, T)) for k in range(T)]

    inputs = [
        pltpu.make_async_copy(w_hbm, wg.at[z], in_s.at[0]),
        pltpu.make_async_copy(emb_hbm, emb_ref, in_s.at[1]),
        pltpu.make_async_copy(pw_hbm, pw_ref, in_s.at[2]),
        pltpu.make_async_copy(patches_hbm, patches_ref, in_s.at[3]),
    ]
    for copy in inputs:
        copy.start()

    barrier = pltpu.get_barrier_semaphore()
    greeted = x_peers[1:] + z_peers[1:] + t_peers[1:]
    for peer in greeted:
        pl.semaphore_signal(barrier, inc=1, device_id=peer, device_id_type=pl.DeviceIdType.MESH)

    inputs[0].wait()
    inputs[1].wait()
    live = live_ref[0]
    live_rows = lax.broadcasted_iota(jnp.int32, (G, NC), 0) < live
    for k in range(QUAD):
        block = emb_ref[:, k * NC:(k + 1) * NC]
        cot_own[k] = jnp.where(live_rows, block, jnp.zeros_like(block))

    pl.semaphore_wait(barrier, len(greeted))

    def rows_of(half):
        return pl.ds(half * 128, 128)

    for half in (0, 1):
        for k in (1, 3, 2):
            send(cot_own.at[ys[k], rows_of(half)], cot_p1.at[y, rows_of(half)],
                 p1_ss.at[k, half], p1_rs.at[y, half], y_peers[k])

    def w_part(index, half):
        return wg.at[index, pl.ds(half * HALF, HALF)]

    def w_fwd(step, piece):
        for way, to, block in ((0, right, wrap(z - step, Z)), (1, left, wrap(z + step, Z))):
            half = piece if way == 0 else 1 - piece
            part = w_part(block, half)
            if step:
                arrived(part, w_rs.at[way, step - 1, half])
            send(part, part, w_ss.at[way, step, half], w_rs.at[way, step, half], to)

    def w_finish():
        for way, block in ((0, wrap(z - 3, Z)), (1, wrap(z + 3, Z))):
            arrived(w_part(block, 1 - way), w_rs.at[way, 2, 1 - way])
        for way in (0, 1):
            arrived(w_part(wrap(z + 4, Z), way), w_rs.at[way, 3, way])

    w_fwd(0, 0)
    w_fwd(0, 1)
    cot_p1[y] = cot_own[y]

    inputs[2].wait()
    inputs[3].wait()
    for i in range(4):
        rows = pl.ds(i * 256, 256)
        product = dot(pw_ref[...], patches_ref[:, i * 256:(i + 1) * 256])
        product = jnp.transpose(jnp.concatenate([product, jnp.zeros((256 - FS, 256), F32)], axis=0))
        proj_s[0, rows] = product[:, :128]
        proj_s[1, rows] = product[:, 128:]

    parts = []
    for q in range(4):
        rows = pl.ds(q, G, stride=4)
        parts.append(jnp.concatenate([proj_s[0, rows, :], proj_s[1, rows, :]], axis=1)[:, :FS])
    projected = jnp.concatenate(parts, axis=1)

    first, second = group_rows(0), group_rows(4)

    def send_stats(index):
        mine = stats.at[index, t]
        for k in range(1, T):
            send(mine, mine, st_ss.at[index, k], st_rs.at[index, t], t_peers[k])

    def totals(index):
        for k in range(1, T):
            owner = wrap(t + k, T)
            arrived(stats.at[index, owner], st_rs.at[index, owner])
        total = stats[index, 0]
        for k in range(1, T):
            total = total + stats[index, k]
        return total / E

    def spread(rows, value):
        return dot(value, rows, ((0,), (0,)), HIGH)

    stats[0, t] = (
        dot(first, projected, ((1,), (1,)), HIGH)
        + dot(second, projected * projected, ((1,), (1,)), HIGH)
    )
    send_stats(0)
    def cot_over_x(half):
        for k in (1, 3, 2, 0):
            origin = xs[k]
            block = cot_p1.at[origin, rows_of(half)]

            @pl.when(origin != y)
            def _():
                arrived(block, p1_rs.at[origin, half])

            slot = cot_all.at[x, c * QUAD + y, rows_of(half)]
            if k:
                send(block, slot, p2_ss.at[k, half], p2_rs.at[x, half], x_peers[k])
            else:
                slot[...] = block[...]

    def cot_block(k, j):
        return cot_all.at[xs[k], c * QUAD + ys[j]]

    def to_sibling(k, j):
        block = cot_block(k, j)
        send(block, block, cs_ss.at[k, j], cs_rs.at[xs[k], ys[j]], sibling)

    def cot_out(k, half):
        part = cot_block(k, 0).at[rows_of(half)]
        if k:
            arrived(part, p2_rs.at[xs[k], half])
        for j in (1, 3):
            send(part, part, p3_ss.at[k, j, half], p3_rs.at[xs[k], y, half], y_peers[j])
        if half:
            to_sibling(k, 0)

    def cot_on(k):
        for half, j in ((0, 1), (1, 3)):
            part = cot_block(k, j).at[rows_of(half)]
            arrived(part, p3_rs.at[xs[k], ys[j], half])
            send(part, part, ph_ss.at[k, half], ph_rs.at[xs[k], half], y_peers[4 - j])
        for half, j in ((1, 1), (0, 3)):
            arrived(cot_block(k, j).at[rows_of(half)], p3_rs.at[xs[k], ys[j], half])
            to_sibling(k, j)

    def cot_far(k):
        for half in (0, 1):
            arrived(cot_block(k, 2).at[rows_of(half)], ph_rs.at[xs[k], half])
        to_sibling(k, 2)

    def cot_in(k):
        for j in range(Y):
            arrived(cot_all.at[xs[k], (1 - c) * QUAD + ys[j]], cs_rs.at[xs[k], ys[j]])

    cot_over_x(0)
    w_fwd(1, 0)
    cot_out(0, 0)
    cot_over_x(1)
    cot_out(0, 1)
    cot_out(1, 0)
    cot_out(3, 0)
    w_fwd(1, 1)

    means = totals(0)
    row = lax.broadcasted_iota(jnp.int32, (8, G), 0)
    row_mean = pltpu.roll(means, 4, 0)
    inv_scale = jnp.where(row >= 4, lax.rsqrt(
        jnp.where(row >= 4, means - row_mean * row_mean, 1.0) + 1e-05), 0.0)
    inv_wide = spread(second, inv_scale)
    normed = (projected - spread(first, means)) * inv_wide
    normed_s[0] = normed
    normed_s[1] = inv_wide
    merged_all[x] = normed.astype(BF16)
    for k in range(1, X):
        send(merged_all.at[x], merged_all.at[x], m_ss.at[k], m_rs.at[x], x_peers[k])

    cot_out(2, 0)
    cot_out(1, 1)
    cot_out(3, 1)
    w_fwd(2, 0)
    cot_on(0)
    cot_out(2, 1)
    w_fwd(2, 1)
    merged_t[:, pl.ds(x * G, G)] = jnp.transpose(merged_all[x])
    cot_far(0)
    w_fwd(3, 0)
    cot_on(1)
    cot_on(3)
    cot_far(1)
    cot_on(2)
    cot_far(3)
    w_finish()
    for k in (3, 1, 2):
        arrived(merged_all.at[xs[k]], m_rs.at[xs[k]])

    for n in range(X):
        rows = merged_all[xs[(n + 1) % X]]
        for m in range(QUAD):
            block = wg[(1 - c) * QUAD + ys[(m + 1) % Y]]
            e_sib_send[n, m] = dot(rows, block).astype(BF16)
        send(e_sib_send.at[n], e_sib_recv.at[n], es_ss.at[n], es_rs.at[n], sibling)

    cot_far(2)
    for k in (0, 1, 3, 2):
        cot_in(k)

    def d_term(owner):
        total = None
        for block in range(Z):
            term = dot(cot_all[owner, block], wg[block], ((1,), (1,)))
            total = term if total is None else total + term
        return total

    def d_sums(term, owner):
        rounded = term.astype(BF16)
        product = (term * merged_all[owner].astype(F32)).astype(BF16)
        return (dot(first.astype(BF16), rounded, ((1,), (1,)))
                + dot(second.astype(BF16), product, ((1,), (1,))))

    def d_near(way, half, to):
        slot = 1 if way == 0 else 3
        part = pl.ds(half * 128, 128)
        send(d_send_buf.at[slot, part], d_recv_buf.at[way, part], d_ss.at[way, half],
             d_rs.at[way, half], to)

    def d_out(k):
        term = d_term(xs[k])
        d_send_buf[k] = term.astype(BF16)
        sx_send[k] = d_sums(term, xs[k])
        send(sx_send.at[k], sx_recv.at[x], sx_ss.at[k], sx_rs.at[x], x_peers[k])
        if k == 2:
            for way, peer in ((0, x_peers[1]), (1, x_peers[3])):
                send(d_send_buf.at[2, rows_of(way)], d_far.at[way], df_ss.at[way],
                     df_rs.at[way], peer)
        else:
            way = 0 if k == 1 else 1
            d_keep[way] = term[way * 128:(way + 1) * 128]
            d_near(way, 1 - way, x_peers[k])

    def d_combine():
        for way, slot, to in ((0, 1, x_peers[1]), (1, 3, x_peers[3])):
            arrived(d_far.at[way], df_rs.at[way])
            d_send_buf[slot, rows_of(way)] = (d_keep[way] + d_far[way].astype(F32)).astype(BF16)
            d_near(way, way, to)

    def e_term(n, m):
        value = dot(merged_all[xs[(n + 1) % X]], wg[c * QUAD + ys[(m + 1) % Y]])
        e_send[n, m] = (value + e_sib_recv[n, m].astype(F32)).astype(BF16)

    def e_far_out(n):
        arrived(e_sib_recv.at[n], es_rs.at[n])
        e_term(n, 1)
        for way, peer in ((0, y_peers[1]), (1, y_peers[3])):
            send(e_send.at[n, 1, rows_of(way)], e_far.at[n, way], ef_ss.at[n, way],
                 ef_rs.at[n, way], peer)

    def e_near_out(n):
        e_term(n, 0)
        e_near(n, 0, 1)
        e_term(n, 2)
        e_near(n, 1, 0)
        e_term(n, 3)

    def e_near(n, way, half):
        slot, peer = (0, y_peers[1]) if way == 0 else (2, y_peers[3])
        send(e_send.at[n, slot, rows_of(half)], e_recv.at[n, way, rows_of(half)],
             ey_ss.at[n, way, half], ey_rs.at[n, way, half], peer)

    def e_combine(n):
        for way, slot in ((0, 0), (1, 2)):
            arrived(e_far.at[n, way], ef_rs.at[n, way])
            part = e_send.at[n, slot, rows_of(way)]
            part[...] = (part[...].astype(F32) + e_far[n, way].astype(F32)).astype(BF16)
            e_near(n, way, way)

    def e_sum_up(n):
        total = e_send[n, QUAD - 1].astype(F32)
        for way in (0, 1):
            for half in (1 - way, way):
                arrived(e_recv.at[n, way, rows_of(half)], ey_rs.at[n, way, half])
            total = total + e_recv[n, way].astype(F32)
        total = total.astype(BF16)
        if n < X - 1:
            e_sum[n] = total
            send(e_sum.at[n], e_p2.at[x], e2_ss.at[n], e2_rs.at[x], x_peers[n + 1])
        else:
            e_p2[x] = total

    def e_home(k):
        origin = ys[k]
        block = e_p2.at[origin]

        @pl.when(origin != x)
        def _():
            arrived(block, e2_rs.at[origin])

        if k:
            send(block, e_fin.at[y], e1_ss.at[k], e1_rs.at[y], y_peers[k])
        else:
            e_fin[y] = block[...]

    d_out(2)
    for k in range(1, X):
        merged_t[:, pl.ds(xs[k] * G, G)] = jnp.transpose(merged_all[xs[k]])

    def merge_term(block, rows=slice(None)):
        return dot(merged_t[rows], cot_all[:, block].reshape(X * G, NC))

    def g_block(way, step):
        return wrap(z + 4 - step, Z) if way == 0 else wrap(z - 4 + step, Z)

    def g_out(way, step, half, value):
        g_send_buf[way, step, half] = value.astype(BF16)
        send(g_send_buf.at[way, step, half], g_recv_buf.at[way, step, half],
             g_ss.at[way, step, half], g_rs.at[way, step, half], right if way == 0 else left)

    def g_in(way, step, half):
        arrived(g_recv_buf.at[way, step, half], g_rs.at[way, step, half])
        return g_recv_buf[way, step, half].astype(F32)

    def half_rows(half):
        return slice(half * HALF, (half + 1) * HALF)

    for way in (0, 1):
        g_out(way, 0, way, merge_term(g_block(way, 0), half_rows(way)))
    for way in (0, 1):
        g_out(way, 1, 1 - way, merge_term(g_block(way, 1), half_rows(1 - way)))

    def g_piece(step, piece):
        for way in (0, 1):
            half = 1 - way if piece == 0 else way
            term = merge_term(g_block(way, step), half_rows(half))
            g_out(way, step, half, term + g_in(way, step - 1, half))

    e_far_out(0)
    e_near_out(0)
    d_out(1)
    d_out(3)
    term = d_term(x)
    d_own[...] = term
    total = d_sums(term, x)
    d_combine()
    for k in range(1, X):
        arrived(sx_recv.at[xs[k]], sx_rs.at[xs[k]])
        total = total + sx_recv[xs[k]]
    stats[1, t] = total
    send_stats(1)
    g_piece(1, 1)
    for n in (1, 2, 3):
        e_far_out(n)
    e_combine(0)
    for n in (1, 2, 3):
        e_near_out(n)
    g_piece(2, 0)
    for n in (1, 2):
        e_combine(n)

    means = totals(1)
    d_mean = spread(first, means)
    dn_mean = spread(second, means)
    dnormed = d_own[...]
    for way in (0, 1):
        for half in (1 - way, way):
            arrived(d_recv_buf.at[way, rows_of(half)], d_rs.at[way, half])
        dnormed = dnormed + d_recv_buf[way].astype(F32)
    grad_input = (dnormed - d_mean - normed_s[0] * dn_mean) * normed_s[1]
    for q in range(4):
        part = grad_input[:, q * FS:(q + 1) * FS]
        part = jnp.concatenate([part, jnp.zeros((G, 256 - FS), F32)], axis=1)
        rows = pl.ds(q, G, stride=4)
        proj_s[0, rows, :] = part[:, :128]
        proj_s[1, rows, :] = part[:, 128:]
    grad_rows = jnp.concatenate([proj_s[0], proj_s[1]], axis=1)
    grad_rows = jnp.transpose(grad_rows)[:FS].astype(BF16)

    e_combine(3)

    for chunk in (0, 1):
        low, high = 640 * chunk, min(640 * (chunk + 1), PD)
        if chunk:
            t_s[chunk, :, 512:] = jnp.zeros((FS, 128), BF16)
        t_s[chunk, :, :high - low] = dot(
            grad_rows, patches_ref[low:high], ((1,), (1,))).astype(BF16)
        for p in range(50):
            i, j = p % 10, p // 10
            a_own[chunk, p // 13, p % 13] = t_s[chunk, 16 * i:16 * (i + 1), 128 * j:128 * (j + 1)]
        for p in range(50, 52):
            a_own[chunk, p // 13, p % 13] = jnp.zeros((16, 128), BF16)
        for k in (1, 3, 2):
            send(a_own.at[chunk, xs[k]], a_xr.at[chunk, x], ax_ss.at[chunk, k],
                 ax_rs.at[chunk, x], x_peers[k])

    def over_z(chunk):
        total = a_own[chunk, x].astype(F32)
        for k in (3, 1, 2):
            arrived(a_xr.at[chunk, xs[k]], ax_rs.at[chunk, xs[k]])
            total = total + a_xr[chunk, xs[k]].astype(F32)
        a_x[chunk, pl.ds(0, 13)] = total.astype(BF16)
        a_x[chunk, pl.ds(13, 3)] = jnp.zeros((3, 16, 128), BF16)
        for k in (1, 7, 2, 6, 3, 5, 4):
            send(a_x.at[chunk, pl.ds(2 * zs[k], 2)], a_zr.at[chunk, z], az_ss.at[chunk, k],
                 az_rs.at[chunk, z], z_peers[k])

    def back_over_z(chunk):
        total = a_x[chunk, pl.ds(2 * z, 2)].astype(F32)
        for k in range(1, Z):
            arrived(a_zr.at[chunk, zs[k]], az_rs.at[chunk, zs[k]])
            total = total + a_zr[chunk, zs[k]].astype(F32)
        mine = a_all.at[chunk, x, pl.ds(2 * z, 2)]
        mine[...] = total.astype(BF16)
        for k in (1, 7, 2, 6, 3, 5, 4):
            send(mine, mine, bz_ss.at[chunk, k], bz_rs.at[chunk, z], z_peers[k])

    def back_over_x(chunk):
        for k in range(1, Z):
            arrived(a_all.at[chunk, x, pl.ds(2 * zs[k], 2)], bz_rs.at[chunk, zs[k]])
        mine = a_all.at[chunk, x, pl.ds(0, 13)]
        for k in (1, 3, 2):
            send(mine, mine, bx_ss.at[chunk, k], bx_rs.at[chunk, x], x_peers[k])

    outputs = []

    def g_finish():
        term = merge_term(z)
        for half in (0, 1):
            gm_ref[pl.ds(half * HALF, HALF)] = (
                term[half_rows(half)] + g_in(0, 3, half) + g_in(1, 3, half))
        outputs.append(pltpu.make_async_copy(gm_ref, gm_hbm, out_s.at[0]))
        outputs[0].start()

    g_piece(2, 1)
    e_sum_up(0)
    g_piece(3, 0)
    e_sum_up(1)
    over_z(0)
    e_sum_up(2)
    over_z(1)
    e_sum_up(3)
    back_over_z(0)
    for k in (1, 3, 2, 0):
        e_home(k)
    back_over_z(1)
    g_piece(3, 1)
    back_over_x(0)
    back_over_x(1)
    g_finish()

    for k in range(1, Y):
        arrived(e_fin.at[ys[k]], e1_rs.at[ys[k]])
    for k in range(QUAD):
        block = e_fin[k]
        embeds_ref[:, k * NC:(k + 1) * NC] = jnp.where(live_rows, block, jnp.zeros_like(block))
    outputs.append(pltpu.make_async_copy(embeds_ref, embeds_hbm, out_s.at[1]))
    outputs[1].start()

    for chunk in (0, 1):
        for k in range(1, X):
            arrived(a_all.at[chunk, xs[k], pl.ds(0, 13)], bx_rs.at[chunk, xs[k]])
        for p in range(50):
            i, j = p % 10, 5 * chunk + p // 10
            rows = slice(16 * i, 16 * (i + 1))
            tile = a_all[chunk, p // 13, p % 13].astype(F32)
            if j < 9:
                gp_ref[rows, 128 * j:128 * (j + 1)] = tile
            else:
                gp_ref[rows, 1152:] = tile[:, :PD - 1152]
    outputs.append(pltpu.make_async_copy(gp_ref, gp_hbm, out_s.at[2]))
    outputs[2].start()

    for copy in outputs:
        copy.wait()
    for copy in started:
        copy.wait_send()


def finish(embeds_in, gm_in, gp_in, embeds_out, gm_out, gp_out, embeds_s, gm_s, gp_s, sems):
    parts = []
    for i, (src, held, dst, rows) in enumerate((
        (embeds_in, embeds_s, embeds_out, G), (gm_in, gm_s, gm_out, K), (gp_in, gp_s, gp_out, FS)
    )):
        for half in (0, 1):
            part = pl.ds(half * rows // 2, rows // 2)
            parts.append((
                pltpu.make_async_copy(src.at[part], held.at[part], sems.at[0, i, half]),
                pltpu.make_async_copy(held.at[part], dst.at[part], sems.at[1, i, half]),
            ))
    for load, _ in parts:
        load.start()
    for load, store in parts:
        load.wait()
        store.start()
    for _, store in parts:
        store.wait()


def body(patches, rank_groups, patch_weight, merge_weight, emb_grad):
    dma = pltpu.SemaphoreType.DMA
    rows = 4 * G
    scratch = [
        pltpu.VMEM((G, QUAD * NC), BF16),
        pltpu.VMEM((K, NC), F32),
        pltpu.VMEM((FS, PD), F32),
        pltpu.VMEM((PD, rows), BF16),
        pltpu.VMEM((FS, PD), BF16),
        pltpu.VMEM((G, QUAD * NC), BF16),
        pltpu.VMEM((Z, K, NC), BF16),
        pltpu.VMEM((QUAD, G, NC), BF16),
        pltpu.VMEM((Y, G, NC), BF16),
        pltpu.VMEM((X, Z, G, NC), BF16),
        pltpu.VMEM((X, G, K), BF16),
        pltpu.VMEM((K, X * G), BF16),
        pltpu.VMEM((2, rows, 128), F32),
        pltpu.VMEM((2, G, K), F32),
        pltpu.VMEM((2, T, 8, G), F32),
        pltpu.VMEM((X, 8, G), F32),
        pltpu.VMEM((X, 8, G), F32),
        pltpu.VMEM((2, 4, 2, HALF, NC), BF16),
        pltpu.VMEM((2, 4, 2, HALF, NC), BF16),
        pltpu.VMEM((X, G, K), BF16),
        pltpu.VMEM((2, 128, K), F32),
        pltpu.VMEM((2, 128, K), BF16),
        pltpu.VMEM((G, K), F32),
        pltpu.VMEM((2, G, K), BF16),
        pltpu.VMEM((X, QUAD, G, NC), BF16),
        pltpu.VMEM((X, QUAD, G, NC), BF16),
        pltpu.VMEM((X, QUAD, G, NC), BF16),
        pltpu.VMEM((X, 2, 128, NC), BF16),
        pltpu.VMEM((X, 2, G, NC), BF16),
        pltpu.VMEM((X, G, NC), BF16),
        pltpu.VMEM((X, G, NC), BF16),
        pltpu.VMEM((QUAD, G, NC), BF16),
        pltpu.VMEM((2, FS, 640), BF16),
        pltpu.VMEM((2, X, 13, 16, 128), BF16),
        pltpu.VMEM((2, X, 13, 16, 128), BF16),
        pltpu.VMEM((2, 16, 16, 128), BF16),
        pltpu.VMEM((2, Z, 2, 16, 128), BF16),
        pltpu.VMEM((2, X, 16, 16, 128), BF16),
        dma((4,)),
        dma((3,)),
    ]
    for shape in (
        (2, 4, 2), (4, 2), (4, 2), (4, 4, 2), (4, 2), (4, 4), (2, 8), (4,), (4,),
        (2, 2), (2,), (2, 4, 2), (4,), (4, 2), (4, 2, 2), (4,), (4,), (2, 4), (2, 8), (2, 8), (2, 4),
    ):
        scratch += [dma(shape), dma(shape)]
    results = (
        jax.ShapeDtypeStruct((G, QUAD * NC), BF16),
        jax.ShapeDtypeStruct((K, NC), F32),
        jax.ShapeDtypeStruct((FS, PD), F32),
    )
    hbm = pl.BlockSpec(memory_space=pl.ANY)
    partial = pl.pallas_call(
        kernel,
        out_shape=results,
        in_specs=[pl.BlockSpec(memory_space=pltpu.SMEM)] + [hbm] * 4,
        out_specs=(hbm, hbm, hbm),
        scratch_shapes=scratch,
        compiler_params=pltpu.CompilerParams(
            collective_id=0, has_side_effects=True, vmem_limit_bytes=56 * 2**20
        ),
        name="tower",
    )(rank_groups, patches.T, patch_weight.T, merge_weight.reshape(K, NC), emb_grad)
    embeds, grad_merge, grad_patch = pl.pallas_call(
        finish,
        out_shape=results,
        in_specs=[hbm, hbm, hbm],
        out_specs=(hbm, hbm, hbm),
        scratch_shapes=[
            pltpu.VMEM((G, QUAD * NC), BF16),
            pltpu.VMEM((K, NC), F32),
            pltpu.VMEM((FS, PD), F32),
            dma((2, 3, 2)),
        ],
        name="finish",
    )(*partial)
    return embeds, grad_merge.reshape(4, FS, NC), grad_patch.T


def solution(mesh):
    return jax.shard_map(
        body,
        mesh=mesh,
        in_specs=(
            P("dp", None),
            P("dp"),
            P(None, "tensor"),
            P(None, "tensor", "dp"),
            P("dp", "tensor"),
        ),
        out_specs=(P("dp", "tensor"), P(None, "tensor", "dp"), P(None, "tensor")),
        check_vma=False,
    )
```
